32 devices in a mesh: dp: 8 (over y, x, core), expert: 4 (over z).
Axes of the slice: x: 2, y: 2, z: 4, core: 2. Of those that a mesh axis runs over, the one named last changes fastest.
Arguments:
- tokens: bfloat16 [4096, 2048], P(('dp', 'expert')), may hold values from -6 to 6
- lengths: int32 [64], replicated, may hold values from 32 to 96, as said below
- permutation: int32 [64], replicated, may hold values from 0 to 63, as said below
- routes: int32 [4096, 8], P(('dp', 'expert')), may hold values from 0 to 15, all different within a row; in each aligned block of 128 rows (0 to 127, 128 to 255, ...) at most 80 rows name the same one
- norm_gains: bfloat16 [2048, 4], P(('dp', 'expert')), may hold values from 0.25 to 1.75
- w_qkv: bfloat16 [2048, 6144], P(('dp', 'expert')), may hold values from -0.125 to 0.125
- w_out: bfloat16 [2048, 2048], P(('dp', 'expert')), may hold values from -0.75 to 0.75
- router: bfloat16 [2048, 16], P(('dp', 'expert')), may hold values from -0.0625 to 0.0625
- w_gate_up: bfloat16 [2048, 16, 2048], P('dp', 'expert'), may hold values from -0.125 to 0.125
- w_down: bfloat16 [2048, 16, 1024], P('dp', 'expert'), may hold values from -0.75 to 0.75
- cotangent: bfloat16 [4096, 2048], P(('dp', 'expert')), may hold values from -6 to 6
Outputs:
- output: float32 [4096, 2048], P(('dp', 'expert'))
- grad_tokens: float32 [4096, 2048], P(('dp', 'expert'))
- grad_gains: float32 [2048, 4], P(('dp', 'expert'))
- grad_w_qkv: float32 [2048, 6144], P(('dp', 'expert'))
- grad_w_out: float32 [2048, 2048], P(('dp', 'expert'))
- grad_router: float32 [2048, 16], P(('dp', 'expert'))
- grad_w_gate_up: float32 [2048, 16, 2048], P('dp', 'expert')
- grad_w_down: float32 [2048, 16, 1024], P('dp', 'expert')
The draws below stay inside these ranges and needn't reach their ends.
Inputs may be any that keep to these rules, and one draw needn't show every extreme that they name: `lengths`: the 2 sequences dealt to one block fill its 128 rows; some sequence has exactly 96 tokens. A permutation of the sequence numbers. `routes`: each row names 8 different experts; among the 32 aligned blocks of 128 rows (the rows of one device), no expert is named in more than 80 rows of a block, and some expert reaches 80.
All inputs are finite; a program needn't handle non-finite values.
Results may differ from the reference program's by a relative error of at most 0.017.
Values may be sent and summed in bfloat16 or wider, within the bound.
No kernel may reach another device: no remote copies, remote signals or barrier semaphores. Data moves between devices by JAX's collectives and lax.ppermute only.
A program may use at most 384 MiB of HBM per device.

```python
import math
import jax
import jax.numpy as jnp
import numpy as np
from jax import lax

D = 2048
HEADS = 16
HEAD_DIM = 128
EFF = 1024
TOP = 8
EXPERTS = 16
TOK_DEV = 128
SEQ_DEV = 2
MINLEN = 32
MAXLEN = 96
CAP = 80
TOKENS = 4096
NSEQ = 64


def dealing(base_key):
    devices = NSEQ // SEQ_DEV
    first_len = jax.random.randint(jax.random.fold_in(base_key, 11), (devices,), MINLEN, MAXLEN + 1)
    chosen = jax.random.randint(jax.random.fold_in(base_key, 12), (), 0, devices)
    first_len = jnp.where(jnp.arange(devices) == chosen, MAXLEN, first_len)
    packed = jnp.stack([first_len, TOK_DEV - first_len], axis=1).reshape(-1).astype(jnp.int32)
    dealt_order = jax.random.permutation(jax.random.fold_in(base_key, 13), NSEQ).astype(jnp.int32)
    lengths = jnp.zeros((NSEQ,), jnp.int32).at[dealt_order].set(packed)
    return (lengths, dealt_order)


def draw_lengths(key, part):
    shared = dealing(key)
    return shared[0]


def draw_permutation(key, part):
    shared = dealing(key)
    return shared[1]


def steps_of(rng, dims, shards, low, top_value):
    def one(axis_at, shards_of):
        heights = jax.random.uniform(jax.random.fold_in(jax.random.fold_in(rng, 6), axis_at), (shards_of,), jnp.float32, low / len(shards), top_value / len(shards))
        return jnp.repeat(jnp.exp(heights), dims[axis_at] // shards_of).reshape((-1,) + (1,) * (len(dims) - axis_at - 1))

    loudness = one(*shards[0])
    for cut in shards[1:]:
        loudness = loudness * one(*cut)
    return loudness


def assign_block(key, own, number, rows, number_of, top, most, lean):
    ranking = jax.random.permutation(key, number_of)
    crowded, common = load_shares(number_of, rows * top, most, lean, True), load_shares(number_of, rows * top, most, lean, False)
    places = jnp.arange(number_of)

    def named(sizes, rotation):
        used = int((sizes > 0).sum())
        fixed = max(1, used // 4)
        shifted = fixed + (places - fixed + rotation * (used - fixed)) % max(1, number_of - fixed)
        return jnp.zeros((number_of,), jnp.int32).at[ranking[jnp.where(places < fixed, places, shifted)]].set(jnp.asarray(sizes, jnp.int32))

    sizes = jnp.where(number % 4 == 0, named(crowded, number // 4), named(common, number - number // 4 - 1))
    mixed = jax.random.permutation(jax.random.fold_in(own, 3), number_of)
    donor, receiver = mixed[0:number_of // 2 * 2:2], mixed[1:number_of // 2 * 2:2]
    slack = jnp.minimum(sizes[donor] - 1, most - sizes[receiver]) // 2
    slack = jnp.where((donor == ranking[0]) | (receiver == ranking[0]) | (sizes[receiver] == 0), 0, jnp.maximum(slack, 0))
    shifted = jax.random.randint(jax.random.fold_in(own, 4), (number_of // 2,), 0, 1 << 20) % (slack + 1)
    sizes = sizes.at[donor].add(-shifted).at[receiver].add(shifted)
    members = jnp.searchsorted(jnp.cumsum(sizes), jnp.arange(rows * top), side="right").astype(jnp.int32)
    listing = members.reshape(top, rows).T
    listing = listing[jax.random.permutation(jax.random.fold_in(own, 1), rows)]
    rotation = jax.random.randint(jax.random.fold_in(own, 2), (rows, 1), 0, top)
    return jnp.take_along_axis(listing, (jnp.arange(top)[None, :] + rotation) % top, axis=1)


def load_shares(amount, total, most, slope, full):
    portions = [(1 << 20) // math.isqrt(grade ** slope) + 1 for grade in range(1, amount + 1)]
    largest = most if full else min(most, max(-(-total // amount), total * portions[0] // sum(portions)))
    least = 1 if total - largest >= amount - 1 else 0
    given, surplus = [largest] + [least] * (amount - 1), total - largest - least * (amount - 1)
    while surplus > 0:
        movable = [i for i in range(1, amount) if given[i] < largest] or [i for i in range(1, amount) if given[i] < most]
        mass, budget = sum([portions[i] for i in movable]), surplus
        for i in movable:
            more = min(most - given[i], max(1, budget * portions[i] // mass), surplus)
            given[i] = given[i] + more
            surplus = surplus - more
    return np.array(given)


def bell_draw(own_key, shape, scale, reach, pieces=(), kind=jnp.bfloat16):
    values = jax.random.normal(own_key, shape, jnp.float32) * scale
    if len(pieces) > 0:
        values = steps_of(own_key, shape, pieces, -0.22, 0.18) * values
    return jnp.clip(values, min=-reach, max=reach).astype(kind)


def setup_inputs(seed: int = 0) -> dict:
    key_of = jax.random.split(jax.random.key(seed), 12)
    tokens = bell_draw(key_of[0], (TOKENS, D), 1.0, 6.0, ((0, 32),))
    lengths = draw_lengths(jax.random.fold_in(key_of[11], 71), 0)
    permutation = draw_permutation(jax.random.fold_in(key_of[11], 71), 0)
    routes_keys = jax.random.split(jax.random.fold_in(key_of[3], 1), TOKENS // TOK_DEV)
    routes_turns = jax.random.permutation(jax.random.fold_in(key_of[3], 3), TOKENS // TOK_DEV)
    routes = jax.vmap(lambda own, number: assign_block(jax.random.fold_in(key_of[3], 2), own, number, TOK_DEV, EXPERTS, TOP, CAP, 1))(routes_keys, routes_turns).reshape((TOKENS, TOP))
    norm_gains = jnp.clip(1.0 + 0.15 * jax.random.normal(key_of[4], (D, 4), jnp.float32), 0.25, 1.75).astype(jnp.bfloat16)
    w_qkv = bell_draw(key_of[5], (D, 3 * D), D ** -0.5, 0.125, ((0, 32),))
    w_out = bell_draw(key_of[6], (D, D), (D // 32) ** -0.5, 0.75, ((0, 32),))
    router = bell_draw(key_of[7], (D, EXPERTS), (4 * D) ** -0.5, 0.0625, ((0, 32),))
    w_gate_up = bell_draw(key_of[8], (D, EXPERTS, 2 * EFF), D ** -0.5, 0.125, ((0, 8), (1, 4)))
    w_down = bell_draw(key_of[9], (D, EXPERTS, EFF), (EFF // 16) ** -0.5, 0.75, ((0, 8), (1, 4)))
    cotangent = bell_draw(key_of[10], (TOKENS, D), 1.0, 6.0, ((0, 32),))
    return {"tokens": tokens, "lengths": lengths, "permutation": permutation, "routes": routes, "norm_gains": norm_gains, "w_qkv": w_qkv, "w_out": w_out, "router": router, "w_gate_up": w_gate_up, "w_down": w_down, "cotangent": cotangent}


EPSILON = 1e-06
ROPE_BASE = 50000.0

@jax.custom_vjp
def low(v):
    return lax.optimization_barrier(v.astype(jnp.bfloat16)).astype(jnp.float32)

@jax.custom_vjp
def low_back(v):
    return v

def low_keep(v):
    return (low(v), None)

def low_pass(kept, grad):
    return (grad,)

def back_keep(v):
    return (v, None)

def back_low(kept, grad):
    return (low(grad),)
low.defvjp(low_keep, low_pass)
low_back.defvjp(back_keep, back_low)

def rms_scale(values, gain_vec):
    return values * lax.rsqrt(lax.optimization_barrier(jnp.mean(values * values, axis=-1, keepdims=True)) + EPSILON) * gain_vec

def rotate(values, cos_table, sin_table):
    half_dim = values.shape[-1] // 2
    first_half = values[..., :half_dim]
    second_half = values[..., half_dim:]
    return jnp.concatenate([first_half * cos_table - second_half * sin_table, second_half * cos_table + first_half * sin_table], axis=-1)

def angles(position):
    half_dim = HEAD_DIM // 2
    inverse = ROPE_BASE ** (-2.0 * jnp.arange(half_dim, dtype=jnp.float32) / HEAD_DIM)
    turned = position.astype(jnp.float32)[..., None] * inverse
    return (jnp.cos(turned)[..., None, :], jnp.sin(turned)[..., None, :])

def layout(lengths, permutation):
    dealt_lens = jnp.take(lengths, permutation).reshape(-1, SEQ_DEV)
    seq_ends = jnp.cumsum(dealt_lens, axis=1).astype(jnp.int32)
    places = jnp.arange(TOK_DEV, dtype=jnp.int32)
    segment = lax.optimization_barrier(jnp.sum((places[None, :, None] >= seq_ends[:, None, :]).astype(jnp.int32), axis=2)).astype(jnp.int32)
    starts = seq_ends - dealt_lens
    offset = lax.optimization_barrier(jnp.sum(jnp.where(segment[:, :, None] == jnp.arange(SEQ_DEV, dtype=jnp.int32)[None, None, :], starts[:, None, :], 0), axis=2)).astype(jnp.int32)
    return (segment, places[None, :] - offset)

def layer_forward(residual, weight_set, route_rows, segment, cos_table, sin_table):
    norm_gains, w_qkv, w_out, router, w_gate_up, w_down = weight_set
    tok_rows = residual.shape[0]
    model_width = residual.shape[1]
    highest = lax.Precision.HIGHEST
    normed = low(rms_scale(residual, norm_gains[:, 0]))
    proj_qkv = low_back(jnp.dot(normed, w_qkv, precision=highest))
    query_part = rms_scale(proj_qkv[:, :model_width], norm_gains[:, 1]).reshape(tok_rows, HEADS, HEAD_DIM)
    keys_part = rms_scale(proj_qkv[:, model_width:2 * model_width], norm_gains[:, 2]).reshape(tok_rows, HEADS, HEAD_DIM)
    values_low = low(proj_qkv[:, 2 * model_width:]).reshape(tok_rows, HEADS, HEAD_DIM)
    query_rot = low(rotate(query_part, cos_table, sin_table))
    keys_rot = low(rotate(keys_part, cos_table, sin_table))
    scores = low_back(jnp.einsum('thd,shd->hts', query_rot, keys_rot, precision=highest) * HEAD_DIM ** (-0.5))
    same_seq = segment[:, None] == segment[None, :]
    scores = jnp.where(same_seq[None], scores, -1e+30)
    row_peak = lax.optimization_barrier(jnp.max(scores, axis=2, keepdims=True))
    exp_scores = jnp.exp(scores - row_peak)
    attn_probs = low(exp_scores / lax.optimization_barrier(jnp.sum(exp_scores, axis=2, keepdims=True)))
    mixed = jnp.einsum('hts,shd->thd', attn_probs, values_low, precision=highest).reshape(tok_rows, model_width)
    mixed = low(low_back(mixed))
    hidden = residual + low_back(jnp.dot(mixed, w_out, precision=highest))
    moe_in = low(rms_scale(hidden, norm_gains[:, 3]))
    logits = low_back(jnp.dot(moe_in, router, precision=highest))
    picked = jnp.take_along_axis(logits, route_rows, axis=1)
    gate_prob = jax.nn.softmax(picked, axis=1)
    chosen = route_rows[:, :, None] == jnp.arange(EXPERTS, dtype=jnp.int32)[None, None, :]
    route_share = lax.optimization_barrier(jnp.sum(jnp.where(chosen, gate_prob[:, :, None], 0.0), axis=1))

    def expert_step(running, expert_item):
        gate_up, down_proj, expert_share = expert_item
        inside = low_back(moe_in)
        gate_up_val = low_back(jnp.dot(inside, gate_up, precision=highest))
        activation = low(jax.nn.silu(gate_up_val[:, :EFF]) * gate_up_val[:, EFF:])
        result = low(low_back(jnp.dot(activation, down_proj.T, precision=highest)))
        return (running + expert_share[:, None] * result, None)
    mixture, unused = lax.scan(jax.checkpoint(expert_step), jnp.zeros_like(hidden), (jnp.moveaxis(w_gate_up, 1, 0), jnp.moveaxis(w_down, 1, 0), route_share.T))
    return hidden + mixture

def reference(tokens, lengths, permutation, routes, norm_gains, w_qkv, w_out, router, w_gate_up, w_down, cotangent):
    segment, position = layout(lengths, permutation)
    cos_table, sin_table = angles(position)
    blocks = segment.shape[0]
    residual = tokens.astype(jnp.float32).reshape(blocks, TOK_DEV, D)
    route_blocks = routes.reshape(blocks, TOK_DEV, TOP)
    weight_set = (norm_gains.astype(jnp.float32), w_qkv.astype(jnp.float32), w_out.astype(jnp.float32), router.astype(jnp.float32), w_gate_up.astype(jnp.float32), w_down.astype(jnp.float32))

    def whole_pass(residual_all, weight_all):

        def one_block(block_item):
            return layer_forward(block_item[0], weight_all, block_item[1], block_item[2], block_item[3], block_item[4])
        return lax.map(jax.checkpoint(one_block), (residual_all, route_blocks, segment, cos_table, sin_table))
    output, pullback = jax.vjp(whole_pass, residual, weight_set)
    grad_residual, grad_weights = pullback(cotangent.astype(jnp.float32).reshape(blocks, TOK_DEV, D))
    return (output.reshape(-1, D), grad_residual.reshape(-1, D), grad_weights[0], grad_weights[1], grad_weights[2], grad_weights[3], grad_weights[4], grad_weights[5])
```

```python
import jax
import jax.numpy as jnp
from jax import lax
from jax.sharding import PartitionSpec as P

HEADS = 16
HEAD_DIM = 128
SEQ_DEV = 2
EPSILON = 1e-06
ROPE_BASE = 50000.0
EXTRA = 128

F32 = jnp.float32
BF16 = jnp.bfloat16


def dot(a, b, dims, out=F32):
    return lax.dot_general(a, b, (dims, ((), ())), preferred_element_type=F32).astype(out)


def nn(a, b, out=F32):
    return dot(a, b, ((1,), (0,)), out)


def nt(a, b, out=F32):
    return dot(a, b, ((1,), (1,)), out)


def tn(a, b, out=F32):
    return dot(a, b, ((0,), (0,)), out)


def flip(v, bit):
    return lax.ppermute(v, "dp", [(i, i ^ bit) for i in range(lax.axis_size("dp"))])


def shift(v, step):
    n = lax.axis_size("expert")
    return lax.ppermute(v, "expert", [(i, i + step) for i in range(n) if 0 <= i + step < n])


def gather_line(v):
    n = lax.axis_size("expert")
    rows = v.shape[0]
    below, above = [v], [v]
    for _ in range(n - 1):
        below.append(shift(below[-1], 1))
        above.append(shift(above[-1], -1))
    line = jnp.concatenate(below[:0:-1] + above, axis=0)
    start = (n - 1 - lax.axis_index("expert")) * rows
    return lax.dynamic_slice_in_dim(line, start, n * rows, axis=0)


def bits_of(low, high):
    out = []
    while low < high:
        out.append(low)
        low *= 2
    return out


def pick(v, index, axis):
    return lax.dynamic_index_in_dim(v, index, axis, keepdims=False)


def spread(w):
    rows, local, k = w.shape
    n = lax.axis_size("dp")
    me = lax.axis_index("dp")
    own = lax.rem(me, local)
    have = {(0, e): pick(w, own ^ e, 1) for e in range(local)}
    groups = []
    for bit in bits_of(1, local):
        keys = sorted(key for key in have if key[1] & bit)
        got = flip(jnp.stack([have.pop(key) for key in keys]), bit)
        for at, key in enumerate(keys):
            have[(key[0] ^ bit, key[1] ^ bit)] = got[at]
    rows_of = {key[0]: v for key, v in have.items()}
    for bit in bits_of(local, n):
        for half in (0, 1):
            keys = sorted(r for r in rows_of if r < bit and (r & (local // 2) > 0) == (half == 1))
            got = flip(jnp.stack([rows_of[r] for r in keys]), bit)
            for at, r in enumerate(keys):
                rows_of[r ^ bit] = got[at]
    full = jnp.zeros((n, rows, k), w.dtype)
    for r, v in rows_of.items():
        full = lax.dynamic_update_index_in_dim(full, v, me ^ r, 0)
    return full.reshape(n * rows, k)


def collect(g, local):
    n = lax.axis_size("dp")
    me = lax.axis_index("dp")
    own = lax.rem(me, local)
    rows, k = g.shape[0] // n, g.shape[1]
    g = g.reshape(n, rows, k)
    held = {r: pick(g, me ^ r, 0) for r in range(n)}
    for bit in reversed(bits_of(local, n)):
        keys = sorted(r for r in held if r & bit)
        got = flip(jnp.stack([held.pop(r) for r in keys]), bit)
        for at, r in enumerate(keys):
            held[r ^ bit] = (held[r ^ bit].astype(F32) + got[at].astype(F32)).astype(BF16)
    have = {(r, 0): v for r, v in held.items()}
    for bit in reversed(bits_of(1, local)):
        keys = sorted(key for key in have if key[0] & bit)
        got = flip(jnp.stack([have.pop(key) for key in keys]), bit)
        for at, key in enumerate(keys):
            have[(key[0] ^ bit, key[1] ^ bit)] = got[at]
    stacked = jnp.stack([have[(0, e)] for e in range(local)])
    return jnp.stack([pick(stacked, own ^ e, 0) for e in range(local)], axis=1).astype(F32)


def share(v, local):
    for bit in reversed(bits_of(1, local)):
        v = jnp.concatenate([v, flip(v, bit)], axis=0)
    return v


def unshare(v, local):
    for bit in bits_of(1, local):
        half = v.shape[0] // 2
        v = (v[:half].astype(F32) + flip(v[half:], bit).astype(F32)).astype(BF16)
    return v


def inv_rms(v):
    return lax.rsqrt(jnp.mean(v * v, axis=-1, keepdims=True) + EPSILON)


def rms_back(v, r, gain, c):
    gc = gain * c
    return r * gc - v * (r * r * r) * jnp.mean(v * gc, axis=-1, keepdims=True)


def rotate(v, cos, sin):
    half = v.shape[-1] // 2
    u, w = v[..., :half], v[..., half:]
    return jnp.concatenate([u * cos - w * sin, w * cos + u * sin], axis=-1)


def on_device(
    tokens,
    lengths,
    permutation,
    routes,
    norm_gains,
    w_qkv,
    w_out,
    router,
    w_gate_up,
    w_down,
    cotangent,
):
    rows, width = tokens.shape
    zs = lax.axis_size("expert")
    dps = lax.axis_size("dp")
    z = lax.axis_index("expert")
    dp = lax.axis_index("dp")
    local = w_gate_up.shape[1]
    ff = w_down.shape[2]
    experts = router.shape[1]
    own_rows = w_qkv.shape[0]
    cols = width // zs
    heads = HEADS // zs
    scale = HEAD_DIM ** (-0.5)
    expert = z * local + lax.rem(dp, local)

    extra = jnp.concatenate(
        [router, norm_gains, jnp.zeros((own_rows, EXTRA - experts - 4), BF16)], axis=1
    )
    parts = w_qkv.reshape(own_rows, 3, zs, cols)
    sent = jnp.stack(
        [
            jnp.concatenate([parts[:, i, e] for i in range(3)] + [extra], axis=1)
            for e in range(zs)
        ]
    )
    mine = lax.all_to_all(sent, "expert", split_axis=0, concat_axis=0, tiled=True)
    attn_w = lax.all_gather(
        mine.reshape(zs * own_rows, 3 * cols + EXTRA), "dp", axis=0, tiled=True
    )
    qkv_w = attn_w[:, : 3 * cols]
    router_full = attn_w[:, 3 * cols : 3 * cols + experts]
    gains = attn_w[:, 3 * cols + experts : 3 * cols + experts + 4].astype(F32).T
    moved = [(b, (b % dps) * zs + b // dps) for b in range(dps * zs)]
    out_w = lax.all_gather(
        lax.ppermute(w_out, ("dp", "expert"), moved), "dp", axis=0, tiled=True
    )

    x_all = gather_line(tokens)
    mask = jnp.sum(
        (routes[:, :, None] == jnp.arange(experts, dtype=jnp.int32)).astype(BF16), axis=1
    )
    mask_pad = jnp.concatenate([mask, jnp.zeros((rows, EXTRA - experts), BF16)], axis=1)
    g_line = gather_line(jnp.concatenate([cotangent, mask_pad], axis=1))
    w_gu = spread(w_gate_up)
    w_dn = spread(w_down)
    g_share = share(g_line, local)
    g_all = g_share[:, :width]
    mask_all = g_share[:, width : width + experts].astype(F32)

    dealt = lax.dynamic_slice_in_dim(permutation, dp * zs * SEQ_DEV, zs * SEQ_DEV)
    lens = jnp.take(lengths, dealt).reshape(zs, SEQ_DEV)
    ends = jnp.cumsum(lens, axis=1)
    places = jnp.arange(rows, dtype=jnp.int32)
    segment = jnp.sum((places[None, :, None] >= ends[:, None, :]).astype(jnp.int32), axis=2)
    starts = ends - lens
    offset = jnp.sum(
        jnp.where(
            segment[:, :, None] == jnp.arange(SEQ_DEV, dtype=jnp.int32), starts[:, None, :], 0
        ),
        axis=2,
    )
    half = HEAD_DIM // 2
    inverse = ROPE_BASE ** (-2.0 * jnp.arange(half, dtype=F32) / HEAD_DIM)
    turned = (places[None] - offset).astype(F32)[..., None] * inverse
    cos, sin = jnp.cos(turned)[:, :, None, :], jnp.sin(turned)[:, :, None, :]
    same = (segment[:, :, None] == segment[:, None, :])[:, None]

    xf = x_all.astype(F32)
    r_attn = inv_rms(xf)
    a_all = (xf * r_attn * gains[0]).astype(BF16)
    qkv = nn(a_all, qkv_w)
    q, k, v = qkv[:, :cols], qkv[:, cols : 2 * cols], qkv[:, 2 * cols :]
    squares = lax.psum(
        jnp.stack([jnp.sum(q * q, axis=1), jnp.sum(k * k, axis=1)]), "expert"
    )
    r_q = lax.rsqrt(squares[0] / width + EPSILON)[:, None]
    r_k = lax.rsqrt(squares[1] / width + EPSILON)[:, None]
    gain_q = lax.dynamic_slice_in_dim(gains[1], z * cols, cols)
    gain_k = lax.dynamic_slice_in_dim(gains[2], z * cols, cols)
    split = (zs, rows, heads, HEAD_DIM)
    qr = rotate((q * r_q * gain_q).reshape(split), cos, sin).astype(BF16)
    kr = rotate((k * r_k * gain_k).reshape(split), cos, sin).astype(BF16)
    vb = v.astype(BF16).reshape(split)
    s = jnp.einsum("bthd,bshd->bhts", qr, kr, preferred_element_type=F32) * scale
    s = jnp.where(same, s, -1e30)
    es = jnp.exp(s - jnp.max(s, axis=3, keepdims=True))
    p = es / jnp.sum(es, axis=3, keepdims=True)
    pb = p.astype(BF16)
    o = (
        jnp.einsum("bhts,bshd->bthd", pb, vb, preferred_element_type=F32)
        .reshape(zs * rows, cols)
        .astype(BF16)
    )
    added = lax.psum_scatter(
        nn(o, out_w, BF16), "expert", scatter_dimension=0, tiled=True
    ).astype(F32)
    hid = tokens.astype(F32) + added
    r_ffn = inv_rms(hid)
    m = (hid * r_ffn * gains[3]).astype(BF16)
    m_line = lax.all_gather(m, "expert", axis=0, tiled=True)
    m_all = share(m_line, local)

    def gates(rows_m, rows_mask):
        logits = jnp.where(rows_mask > 0, nn(rows_m, router_full), -1e30)
        e = jnp.where(
            rows_mask > 0, jnp.exp(logits - jnp.max(logits, axis=1, keepdims=True)), 0.0
        )
        return e / jnp.sum(e, axis=1, keepdims=True)

    mine_e = (jnp.arange(experts) == expert).astype(F32)
    gate = jnp.sum(gates(m_all, mask_all) * mine_e, axis=1, keepdims=True)
    gw = nn(g_all, w_dn)
    gu = nn(m_all, w_gu)
    g, u = gu[:, :ff], gu[:, ff:]
    sg = jax.nn.sigmoid(g)
    act = (g * sg * u).astype(BF16).astype(F32)
    gact = (gate * act).astype(BF16)
    dgate = jnp.sum(act * gw, axis=1, keepdims=True)
    dact = gate * gw
    dgu = jnp.concatenate(
        [dact * u * (sg * (1.0 + g * (1.0 - sg))), dact * (g * sg)], axis=1
    ).astype(BF16)
    dg_e = jnp.where(gate > 0, dgate, 0.0) * mine_e
    dg_hi = dg_e.astype(BF16)
    dg_lo = (dg_e - dg_hi.astype(F32)).astype(BF16)
    dg_pad = jnp.concatenate(
        [dg_hi, dg_lo, jnp.zeros((dg_e.shape[0], EXTRA - 2 * experts), BF16)], axis=1
    )
    dm_part = jnp.concatenate([nt(dgu, w_gu, BF16), dg_pad], axis=1)
    dm = lax.psum_scatter(
        unshare(dm_part, local), "expert", scatter_dimension=0, tiled=True
    ).astype(F32)
    y = lax.psum_scatter(
        unshare(nt(gact, w_dn, BF16), local), "expert", scatter_dimension=0, tiled=True
    ).astype(F32)
    output = hid + y
    grad_gu = collect(tn(m_all, dgu, BF16), local)
    grad_dn = collect(tn(g_all, gact, BF16), local)

    gate_own = gates(m, mask.astype(F32))
    dgates = dm[:, width : width + experts] + dm[:, width + experts : width + 2 * experts]
    dz = (
        gate_own * (dgates - jnp.sum(gate_own * dgates, axis=1, keepdims=True))
    ).astype(BF16)
    dmt = nt(dz, router_full) + dm[:, :width]
    router_part = tn(m, dz)
    grad_out = cotangent.astype(F32)
    dh = grad_out + rms_back(hid, r_ffn, gains[3], dmt)
    gain_ffn = jnp.sum(dmt * hid * r_ffn, axis=0)

    dhb = lax.all_gather(dh.astype(BF16), "expert", axis=0, tiled=True)
    do = nt(dhb, out_w, BF16).reshape(split)
    grad_out_w = lax.psum_scatter(
        tn(o, dhb, BF16), "dp", scatter_dimension=0, tiled=True
    )
    grad_w_out = lax.ppermute(
        grad_out_w, ("dp", "expert"), [(b, a) for a, b in moved]
    ).astype(F32)
    dp_ = jnp.einsum("bthd,bshd->bhts", do, vb, preferred_element_type=F32)
    dv = jnp.einsum("bhts,bthd->bshd", pb, do, preferred_element_type=F32)
    ds = (p * (dp_ - jnp.sum(p * dp_, axis=3, keepdims=True))).astype(BF16)
    dqr = jnp.einsum("bhts,bshd->bthd", ds, kr, preferred_element_type=F32) * scale
    dkr = jnp.einsum("bhts,bthd->bshd", ds, qr, preferred_element_type=F32) * scale
    dqn = rotate(dqr, cos, -sin).reshape(zs * rows, cols)
    dkn = rotate(dkr, cos, -sin).reshape(zs * rows, cols)
    means = lax.psum(
        jnp.stack(
            [jnp.sum(q * (gain_q * dqn), axis=1), jnp.sum(k * (gain_k * dkn), axis=1)]
        ),
        "expert",
    )
    dq = r_q * gain_q * dqn - q * (r_q * r_q * r_q) * (means[0] / width)[:, None]
    dk = r_k * gain_k * dkn - k * (r_k * r_k * r_k) * (means[1] / width)[:, None]
    dqkv = jnp.concatenate([dq, dk, dv.reshape(zs * rows, cols)], axis=1).astype(BF16)
    da_part = nt(dqkv, qkv_w)
    da = lax.psum_scatter(
        da_part.astype(BF16), "expert", scatter_dimension=0, tiled=True
    ).astype(F32)
    gain_attn = jnp.sum(da_part * (xf * r_attn), axis=0)
    at = z * cols
    zero = jnp.zeros((width,), F32)
    gain_query = lax.dynamic_update_slice_in_dim(zero, jnp.sum(dqn * q * r_q, axis=0), at, 0)
    gain_keys = lax.dynamic_update_slice_in_dim(zero, jnp.sum(dkn * k * r_k, axis=0), at, 0)
    gain_part = jnp.stack([gain_attn, gain_query, gain_keys, gain_ffn], axis=1)
    extra_part = jnp.concatenate(
        [router_part, gain_part, jnp.zeros((width, EXTRA - experts - 4), F32)], axis=1
    ).astype(BF16)
    qkv_part = jnp.concatenate([tn(a_all, dqkv, BF16), extra_part], axis=1)
    summed = lax.psum_scatter(qkv_part, "dp", scatter_dimension=0, tiled=True)
    back = lax.all_to_all(
        summed.reshape(zs, own_rows, 3 * cols + EXTRA),
        "expert",
        split_axis=0,
        concat_axis=0,
        tiled=True,
    ).astype(F32)
    grad_w_qkv = jnp.concatenate(
        [back[e, :, i * cols : (i + 1) * cols] for i in range(3) for e in range(zs)], axis=1
    )
    extra_sum = jnp.sum(back[:, :, 3 * cols :], axis=0)
    grad_router = extra_sum[:, :experts]
    grad_gains = extra_sum[:, experts : experts + 4]

    x_own = tokens.astype(F32)
    grad_tokens = dh + rms_back(x_own, inv_rms(x_own), gains[0], da)
    return (
        output,
        grad_tokens,
        grad_gains,
        grad_w_qkv,
        grad_w_out,
        grad_router,
        grad_gu,
        grad_dn,
    )


def solution(mesh):
    both = P(("dp", "expert"), None)
    experts = P("dp", "expert", None)
    return jax.shard_map(
        on_device,
        mesh=mesh,
        in_specs=(both, P(), P(), both, both, both, both, both, experts, experts, both),
        out_specs=(both, both, both, both, both, both, experts, experts),
        check_vma=False,
    )
```

```python
import functools

import jax
import jax.numpy as jnp
from jax import lax
from jax.experimental import pallas as pl
from jax.experimental.pallas import tpu as pltpu
from jax.sharding import PartitionSpec as P

HEADS = 16
HEAD_DIM = 128
SEQ_DEV = 2
EPSILON = 1e-06
ROPE_BASE = 50000.0
CAP = 80
EXTRA = 128
VMEM = 56 * 2**20

F32 = jnp.float32
BF16 = jnp.bfloat16


def dot(a, b, dims, out=F32):
    return lax.dot_general(a, b, (dims, ((), ())), preferred_element_type=F32).astype(out)


def nn(a, b, out=F32):
    return dot(a, b, ((1,), (0,)), out)


def nt(a, b, out=F32):
    return dot(a, b, ((1,), (1,)), out)


def tn(a, b, out=F32):
    return dot(a, b, ((0,), (0,)), out)


def flip(v, bit):
    return lax.ppermute(v, "dp", [(i, i ^ bit) for i in range(lax.axis_size("dp"))])


def ring(n):
    return [*range(0, n, 2), *reversed(range(1, n, 2))]


def hop(v, back=False):
    order = ring(lax.axis_size("expert"))
    pairs = list(zip(order, order[1:] + order[:1], strict=True))
    return lax.ppermute(v, "expert", [(b, a) for a, b in pairs] if back else pairs)


def gather_ring(v):
    out = [v]
    for _ in range(lax.axis_size("expert") - 1):
        out.append(hop(out[-1]))
    return out


def places_in_ring():
    n = lax.axis_size("expert")
    at = [ring(n).index(i) for i in range(n)]
    at = jnp.asarray(at, jnp.int32)
    return lax.rem(at[lax.axis_index("expert")] - at + n, n)


def by_line(blocks):
    where = places_in_ring()
    stacked = jnp.stack(blocks)
    return jnp.concatenate([pick(stacked, where[i], 0) for i in range(len(blocks))], axis=0)


def bits_of(low, high):
    out = []
    while low < high:
        out.append(low)
        low *= 2
    return out


def pick(v, index, axis):
    return lax.dynamic_index_in_dim(v, index, axis, keepdims=False)


def tie(*values):
    return lax.optimization_barrier(values)


class Weights:
    def __init__(self, gate_up, down):
        self.rows, self.local, wide = gate_up.shape
        self.k = wide + down.shape[2]
        self.n = lax.axis_size("dp")
        self.me = lax.axis_index("dp")
        own = lax.rem(self.me, self.local)
        self.have = {
            (0, e): jnp.concatenate([pick(gate_up, own ^ e, 1), pick(down, own ^ e, 1)], axis=1)
            for e in range(self.local)
        }
        self.steps = self.plan()

    def plan(self):
        if self.local == 4 and self.n == 8:
            return [
                [([(0, 1), (0, 3)], 1), ([(0, 0)], 4)],
                [([(0, 2)], 2), ([(1, 0)], 4)],
                [([(1, 2)], 2), ([(2, 0)], 4)],
                [([(3, 0)], 4)],
            ]
        out, rows = [], [0]
        for bit in bits_of(1, self.local):
            left = [e for e in range(self.local) if e % bit == 0]
            out.append([([(r, e) for r in rows for e in left if e & bit], bit)])
            rows = rows + [r ^ bit for r in rows]
        for bit in bits_of(self.local, self.n):
            out.append([([(r, 0) for r in rows], bit)])
            rows = rows + [r ^ bit for r in rows]
        return out

    def step(self, at):
        if at >= len(self.steps):
            return
        for keys, bit in self.steps[at]:
            keep = keys[0][1] == 0
            v = [self.have[key] if keep else self.have.pop(key) for key in keys]
            got = flip(jnp.stack(v) if len(v) > 1 else v[0][None], bit)
            for i, (r, e) in enumerate(keys):
                self.have[(r ^ bit, e if keep else e ^ bit)] = got[i]

    def join(self, *values):
        keys = sorted(self.have)
        out = tie(*values, *[self.have[key] for key in keys])
        for key, v in zip(keys, out[len(values) :], strict=True):
            self.have[key] = v
        return out[: len(values)]

    def whole(self):
        for at in range(4, len(self.steps)):
            self.step(at)
        rows = [self.have[key] for key in sorted(self.have)]
        return jnp.concatenate(rows, axis=0)


class Tail:
    def __init__(self, held, local, n):
        self.local = local
        self.have = {(r, 0): v for r, v in held.items()}
        self.own = lax.rem(lax.axis_index("dp"), local)
        for bit in reversed(bits_of(local, n // 2)):
            for key in sorted(k for k in self.have if k[0] & bit):
                got = flip(self.have.pop(key), bit)
                to = (key[0] ^ bit, 0)
                self.have[to] = add(self.have[to], got)
        self.bits = list(reversed(bits_of(1, local)))

    def step(self, at):
        if at >= len(self.bits):
            return
        bit = self.bits[at]
        keys = sorted(key for key in self.have if key[0] & bit)
        got = flip(jnp.stack([self.have.pop(key) for key in keys]), bit)
        for i, (r, e) in enumerate(keys):
            self.have[(r ^ bit, e ^ bit)] = got[i]

    def join(self, *values):
        keys = sorted(self.have)
        out = tie(*values, *[self.have[key] for key in keys])
        for key, v in zip(keys, out[len(values) :], strict=True):
            self.have[key] = v
        return out[: len(values)]

    def done(self, ff):
        stacked = jnp.stack([self.have[(0, e)] for e in range(self.local)])
        blocks = [pick(stacked, self.own ^ e, 0) for e in range(self.local)]
        return (
            jnp.stack([b[:, : 2 * ff] for b in blocks], axis=1).astype(F32),
            jnp.stack([b[:, 2 * ff :] for b in blocks], axis=1).astype(F32),
        )


def fan(pieces, low):
    out = [list(pieces)]
    for bit in bits_of(1, low):
        out = out + [[flip(x, bit) for x in xs] for xs in out]
    return out


def add(a, b):
    return (a.astype(F32) + b.astype(F32)).astype(BF16)


def match(pieces, like):
    if len(pieces) == len(like):
        return pieces
    step = like[0].shape[0]
    return [x[i : i + step] for x in pieces for i in range(0, x.shape[0], step)]


def fold(parts):
    parts = list(parts)
    while len(parts) > 1:
        half = len(parts) // 2
        for i in range(half):
            got = match([flip(x, half) for x in reversed(parts[half + i])][::-1], parts[i])
            parts[i] = [add(a, b) for a, b in zip(parts[i], got, strict=True)]
        parts = parts[:half]
    return parts[0]


def scatter_dp(part, rows):
    n = lax.axis_size("dp")
    held = [part[r * rows : (r + 1) * rows] for r in range(n)]
    for bit in bits_of(1, n):
        odd = jnp.concatenate(held[1::2], axis=0) if len(held) > 2 else held[1]
        got = flip(odd, bit)
        held = [add(v, got[i * rows : (i + 1) * rows]) for i, v in enumerate(held[::2])]
    return held[0]


def blocks_of(parts, tok):
    return [(i, at) for i, p in enumerate(parts) for at in range(0, p.shape[0], tok)]


def onehot(pos_ref, b):
    slot = lax.broadcasted_iota(jnp.int32, (CAP, pos_ref.shape[1]), 0)
    return slot == pos_ref[b : b + 1, :]


def mm(a, b, dims):
    return lax.dot_general(a, b, (dims, ((), ())), preferred_element_type=F32)


def front_kernel(count, me, *refs):
    parts, (pos, wd, rows_out, gw) = refs[:count], refs[count:]
    tok = pos.shape[1]
    width = rows_out.shape[1]

    @pl.when(pl.program_id(0) == 0)
    def _():
        for b, (i, at) in enumerate(blocks_of(parts, tok)):
            part = parts[i][at : at + tok, :width]
            hot = onehot(pos, b).astype(BF16)
            found = mm(hot, part, ((1,), (0,))).astype(BF16)
            to_distance(rows_out, slice(b * CAP, (b + 1) * CAP), found, me[0])

    gw[...] = mm(rows_out[...], wd[...], ((1,), (0,)))


def front(parts, pos, weights, ff, me):
    count, width = len(parts), weights.shape[0]
    slots = pos.shape[0] * CAP
    tile = min(256, ff)
    first = (weights.shape[1] - ff) // tile
    whole = lambda x: pl.BlockSpec(x.shape, lambda n, me: (0, 0))
    return pl.pallas_call(
        functools.partial(front_kernel, count),
        grid_spec=pltpu.PrefetchScalarGridSpec(
            num_scalar_prefetch=1,
            grid=(ff // tile,),
            in_specs=[whole(x) for x in parts]
            + [whole(pos), pl.BlockSpec((width, tile), lambda n, me: (0, first + n))],
            out_specs=[
                pl.BlockSpec((slots, width), lambda n, me: (0, 0)),
                pl.BlockSpec((slots, tile), lambda n, me: (0, n)),
            ],
        ),
        out_shape=[
            jax.ShapeDtypeStruct((slots, width), BF16),
            jax.ShapeDtypeStruct((slots, ff), F32),
        ],
        compiler_params=pltpu.CompilerParams(vmem_limit_bytes=VMEM),
        cost_estimate=pl.CostEstimate(
            flops=2 * slots * width * ff,
            bytes_accessed=2 * width * ff + 6 * slots * width,
            transcendentals=0,
        ),
        name="front",
    )(me, *parts, pos, weights)


def to_distance(ref, rows, value, me):
    n = lax.axis_size("dp")
    wide = value.shape[1] // n
    for c in range(n):
        at = pl.multiple_of((me ^ c) * wide, wide)
        ref[rows, pl.ds(at, wide)] = value[:, c * wide : (c + 1) * wide]


def expert_kernel(count, expert, *refs):
    parts = refs[:count]
    pos, named, router, wg, wu, gw = refs[count : count + 6]
    backs = refs[count + 6 : 2 * count + 6]
    rows_out, dg_out, du_out, gact_out, acc, gate, dgate = refs[2 * count + 6 :]
    n = pl.program_id(0)
    tok = pos.shape[1]
    width = rows_out.shape[1]
    experts = router.shape[0]

    @pl.when(n == 0)
    def _():
        for b, (i, first) in enumerate(blocks_of(parts, tok)):
            at = slice(b * CAP, (b + 1) * CAP)
            part = parts[i][first : first + tok, :]
            hot = onehot(pos, b)
            found = mm(hot.astype(BF16), part, ((1,), (0,))).astype(BF16)
            to_distance(rows_out, at, found, expert[1])
            chosen = named[b] > 0
            logits = jnp.where(chosen, mm(router[...], part, ((1,), (1,))), -1e30)
            e = jnp.where(chosen, jnp.exp(logits - jnp.max(logits, axis=0, keepdims=True)), 0.0)
            gates = e / jnp.sum(e, axis=0, keepdims=True)
            mine = lax.broadcasted_iota(jnp.int32, gates.shape, 0) == expert[0]
            row = jnp.sum(jnp.where(mine, gates, 0.0), axis=0, keepdims=True)
            gate[at, :] = jnp.sum(jnp.where(hot, row, 0.0), axis=1, keepdims=True)
            dgate[at, :] = jnp.zeros((CAP, 1), F32)

    rows = rows_out[...]
    g = mm(rows, wg[...], ((1,), (0,)))
    u = mm(rows, wu[...], ((1,), (0,)))
    sg = 1.0 / (1.0 + jnp.exp(-g))
    silu = g * sg
    act = (silu * u).astype(BF16).astype(F32)
    gw_v = gw[...]
    dgate[...] += jnp.sum(act * gw_v, axis=1, keepdims=True)
    gate_v = gate[...]
    gact_out[...] = (gate_v * act).astype(BF16)
    dact = gate_v * gw_v
    dg = (dact * u * (sg * (1.0 + g * (1.0 - sg)))).astype(BF16)
    du = (dact * silu).astype(BF16)
    dg_out[...] = dg
    du_out[...] = du
    back = mm(dg, wg[...], ((1,), (1,))) + mm(du, wu[...], ((1,), (1,)))

    @pl.when(n == 0)
    def _():
        acc[...] = back

    @pl.when(n > 0)
    def _():
        acc[...] += back

    @pl.when(n == pl.num_programs(0) - 1)
    def _():
        lane = lax.broadcasted_iota(jnp.int32, (CAP, EXTRA), 1)
        for b, (i, first) in enumerate(blocks_of(parts, tok)):
            at = slice(b * CAP, (b + 1) * CAP)
            to = slice(first, first + tok)
            hot = onehot(pos, b).astype(BF16)
            out = backs[i]
            found = mm(hot, acc[at, :].astype(BF16), ((0,), (0,))).astype(BF16)
            to_distance(out, to, found, expert[1])
            d = dgate[at, :]
            hi = d.astype(BF16).astype(F32)
            beside = jnp.where(
                lane == expert[0], hi, jnp.where(lane == experts + expert[0], d - hi, 0.0)
            ).astype(BF16)
            out[to, width:] = mm(hot, beside, ((0,), (0,))).astype(BF16)


def run_expert(parts, pos, named, router, weights, gw, expert, ff):
    count, width = len(parts), weights.shape[0]
    slots = pos.shape[0] * CAP
    tile = min(256, ff)
    steps = ff // tile
    whole = lambda x: pl.BlockSpec(x.shape, lambda n, e: (0,) * x.ndim)
    column = pl.BlockSpec((slots, tile), lambda n, e: (0, n))
    backs = [jax.ShapeDtypeStruct((x.shape[0], width + EXTRA), BF16) for x in parts]
    thin = jax.ShapeDtypeStruct((slots, ff), BF16)
    outs = pl.pallas_call(
        functools.partial(expert_kernel, count),
        grid_spec=pltpu.PrefetchScalarGridSpec(
            num_scalar_prefetch=1,
            grid=(steps,),
            in_specs=[whole(x) for x in parts]
            + [
                whole(pos),
                whole(named),
                whole(router),
                pl.BlockSpec((width, tile), lambda n, e: (0, n)),
                pl.BlockSpec((width, tile), lambda n, e: (0, steps + n)),
                column,
            ],
            out_specs=[whole(x) for x in backs]
            + [pl.BlockSpec((slots, width), lambda n, e: (0, 0)), column, column, column],
            scratch_shapes=[
                pltpu.VMEM((slots, width), F32),
                pltpu.VMEM((slots, 1), F32),
                pltpu.VMEM((slots, 1), F32),
            ],
        ),
        out_shape=backs
        + [jax.ShapeDtypeStruct((slots, width), BF16), thin, thin, thin],
        compiler_params=pltpu.CompilerParams(vmem_limit_bytes=VMEM),
        cost_estimate=pl.CostEstimate(
            flops=8 * slots * width * ff,
            bytes_accessed=4 * width * ff + 12 * slots * width,
            transcendentals=slots * ff,
        ),
        name="expert",
    )(expert, *parts, pos, named, router, weights, weights, gw)
    return outs[:count], outs[count:]


def result_kernel(count, me, gact, wd, pos, *outs):
    tok = pos.shape[1]
    y = mm(gact[...], wd[...], ((1,), (1,))).astype(BF16)
    for b, (i, at) in enumerate(blocks_of(outs, tok)):
        hot = onehot(pos, b).astype(BF16)
        outs[i][at : at + tok, :] = mm(
            hot, y[b * CAP : (b + 1) * CAP, :], ((0,), (0,))
        ).astype(BF16)


def result(gact, pos, weights, count, me):
    slots, ff = gact.shape
    width = weights.shape[0]
    tile = width // lax.axis_size("dp")
    last = (weights.shape[1] - ff) // ff
    out = jax.ShapeDtypeStruct((pos.shape[0] // count * pos.shape[1], width), BF16)
    return pl.pallas_call(
        functools.partial(result_kernel, count),
        grid_spec=pltpu.PrefetchScalarGridSpec(
            num_scalar_prefetch=1,
            grid=(width // tile,),
            in_specs=[
                pl.BlockSpec((slots, ff), lambda n, me: (0, 0)),
                pl.BlockSpec((tile, ff), lambda n, me: (n, last)),
                pl.BlockSpec(pos.shape, lambda n, me: (0, 0)),
            ],
            out_specs=[pl.BlockSpec((out.shape[0], tile), lambda n, me: (0, me[0] ^ n))] * count,
        ),
        out_shape=[out] * count,
        compiler_params=pltpu.CompilerParams(vmem_limit_bytes=VMEM),
        cost_estimate=pl.CostEstimate(
            flops=2 * slots * width * ff,
            bytes_accessed=2 * width * ff + 2 * count * out.shape[0] * width,
            transcendentals=0,
        ),
        name="result",
    )(me, gact, weights, pos)


def grads_kernel(count, *refs):
    out = refs[-1]
    ff = refs[2].shape[1]
    gate = up = down = 0.0
    for c in range(count):
        rows, gs, dg, du, gact = refs[5 * c : 5 * c + 5]
        gate = gate + mm(rows[...], dg[...], ((0,), (0,)))
        up = up + mm(rows[...], du[...], ((0,), (0,)))
        down = down + mm(gs[...], gact[...], ((0,), (0,)))
    out[0, :, :ff] = gate.astype(BF16)
    out[0, :, ff : 2 * ff] = up.astype(BF16)
    out[0, :, 2 * ff :] = down.astype(BF16)


def grads(chunks, first, blocks, rows):
    ff = chunks[0][2].shape[1]
    specs, ins = [], []
    for chunk in chunks:
        slots = chunk[0].shape[0]
        tall = pl.BlockSpec((slots, rows), lambda i: (0, first + i))
        flat = pl.BlockSpec((slots, ff), lambda i: (0, 0))
        specs += [tall, tall, flat, flat, flat]
        ins += list(chunk)
    slots = sum(chunk[0].shape[0] for chunk in chunks)
    return pl.pallas_call(
        functools.partial(grads_kernel, len(chunks)),
        grid=(blocks,),
        in_specs=specs,
        out_specs=pl.BlockSpec((1, rows, 3 * ff), lambda i: (i, 0, 0)),
        out_shape=jax.ShapeDtypeStruct((blocks, rows, 3 * ff), BF16),
        compiler_params=pltpu.CompilerParams(vmem_limit_bytes=VMEM),
        cost_estimate=pl.CostEstimate(
            flops=6 * slots * blocks * rows * ff,
            bytes_accessed=6 * slots * ff + 6 * blocks * rows * ff,
            transcendentals=0,
        ),
        name="grads",
    )(*ins)


def attn_grads_kernel(me, a, d, *rest):
    k = d.shape[1]
    out = rest[-1]
    out[:, :k] = mm(a[...], d[...], ((0,), (0,))).astype(BF16)
    if len(rest) > 1:
        out[:, k:] = rest[0][...]


def attn_grads(a, d, extra, me, first, stride):
    rows, width = a.shape
    n = lax.axis_size("dp")
    tile = width // n
    count = n // stride
    at = lambda i, me: me[0] ^ (first + stride * i)
    k = d.shape[1] + sum(e.shape[1] for e in extra)
    return pl.pallas_call(
        attn_grads_kernel,
        grid_spec=pltpu.PrefetchScalarGridSpec(
            num_scalar_prefetch=1,
            grid=(count,),
            in_specs=[
                pl.BlockSpec((rows, tile), lambda i, me: (0, at(i, me))),
                pl.BlockSpec(d.shape, lambda i, me: (0, 0)),
            ]
            + [pl.BlockSpec((tile, e.shape[1]), lambda i, me: (at(i, me), 0)) for e in extra],
            out_specs=pl.BlockSpec((tile, k), lambda i, me: (i, 0)),
        ),
        out_shape=jax.ShapeDtypeStruct((count * tile, k), BF16),
        compiler_params=pltpu.CompilerParams(vmem_limit_bytes=VMEM),
        cost_estimate=pl.CostEstimate(
            flops=2 * rows * width * k // stride,
            bytes_accessed=2 * (rows * width + rows * k + width * k // stride),
            transcendentals=0,
        ),
        name="attn_grads",
    )(me, a, d, *extra)


def scatter_wide(odd, even, rows):
    n = lax.axis_size("dp")
    got = flip(odd, 1)
    held = add(even, got)
    wide = held.shape[1] // 256 * 128
    sides = []
    for left, right, order in (
        (0, wide, bits_of(2, n)),
        (wide, held.shape[1], bits_of(2, n)[::-1]),
    ):
        side = {2 * i: held[i * rows : (i + 1) * rows, left:right] for i in range(n // 2)}
        sides.append((side, order))
    for at in range(len(sides[0][1])):
        for side, order in sides:
            bit = order[at]
            keys = sorted(r for r in side if r & bit)
            v = [side.pop(r) for r in keys]
            got = flip(jnp.concatenate(v, axis=0) if len(v) > 1 else v[0], bit)
            for i, r in enumerate(keys):
                side[r ^ bit] = add(side[r ^ bit], got[i * rows : (i + 1) * rows])
    return jnp.concatenate([side[0] for side, _ in sides], axis=1)


def inv_rms(v):
    return lax.rsqrt(jnp.mean(v * v, axis=-1, keepdims=True) + EPSILON)


def rms_back(v, r, gain, c):
    gc = gain * c
    return r * gc - v * (r * r * r) * jnp.mean(v * gc, axis=-1, keepdims=True)


def rotate(v, cos, sin):
    half = v.shape[-1] // 2
    u, w = v[..., :half], v[..., half:]
    return jnp.concatenate([u * cos - w * sin, w * cos + u * sin], axis=-1)


def on_device(
    tokens,
    lengths,
    permutation,
    routes,
    norm_gains,
    w_qkv,
    w_out,
    router,
    w_gate_up,
    w_down,
    cotangent,
):
    rows, width = tokens.shape
    zs = lax.axis_size("expert")
    dps = lax.axis_size("dp")
    z = lax.axis_index("expert")
    dp = lax.axis_index("dp")
    local = w_gate_up.shape[1]
    ff = w_down.shape[2]
    experts = router.shape[1]
    own_rows = w_qkv.shape[0]
    cols = width // zs
    heads = HEADS // zs
    scale = HEAD_DIM ** (-0.5)
    expert = z * local + lax.rem(dp, local)

    extra = jnp.concatenate(
        [router, norm_gains, jnp.zeros((own_rows, EXTRA - experts - 4), BF16)], axis=1
    )
    sent = jnp.stack(
        [
            jnp.concatenate(
                [w_qkv[:, i * width + e * cols : i * width + (e + 1) * cols] for i in range(3)]
                + [extra],
                axis=1,
            )
            for e in range(zs)
        ]
    )
    mine = lax.all_to_all(sent, "expert", split_axis=0, concat_axis=0, tiled=True)
    moved = [(b, (b % dps) * zs + b // dps) for b in range(dps * zs)]
    held = Weights(w_gate_up, w_down)
    first = dict(held.have)
    held.step(0)
    keys = sorted(set(first) & set(held.have))
    out = tie(mine, tokens, w_out, *[first[key] for key in keys])
    mine, tokens_now, out_rows = out[:3]
    for key, v in zip(keys, out[3:], strict=True):
        held.have[key] = v
    x_all = by_line(gather_ring(tokens_now))
    out_rows = lax.ppermute(out_rows, ("dp", "expert"), moved)
    attn_w = lax.all_gather(
        mine.reshape(zs * own_rows, 3 * cols + EXTRA), "dp", axis=0, tiled=True
    )
    mask = jnp.sum(
        (routes[:, :, None] == jnp.arange(experts, dtype=jnp.int32)).astype(BF16), axis=1
    )
    mask_pad = jnp.concatenate([mask, jnp.zeros((rows, EXTRA - experts), BF16)], axis=1)
    g_own = jnp.concatenate([cotangent, mask_pad], axis=1)
    attn_w, x_all, out_rows, g_own = held.join(attn_w, x_all, out_rows, g_own)
    held.step(1)
    out_w = lax.all_gather(out_rows, "dp", axis=0, tiled=True)
    g_line = jnp.concatenate(gather_ring(g_own), axis=0)
    qkv_w = attn_w[:, : 3 * cols]
    router_full = attn_w[:, 3 * cols : 3 * cols + experts]
    gains = attn_w[:, 3 * cols + experts : 3 * cols + experts + 4].astype(F32).T

    dealt = lax.dynamic_slice_in_dim(permutation, dp * zs * SEQ_DEV, zs * SEQ_DEV)
    lens = jnp.take(lengths, dealt).reshape(zs, SEQ_DEV)
    ends = jnp.cumsum(lens, axis=1)
    places = jnp.arange(rows, dtype=jnp.int32)
    segment = jnp.sum((places[None, :, None] >= ends[:, None, :]).astype(jnp.int32), axis=2)
    starts = ends - lens
    offset = jnp.sum(
        jnp.where(
            segment[:, :, None] == jnp.arange(SEQ_DEV, dtype=jnp.int32), starts[:, None, :], 0
        ),
        axis=2,
    )
    half = HEAD_DIM // 2
    inverse = ROPE_BASE ** (-2.0 * jnp.arange(half, dtype=F32) / HEAD_DIM)
    turned = (places[None] - offset).astype(F32)[..., None] * inverse
    cos, sin = jnp.cos(turned)[:, :, None, :], jnp.sin(turned)[:, :, None, :]
    same = (segment[:, :, None] == segment[:, None, :])[:, None]

    xf = x_all.astype(F32)
    r_attn = inv_rms(xf)
    a_all = (xf * r_attn * gains[0]).astype(BF16)
    qkv = nn(a_all, qkv_w)
    q, k, v = qkv[:, :cols], qkv[:, cols : 2 * cols], qkv[:, 2 * cols :]
    squares = lax.psum(
        jnp.stack([jnp.sum(q * q, axis=1), jnp.sum(k * k, axis=1)]), "expert"
    )
    r_q = lax.rsqrt(squares[0] / width + EPSILON)[:, None]
    r_k = lax.rsqrt(squares[1] / width + EPSILON)[:, None]
    gain_q = lax.dynamic_slice_in_dim(gains[1], z * cols, cols)
    gain_k = lax.dynamic_slice_in_dim(gains[2], z * cols, cols)
    split = (zs, rows, heads, HEAD_DIM)
    qr = rotate((q * r_q * gain_q).reshape(split), cos, sin).astype(BF16)
    kr = rotate((k * r_k * gain_k).reshape(split), cos, sin).astype(BF16)
    vb = v.astype(BF16).reshape(split)
    s = jnp.einsum("bthd,bshd->bhts", qr, kr, preferred_element_type=F32) * scale
    s = jnp.where(same, s, -1e30)
    es = jnp.exp(s - jnp.max(s, axis=3, keepdims=True))
    p = es / jnp.sum(es, axis=3, keepdims=True)
    pb = p.astype(BF16)
    o = (
        jnp.einsum("bhts,bshd->bthd", pb, vb, preferred_element_type=F32)
        .reshape(zs * rows, cols)
        .astype(BF16)
    )
    top = local // 2
    added = nn(o, out_w, BF16)
    added, g_line = held.join(added, g_line)
    held.step(2)
    g_far = flip(g_line, top)
    added = lax.psum_scatter(added, "expert", scatter_dimension=0, tiled=True)
    (added,) = held.join(added)
    held.step(3)
    hid = tokens.astype(F32) + added.astype(F32)
    r_ffn = inv_rms(hid)
    m = (hid * r_ffn * gains[3]).astype(BF16)

    m_near, m_far = [m], [flip(m, top)]
    for _ in range(zs - 1):
        m_near.append(hop(m_near[-1]))
        m_far.append(flip(m_near[-1], top))
    weights = held.whole()
    mine_e = (jnp.arange(experts) == expert).astype(F32)
    me_at = jnp.reshape(dp, (1,)).astype(jnp.int32)
    expert_at = jnp.stack([expert, dp]).astype(jnp.int32)
    router_t = router_full.T

    def chunk_front(g_part):
        parts = [x for xs in fan([g_part], top) for x in xs]
        masks = jnp.concatenate([x[:, width : width + experts] for x in parts], axis=0)
        masks = masks.astype(F32).reshape(len(parts) * zs, rows, experts)
        on = jnp.sum(masks * mine_e, axis=2)
        pos = jnp.where(on > 0, jnp.cumsum(on, axis=1) - 1.0, -1.0).astype(jnp.int32)
        gs, gw = front(parts, pos, weights, ff, me_at)
        return pos, masks.transpose(0, 2, 1), gs, gw

    def chunk_expert(blocks, pieces, fronted):
        pos, named, gs, gw = fronted
        parts = [blocks] + fan(pieces, top)[1:]
        flat = [x for xs in parts for x in xs]
        backs, outs = run_expert(flat, pos, named, router_t, weights, gw, expert_at, ff)
        back = []
        for xs in parts:
            back.append(backs[: len(xs)])
            backs = backs[len(xs) :]
        return back, (outs[0], gs, outs[1], outs[2], outs[3])

    near = chunk_front(g_line)
    far = chunk_front(g_far)
    near_back, near_outs = chunk_expert(m_near, [jnp.concatenate(m_near, axis=0)], near)
    mid = zs // 2
    m_far = tie(*m_far, near_outs[4])[:zs]
    far_pieces = [jnp.concatenate(m_far[:mid], axis=0), jnp.concatenate(m_far[mid:], axis=0)]
    far_back, far_outs = chunk_expert(list(m_far), far_pieces, far)
    chunks = [near_outs, far_outs]
    e_rows = w_gate_up.shape[0]

    far_sum = fold(far_back)
    near_sum = fold(near_back)
    acc = None
    for i in reversed(range(zs)):
        here = near_sum[i].astype(F32) + flip(far_sum[i], top).astype(F32)
        acc = here if acc is None else here + hop(acc, back=True).astype(F32)
        acc = acc.astype(BF16)
    dm = acc
    send_high = grads(chunks, 3 * dps // 4, dps // 4, e_rows)
    got_high = flip(send_high, dps // 2)
    send_low = grads(chunks, dps // 2, dps // 4, e_rows)
    y_far = fold([[x] for x in result(far_outs[4], far[0], weights, top, me_at)])[0]
    y_near = fold([[x] for x in result(near_outs[4], near[0], weights, top, me_at)])[0]
    kept = grads(chunks, 0, dps // 2, e_rows)
    dm, got_high, send_low, y_far, y_near, kept = tie(
        dm, got_high, send_low, y_far, y_near, kept
    )
    dm = dm.astype(F32)
    y_far = flip(y_far, top)
    held_g = {}
    for i in range(dps // 4):
        held_g[dps // 4 + i] = add(kept[dps // 4 + i], got_high[i])
    got_low = flip(send_low, dps // 2)

    own_mask = mask.astype(F32)
    own_logits = jnp.where(own_mask > 0, nn(m, router_full), -1e30)
    own_e = jnp.where(
        own_mask > 0, jnp.exp(own_logits - jnp.max(own_logits, axis=1, keepdims=True)), 0.0
    )
    gate_own = own_e / jnp.sum(own_e, axis=1, keepdims=True)
    dgates = dm[:, width : width + experts] + dm[:, width + experts : width + 2 * experts]
    dz = (
        gate_own * (dgates - jnp.sum(gate_own * dgates, axis=1, keepdims=True))
    ).astype(BF16)
    dmt = nt(dz, router_full) + dm[:, :width]
    router_part = tn(m, dz)
    grad_out = cotangent.astype(F32)
    dh = grad_out + rms_back(hid, r_ffn, gains[3], dmt)
    gain_ffn = jnp.sum(dmt * hid * r_ffn, axis=0)

    dhb = lax.all_gather(dh.astype(BF16), "expert", axis=0, tiled=True)
    dhb, y_far = tie(dhb, y_far)
    y_own = add(y_near, y_far)
    y = lax.psum_scatter(
        by_line([y_own[i * rows : (i + 1) * rows] for i in range(zs)]),
        "expert",
        scatter_dimension=0,
        tiled=True,
    )
    do = nt(dhb, out_w, BF16).reshape(split)
    out_blocks = tn(o, dhb, BF16).reshape(dps, own_rows, width)
    grad_out_w = scatter_dp(
        jnp.concatenate([pick(out_blocks, dp ^ r, 0) for r in range(dps)], axis=0), own_rows
    )
    grad_w_out = lax.ppermute(
        grad_out_w, ("dp", "expert"), [(b, a) for a, b in moved]
    ).astype(F32)
    dp_ = jnp.einsum("bthd,bshd->bhts", do, vb, preferred_element_type=F32)
    dv = jnp.einsum("bhts,bthd->bshd", pb, do, preferred_element_type=F32)
    ds = (p * (dp_ - jnp.sum(p * dp_, axis=3, keepdims=True))).astype(BF16)
    dqr = jnp.einsum("bhts,bshd->bthd", ds, kr, preferred_element_type=F32) * scale
    dkr = jnp.einsum("bhts,bthd->bshd", ds, qr, preferred_element_type=F32) * scale
    dqn = rotate(dqr, cos, -sin).reshape(zs * rows, cols)
    dkn = rotate(dkr, cos, -sin).reshape(zs * rows, cols)
    means = lax.psum(
        jnp.stack(
            [jnp.sum(q * (gain_q * dqn), axis=1), jnp.sum(k * (gain_k * dkn), axis=1)]
        ),
        "expert",
    )
    dq = r_q * gain_q * dqn - q * (r_q * r_q * r_q) * (means[0] / width)[:, None]
    dk = r_k * gain_k * dkn - k * (r_k * r_k * r_k) * (means[1] / width)[:, None]
    dqkv = jnp.concatenate([dq, dk, dv.reshape(zs * rows, cols)], axis=1).astype(BF16)
    da_part = nt(dqkv, qkv_w)
    da = lax.psum_scatter(
        da_part.astype(BF16), "expert", scatter_dimension=0, tiled=True
    ).astype(F32)
    gain_attn = jnp.sum(da_part * (xf * r_attn), axis=0)
    at = z * cols
    zero = jnp.zeros((width,), F32)
    gain_query = lax.dynamic_update_slice_in_dim(zero, jnp.sum(dqn * q * r_q, axis=0), at, 0)
    gain_keys = lax.dynamic_update_slice_in_dim(zero, jnp.sum(dkn * k * r_k, axis=0), at, 0)
    gain_part = jnp.stack([gain_attn, gain_query, gain_keys, gain_ffn], axis=1)
    extra_part = jnp.concatenate(
        [router_part, gain_part, jnp.zeros((width, EXTRA - experts - 4), F32)], axis=1
    ).astype(BF16)
    dqkv, got_low = tie(dqkv, got_low)
    for i in range(dps // 4):
        held_g[i] = add(kept[i], got_low[i])
    tail = Tail(held_g, local, dps)
    summed = scatter_wide(
        attn_grads(a_all, dqkv, [extra_part], me_at, 1, 2),
        attn_grads(a_all, dqkv, [extra_part], me_at, 0, 2),
        zs * own_rows,
    )
    tail.step(0)
    tail.step(1)
    output = hid + y.astype(F32)
    grad_gu, grad_dn = tail.done(ff)
    back = lax.all_to_all(
        summed.reshape(zs, own_rows, 3 * cols + EXTRA),
        "expert",
        split_axis=0,
        concat_axis=0,
        tiled=True,
    ).astype(F32)
    grad_w_qkv = jnp.concatenate(
        [back[e, :, i * cols : (i + 1) * cols] for i in range(3) for e in range(zs)], axis=1
    )
    extra_sum = jnp.sum(back[:, :, 3 * cols :], axis=0)
    grad_router = extra_sum[:, :experts]
    grad_gains = extra_sum[:, experts : experts + 4]

    x_own = tokens.astype(F32)
    grad_tokens = dh + rms_back(x_own, inv_rms(x_own), gains[0], da)
    return (
        output,
        grad_tokens,
        grad_gains,
        grad_w_qkv,
        grad_w_out,
        grad_router,
        grad_gu,
        grad_dn,
    )


def solution(mesh):
    both = P(("dp", "expert"), None)
    experts = P("dp", "expert", None)
    return jax.shard_map(
        on_device,
        mesh=mesh,
        in_specs=(both, P(), P(), both, both, both, both, both, experts, experts, both),
        out_specs=(both, both, both, both, both, both, experts, experts),
        check_vma=False,
    )
```

```python
import functools

import jax
import jax.numpy as jnp
from jax import lax
from jax.experimental import pallas as pl
from jax.experimental.pallas import tpu as pltpu
from jax.sharding import PartitionSpec as P

HEADS = 16
HEAD_DIM = 128
SEQ_DEV = 2
EPSILON = 1e-06
ROPE_BASE = 50000.0
CAP = 80
EXTRA = 128
VMEM = 56 * 2**20
COST = pl.CostEstimate(flops=10**6, bytes_accessed=10**5, transcendentals=0)

F32 = jnp.float32
BF16 = jnp.bfloat16


def dot(a, b, dims, out=F32):
    return lax.dot_general(a, b, (dims, ((), ())), preferred_element_type=F32).astype(out)


def nn(a, b, out=F32):
    return dot(a, b, ((1,), (0,)), out)


def nt(a, b, out=F32):
    return dot(a, b, ((1,), (1,)), out)


def tn(a, b, out=F32):
    return dot(a, b, ((0,), (0,)), out)


def flip(v, bit):
    return lax.ppermute(v, "dp", [(i, i ^ bit) for i in range(lax.axis_size("dp"))])


def ring(n):
    return [*range(0, n, 2), *reversed(range(1, n, 2))]


def hop(v, step=1):
    order = ring(lax.axis_size("expert"))
    n = len(order)
    pairs = [(order[i], order[(i + step) % n]) for i in range(n)]
    return lax.ppermute(v, "expert", pairs)


def gather_ring(v):
    return [v] + [hop(v, i) for i in range(1, lax.axis_size("expert"))]


def places_in_ring():
    n = lax.axis_size("expert")
    at = [ring(n).index(i) for i in range(n)]
    at = jnp.asarray(at, jnp.int32)
    return lax.rem(at[lax.axis_index("expert")] - at + n, n)


def by_line(blocks):
    where = places_in_ring()
    stacked = jnp.stack(blocks)
    return jnp.concatenate([pick(stacked, where[i], 0) for i in range(len(blocks))], axis=0)


def bits_of(low, high):
    out = []
    while low < high:
        out.append(low)
        low *= 2
    return out


def pick(v, index, axis):
    return lax.dynamic_index_in_dim(v, index, axis, keepdims=False)


def tie(*values):
    return lax.optimization_barrier(values)


class Flow:
    def __init__(self):
        self.of = {}

    def fence(self, *keys):
        out = tie(*[self.of[key] for key in keys])
        for key, v in zip(keys, out, strict=True):
            self.of[key] = v

    def __getitem__(self, key):
        return self.of[key]

    def __setitem__(self, key, value):
        self.of[key] = value

    def having(self, kind):
        return [key for key in self.of if isinstance(key, tuple) and key[0] == kind]


def fan(pieces, low):
    out = [list(pieces)]
    for bit in bits_of(1, low):
        out = out + [[flip(x, bit) for x in xs] for xs in out]
    return out


def add(a, b):
    return (a.astype(F32) + b.astype(F32)).astype(BF16)


def match(pieces, like):
    if len(pieces) == len(like):
        return pieces
    step = like[0].shape[0]
    return [x[i : i + step] for x in pieces for i in range(0, x.shape[0], step)]


def fold(parts):
    parts = list(parts)
    while len(parts) > 1:
        half = len(parts) // 2
        for i in range(half):
            got = match([flip(x, half) for x in reversed(parts[half + i])][::-1], parts[i])
            parts[i] = [add(a, b) for a, b in zip(parts[i], got, strict=True)]
        parts = parts[:half]
    return parts[0]


def scatter_dp(part, rows):
    n = lax.axis_size("dp")
    held = [part[r * rows : (r + 1) * rows] for r in range(n)]
    for bit in bits_of(1, n):
        odd = jnp.concatenate(held[1::2], axis=0) if len(held) > 2 else held[1]
        got = flip(odd, bit)
        held = [add(v, got[i * rows : (i + 1) * rows]) for i, v in enumerate(held[::2])]
    return held[0]


def blocks_of(parts, tok):
    return [(i, at) for i, p in enumerate(parts) for at in range(0, p.shape[0], tok)]


def onehot_back(pos_t, b):
    slot = lax.broadcasted_iota(jnp.int32, (pos_t.shape[0], CAP), 1)
    return (slot == pos_t[:, b : b + 1]).astype(BF16)


def onehot(pos_ref, b):
    slot = lax.broadcasted_iota(jnp.int32, (CAP, pos_ref.shape[1]), 0)
    return slot == pos_ref[b : b + 1, :]


def mm(a, b, dims):
    return lax.dot_general(a, b, (dims, ((), ())), preferred_element_type=F32)


def front_kernel(count, me, *refs):
    parts, (pos, wd, rows_out, gw) = refs[:count], refs[count:]
    tok = pos.shape[1]
    width = rows_out.shape[1]

    @pl.when(pl.program_id(0) == 0)
    def _():
        for b, (i, at) in enumerate(blocks_of(parts, tok)):
            part = parts[i][at : at + tok, :width]
            hot = onehot(pos, b).astype(BF16)
            found = mm(hot, part, ((1,), (0,))).astype(BF16)
            to_distance(rows_out, slice(b * CAP, (b + 1) * CAP), found, me[0])

    gw[...] = mm(rows_out[...], wd[...], ((1,), (0,)))


def front(parts, pos, weights, ff, me):
    count, width = len(parts), weights.shape[0]
    slots = pos.shape[0] * CAP
    tile = min(256, ff)
    first = (weights.shape[1] - ff) // tile
    whole = lambda x: pl.BlockSpec(x.shape, lambda n, me: (0, 0))
    return pl.pallas_call(
        functools.partial(front_kernel, count),
        grid_spec=pltpu.PrefetchScalarGridSpec(
            num_scalar_prefetch=1,
            grid=(ff // tile,),
            in_specs=[whole(x) for x in parts]
            + [whole(pos), pl.BlockSpec((width, tile), lambda n, me: (0, first + n))],
            out_specs=[
                pl.BlockSpec((slots, width), lambda n, me: (0, 0)),
                pl.BlockSpec((slots, tile), lambda n, me: (0, n)),
            ],
        ),
        out_shape=[
            jax.ShapeDtypeStruct((slots, width), BF16),
            jax.ShapeDtypeStruct((slots, ff), F32),
        ],
        compiler_params=pltpu.CompilerParams(vmem_limit_bytes=VMEM),
        cost_estimate=COST,
        name="front",
    )(me, *parts, pos, weights)


def to_distance(ref, rows, value, me):
    n = lax.axis_size("dp")
    wide = value.shape[1] // n
    for c in range(n):
        at = pl.multiple_of((me ^ c) * wide, wide)
        ref[rows, pl.ds(at, wide)] = value[:, c * wide : (c + 1) * wide]


def expert_kernel(count, expert, *refs):
    parts = refs[:count]
    pos, pos_t, named, router, wg, wu, gw = refs[count : count + 7]
    backs = refs[count + 7 : 2 * count + 7]
    rows_out, dg_out, du_out, gact_out, acc, gate, dgate = refs[2 * count + 7 :]
    n = pl.program_id(0)
    tok = pos.shape[1]
    width = rows_out.shape[1]
    experts = router.shape[0]

    @pl.when(n == 0)
    def _():
        for b, (i, first) in enumerate(blocks_of(parts, tok)):
            at = slice(b * CAP, (b + 1) * CAP)
            part = parts[i][first : first + tok, :]
            hot = onehot(pos, b)
            found = mm(hot.astype(BF16), part, ((1,), (0,))).astype(BF16)
            to_distance(rows_out, at, found, expert[1])
            chosen = named[b] > 0
            logits = jnp.where(chosen, mm(router[...], part, ((1,), (1,))), -1e30)
            e = jnp.where(chosen, jnp.exp(logits - jnp.max(logits, axis=0, keepdims=True)), 0.0)
            gates = e / jnp.sum(e, axis=0, keepdims=True)
            mine = lax.broadcasted_iota(jnp.int32, gates.shape, 0) == expert[0]
            row = jnp.sum(jnp.where(mine, gates, 0.0), axis=0, keepdims=True)
            gate[at, :] = jnp.sum(jnp.where(hot, row, 0.0), axis=1, keepdims=True)
            dgate[at, :] = jnp.zeros((CAP, 1), F32)

    rows = rows_out[...]
    g = mm(rows, wg[...], ((1,), (0,)))
    u = mm(rows, wu[...], ((1,), (0,)))
    sg = 1.0 / (1.0 + jnp.exp(-g))
    silu = g * sg
    act = (silu * u).astype(BF16).astype(F32)
    gw_v = gw[...]
    dgate[...] += jnp.sum(act * gw_v, axis=1, keepdims=True)
    gate_v = gate[...]
    gact_out[...] = (gate_v * act).astype(BF16)
    dact = gate_v * gw_v
    dg = (dact * u * (sg * (1.0 + g * (1.0 - sg)))).astype(BF16)
    du = (dact * silu).astype(BF16)
    dg_out[...] = dg
    du_out[...] = du
    back = mm(dg, wg[...], ((1,), (1,))) + mm(du, wu[...], ((1,), (1,)))

    @pl.when(n == 0)
    def _():
        acc[...] = back

    @pl.when(n > 0)
    def _():
        acc[...] += back

    @pl.when(n == pl.num_programs(0) - 1)
    def _():
        lane = lax.broadcasted_iota(jnp.int32, (CAP, EXTRA), 1)
        for b, (i, first) in enumerate(blocks_of(parts, tok)):
            at = slice(b * CAP, (b + 1) * CAP)
            to = slice(first, first + tok)
            hot = onehot_back(pos_t, b)
            out = backs[i]
            found = mm(hot, acc[at, :].astype(BF16), ((1,), (0,))).astype(BF16)
            to_distance(out, to, found, expert[1])
            d = dgate[at, :]
            hi = d.astype(BF16).astype(F32)
            beside = jnp.where(
                lane == expert[0], hi, jnp.where(lane == experts + expert[0], d - hi, 0.0)
            ).astype(BF16)
            out[to, width:] = mm(hot, beside, ((1,), (0,))).astype(BF16)


def run_expert(parts, pos, pos_t, named, router, weights, gw, expert, ff):
    count, width = len(parts), weights.shape[0]
    slots = pos.shape[0] * CAP
    tile = min(256, ff)
    steps = ff // tile
    whole = lambda x: pl.BlockSpec(x.shape, lambda n, e: (0,) * x.ndim)
    column = pl.BlockSpec((slots, tile), lambda n, e: (0, n))
    backs = [jax.ShapeDtypeStruct((x.shape[0], width + EXTRA), BF16) for x in parts]
    thin = jax.ShapeDtypeStruct((slots, ff), BF16)
    outs = pl.pallas_call(
        functools.partial(expert_kernel, count),
        grid_spec=pltpu.PrefetchScalarGridSpec(
            num_scalar_prefetch=1,
            grid=(steps,),
            in_specs=[whole(x) for x in parts]
            + [
                whole(pos),
                whole(pos_t),
                whole(named),
                whole(router),
                pl.BlockSpec((width, tile), lambda n, e: (0, n)),
                pl.BlockSpec((width, tile), lambda n, e: (0, steps + n)),
                column,
            ],
            out_specs=[whole(x) for x in backs]
            + [pl.BlockSpec((slots, width), lambda n, e: (0, 0)), column, column, column],
            scratch_shapes=[
                pltpu.VMEM((slots, width), F32),
                pltpu.VMEM((slots, 1), F32),
                pltpu.VMEM((slots, 1), F32),
            ],
        ),
        out_shape=backs
        + [jax.ShapeDtypeStruct((slots, width), BF16), thin, thin, thin],
        compiler_params=pltpu.CompilerParams(vmem_limit_bytes=VMEM),
        cost_estimate=COST,
        name="expert",
    )(expert, *parts, pos, pos_t, named, router, weights, weights, gw)
    return outs[:count], outs[count:]


def result_kernel(count, me, gact, wd, pos_t, *outs):
    tok = pos_t.shape[0]
    y = mm(gact[...], wd[...], ((1,), (1,))).astype(BF16)
    for b, (i, at) in enumerate(blocks_of(outs, tok)):
        outs[i][at : at + tok, :] = mm(
            onehot_back(pos_t, b), y[b * CAP : (b + 1) * CAP, :], ((1,), (0,))
        ).astype(BF16)


def result(gact, pos_t, weights, count, me):
    slots, ff = gact.shape
    width = weights.shape[0]
    tile = width // lax.axis_size("dp")
    last = (weights.shape[1] - ff) // ff
    out = jax.ShapeDtypeStruct((pos_t.shape[1] // count * pos_t.shape[0], width), BF16)
    return pl.pallas_call(
        functools.partial(result_kernel, count),
        grid_spec=pltpu.PrefetchScalarGridSpec(
            num_scalar_prefetch=1,
            grid=(width // tile,),
            in_specs=[
                pl.BlockSpec((slots, ff), lambda n, me: (0, 0)),
                pl.BlockSpec((tile, ff), lambda n, me: (n, last)),
                pl.BlockSpec(pos_t.shape, lambda n, me: (0, 0)),
            ],
            out_specs=[pl.BlockSpec((out.shape[0], tile), lambda n, me: (0, me[0] ^ n))] * count,
        ),
        out_shape=[out] * count,
        compiler_params=pltpu.CompilerParams(vmem_limit_bytes=VMEM),
        cost_estimate=COST,
        name="result",
    )(me, gact, weights, pos_t)


def grads_kernel(count, *refs):
    out = refs[-1]
    ff = refs[2].shape[1]
    gate = up = down = 0.0
    for c in range(count):
        rows, gs, dg, du, gact = refs[5 * c : 5 * c + 5]
        gate = gate + mm(rows[...], dg[...], ((0,), (0,)))
        up = up + mm(rows[...], du[...], ((0,), (0,)))
        down = down + mm(gs[...], gact[...], ((0,), (0,)))
    out[0, :, :ff] = gate.astype(BF16)
    out[0, :, ff : 2 * ff] = up.astype(BF16)
    out[0, :, 2 * ff :] = down.astype(BF16)


def grads(chunks, first, blocks, rows):
    ff = chunks[0][2].shape[1]
    specs, ins = [], []
    for chunk in chunks:
        slots = chunk[0].shape[0]
        tall = pl.BlockSpec((slots, rows), lambda i: (0, first + i))
        flat = pl.BlockSpec((slots, ff), lambda i: (0, 0))
        specs += [tall, tall, flat, flat, flat]
        ins += list(chunk)
    slots = sum(chunk[0].shape[0] for chunk in chunks)
    return pl.pallas_call(
        functools.partial(grads_kernel, len(chunks)),
        grid=(blocks,),
        in_specs=specs,
        out_specs=pl.BlockSpec((1, rows, 3 * ff), lambda i: (i, 0, 0)),
        out_shape=jax.ShapeDtypeStruct((blocks, rows, 3 * ff), BF16),
        compiler_params=pltpu.CompilerParams(vmem_limit_bytes=VMEM),
        cost_estimate=COST,
        name="grads",
    )(*ins)


def attn_grads_kernel(me, a, d, *rest):
    k = d.shape[1]
    out = rest[-1]
    out[:, :k] = mm(a[...], d[...], ((0,), (0,))).astype(BF16)
    if len(rest) > 1:
        out[:, k:] = rest[0][...]


def attn_grads(a, d, extra, me, first, stride):
    rows, width = a.shape
    n = lax.axis_size("dp")
    tile = width // n
    count = n // stride
    at = lambda i, me: me[0] ^ (first + stride * i)
    k = d.shape[1] + sum(e.shape[1] for e in extra)
    return pl.pallas_call(
        attn_grads_kernel,
        grid_spec=pltpu.PrefetchScalarGridSpec(
            num_scalar_prefetch=1,
            grid=(count,),
            in_specs=[
                pl.BlockSpec((rows, tile), lambda i, me: (0, at(i, me))),
                pl.BlockSpec(d.shape, lambda i, me: (0, 0)),
            ]
            + [pl.BlockSpec((tile, e.shape[1]), lambda i, me: (at(i, me), 0)) for e in extra],
            out_specs=pl.BlockSpec((tile, k), lambda i, me: (i, 0)),
        ),
        out_shape=jax.ShapeDtypeStruct((count * tile, k), BF16),
        compiler_params=pltpu.CompilerParams(vmem_limit_bytes=VMEM),
        cost_estimate=COST,
        name="attn_grads",
    )(me, a, d, *extra)


def halves(held, rows):
    n = lax.axis_size("dp")
    wide = held.shape[1] // 256 * 128
    out = []
    for left, right, order in (
        (0, wide, bits_of(2, n)),
        (wide, held.shape[1], bits_of(2, n)[::-1]),
    ):
        side = {2 * i: held[i * rows : (i + 1) * rows, left:right] for i in range(n // 2)}
        out.append((side, order))
    return out


def stage(at, sides, step):
    for s, (side, order) in enumerate(sides):
        keys = sorted(r for r in side if r & order[step])
        v = [side[r] for r in keys]
        at["side", s] = flip(jnp.concatenate(v, axis=0) if len(v) > 1 else v[0], order[step])


def unstage(at, sides, step):
    out = []
    for s, (side, order) in enumerate(sides):
        bit = order[step]
        keys = sorted(r for r in side if r & bit)
        rows = side[0].shape[0]
        got = at["side", s]
        kept = {r: v for r, v in side.items() if not r & bit}
        for i, r in enumerate(keys):
            kept[r ^ bit] = add(kept[r ^ bit], got[i * rows : (i + 1) * rows])
        out.append((kept, order))
    return out


def spread(first, n):
    local = len(first)
    have = {(0, e): v for e, v in first.items()}
    for bit in bits_of(1, local):
        for key in sorted(key for key in have if key[1] & bit):
            have[(key[0] ^ bit, key[1] ^ bit)] = flip(have.pop(key), bit)
    for bit in bits_of(local, n):
        for key in sorted(have):
            have[(key[0] ^ bit, 0)] = flip(have[key], bit)
    return jnp.concatenate([have[key] for key in sorted(have)], axis=0)


def gather_back(held, local, n):
    held = dict(held)
    for bit in reversed(bits_of(local, n // 2)):
        for r in sorted(r for r in held if r & bit):
            held[r ^ bit] = add(held[r ^ bit], flip(held.pop(r), bit))
    have = {(r, 0): v for r, v in held.items()}
    for bit in reversed(bits_of(1, local)):
        for key in sorted(key for key in have if key[0] & bit):
            have[(key[0] ^ bit, key[1] ^ bit)] = flip(have.pop(key), bit)
    return {e: v for (_, e), v in have.items()}


def per_row(row):
    return jnp.broadcast_to(row, (row.shape[1], row.shape[1])).T


def turn(v, cos, sin):
    return v * cos + pltpu.roll(v, v.shape[1] // 2, 1) * sin


def softmax_rows(qr, kr, same, scale):
    s = jnp.where(same, mm(qr, kr, ((1,), (1,))) * scale, -1e30)
    e = jnp.exp(s - jnp.max(s, axis=1, keepdims=True))
    return e / jnp.sum(e, axis=1, keepdims=True)


def attend_kernel(scale, qkv, r, gains, cos, sin, seg, qr_out, kr_out, vb_out, o_out):
    cols = o_out.shape[1]
    rq, rk = per_row(r[0, 0:1, :]), per_row(r[0, 1:2, :])
    seg_row = seg[0]
    same = per_row(seg_row) == seg_row
    for h in range(cols // HEAD_DIM):
        at = slice(h * HEAD_DIM, (h + 1) * HEAD_DIM)
        k_at = slice(cols + h * HEAD_DIM, cols + (h + 1) * HEAD_DIM)
        v_at = slice(2 * cols + h * HEAD_DIM, 2 * cols + (h + 1) * HEAD_DIM)
        qr = turn(qkv[:, at] * rq * gains[0:1, at], cos[...], sin[...]).astype(BF16)
        kr = turn(qkv[:, k_at] * rk * gains[1:2, at], cos[...], sin[...]).astype(BF16)
        vb = qkv[:, v_at].astype(BF16)
        p = softmax_rows(qr, kr, same, scale)
        qr_out[:, at] = qr
        kr_out[:, at] = kr
        vb_out[:, at] = vb
        o_out[:, at] = mm(p.astype(BF16), vb, ((1,), (0,))).astype(BF16)


def attend(qkv, r, gains, cos, sin, seg):
    total, cols = qkv.shape[0], qkv.shape[1] // 3
    zs, tok = seg.shape[0], seg.shape[2]
    tall = lambda w: pl.BlockSpec((tok, w), lambda b: (b, 0))
    fixed = lambda x: pl.BlockSpec(x.shape, lambda b: (0, 0))
    thin = jax.ShapeDtypeStruct((total, cols), BF16)
    return pl.pallas_call(
        functools.partial(attend_kernel, HEAD_DIM ** (-0.5)),
        grid=(zs,),
        in_specs=[
            tall(qkv.shape[1]),
            pl.BlockSpec((1, 2, tok), lambda b: (b, 0, 0)),
            fixed(gains),
            tall(HEAD_DIM),
            tall(HEAD_DIM),
            pl.BlockSpec((1, 1, tok), lambda b: (b, 0, 0)),
        ],
        out_specs=[tall(cols)] * 4,
        out_shape=[thin] * 4,
        compiler_params=pltpu.CompilerParams(vmem_limit_bytes=VMEM),
        cost_estimate=COST,
        name="attend",
    )(qkv, r, gains, cos, sin, seg)


def attend_back_kernel(
    scale, dhb, wo, q, k, qr, kr, vb, gains, cos, sin, seg, dq_out, dk_out, dv_out, sums
):
    cols = wo.shape[0]
    seg_row = seg[0]
    same = per_row(seg_row) == seg_row
    do_all = mm(dhb[...], wo[...], ((1,), (1,))).astype(BF16)
    sum_q = sum_k = 0.0
    for h in range(cols // HEAD_DIM):
        at = slice(h * HEAD_DIM, (h + 1) * HEAD_DIM)
        do = do_all[:, at]
        p = softmax_rows(qr[:, at], kr[:, at], same, scale)
        dp = mm(do, vb[:, at], ((1,), (1,)))
        ds = (p * (dp - jnp.sum(p * dp, axis=1, keepdims=True))).astype(BF16)
        dv_out[:, at] = mm(p.astype(BF16), do, ((0,), (0,))).astype(BF16)
        dq = turn(mm(ds, kr[:, at], ((1,), (0,))) * scale, cos[...], -sin[...])
        dk = turn(mm(ds, qr[:, at], ((0,), (0,))) * scale, cos[...], -sin[...])
        dq_out[:, at] = dq
        dk_out[:, at] = dk
        sum_q = sum_q + jnp.sum(q[:, at] * gains[0:1, at] * dq, axis=1, keepdims=True)
        sum_k = sum_k + jnp.sum(k[:, at] * gains[1:2, at] * dk, axis=1, keepdims=True)
    tok = dhb.shape[0]
    sums[0, 0:1, :] = jnp.broadcast_to(sum_q, (tok, tok)).T[0:1, :]
    sums[0, 1:2, :] = jnp.broadcast_to(sum_k, (tok, tok)).T[0:1, :]


def attend_back(dhb, wo, qkv, qr, kr, vb, gains, cos, sin, seg):
    total, cols = qkv.shape[0], wo.shape[0]
    zs, tok = seg.shape[0], seg.shape[2]
    tall = lambda w, at=0: pl.BlockSpec((tok, w), lambda b: (b, at))
    fixed = lambda x: pl.BlockSpec(x.shape, lambda b: (0, 0))
    wide = jax.ShapeDtypeStruct((total, cols), F32)
    return pl.pallas_call(
        functools.partial(attend_back_kernel, HEAD_DIM ** (-0.5)),
        grid=(zs,),
        in_specs=[
            tall(dhb.shape[1]),
            fixed(wo),
            tall(cols, 0),
            tall(cols, 1),
            tall(cols),
            tall(cols),
            tall(cols),
            fixed(gains),
            tall(HEAD_DIM),
            tall(HEAD_DIM),
            pl.BlockSpec((1, 1, tok), lambda b: (b, 0, 0)),
        ],
        out_specs=[tall(cols)] * 3 + [pl.BlockSpec((1, 2, tok), lambda b: (b, 0, 0))],
        out_shape=[
            wide,
            wide,
            jax.ShapeDtypeStruct((total, cols), BF16),
            jax.ShapeDtypeStruct((zs, 2, tok), F32),
        ],
        compiler_params=pltpu.CompilerParams(vmem_limit_bytes=VMEM),
        cost_estimate=COST,
        name="attend_back",
    )(dhb, wo, qkv, qkv, qr, kr, vb, gains, cos, sin, seg)


def join_back_kernel(q, k, dqn, dkn, dv, r, means, gains, out, gain_out):
    cols = dv.shape[1]
    for at, v, d in ((0, q, dqn), (1, k, dkn)):
        rr = per_row(r[0, at : at + 1, :])
        mean = per_row(means[0, at : at + 1, :])
        part = []
        for h in range(cols // HEAD_DIM):
            to = slice(h * HEAD_DIM, (h + 1) * HEAD_DIM)
            vr = v[:, to] * rr
            out[:, at * cols + h * HEAD_DIM : at * cols + (h + 1) * HEAD_DIM] = (
                rr * (gains[at : at + 1, to] * d[:, to]) - vr * (rr * rr) * mean
            ).astype(BF16)
            part.append(jnp.sum(d[:, to] * vr, axis=0, keepdims=True))
        row = jnp.concatenate(part, axis=1)

        @pl.when(pl.program_id(0) == 0)
        def _():
            gain_out[at : at + 1, :] = row

        @pl.when(pl.program_id(0) > 0)
        def _():
            gain_out[at : at + 1, :] += row

    out[:, 2 * cols :] = dv[...]


def join_back(qkv, dqn, dkn, dv, r, means, gains):
    total, cols = dv.shape
    zs, tok = r.shape[0], r.shape[2]
    tall = lambda w, at=0: pl.BlockSpec((tok, w), lambda b: (b, at))
    row = pl.BlockSpec((1, 2, tok), lambda b: (b, 0, 0))
    return pl.pallas_call(
        join_back_kernel,
        grid=(zs,),
        in_specs=[tall(cols, 0), tall(cols, 1), tall(cols), tall(cols), tall(cols), row, row]
        + [pl.BlockSpec(gains.shape, lambda b: (0, 0))],
        out_specs=[tall(3 * cols), pl.BlockSpec((2, cols), lambda b: (0, 0))],
        out_shape=[
            jax.ShapeDtypeStruct((total, 3 * cols), BF16),
            jax.ShapeDtypeStruct((2, cols), F32),
        ],
        compiler_params=pltpu.CompilerParams(vmem_limit_bytes=VMEM),
        cost_estimate=COST,
        name="join_back",
    )(qkv, qkv, dqn, dkn, dv, r, means, gains)


def first_back_kernel(d, w, x, r, da, gain):
    back = mm(d[...], w[...], ((1,), (1,)))
    da[...] = back.astype(BF16)
    row = jnp.sum(back * (x[...].astype(F32) * r[...]), axis=0, keepdims=True)

    @pl.when(pl.program_id(0) == 0)
    def _():
        gain[...] = row

    @pl.when(pl.program_id(0) > 0)
    def _():
        gain[...] += row


def first_back(d, w, x, r, tok):
    total, width = x.shape
    k = d.shape[1]
    return pl.pallas_call(
        first_back_kernel,
        grid=(total // tok,),
        in_specs=[
            pl.BlockSpec((tok, k), lambda b: (b, 0)),
            pl.BlockSpec((width, k), lambda b: (0, 0)),
            pl.BlockSpec((tok, width), lambda b: (b, 0)),
            pl.BlockSpec((tok, 1), lambda b: (b, 0)),
        ],
        out_specs=[
            pl.BlockSpec((tok, width), lambda b: (b, 0)),
            pl.BlockSpec((1, width), lambda b: (0, 0)),
        ],
        out_shape=[
            jax.ShapeDtypeStruct((total, width), BF16),
            jax.ShapeDtypeStruct((1, width), F32),
        ],
        compiler_params=pltpu.CompilerParams(vmem_limit_bytes=VMEM),
        cost_estimate=COST,
        name="first_back",
    )(d, w, x, r)


def inv_rms(v):
    return lax.rsqrt(jnp.mean(v * v, axis=-1, keepdims=True) + EPSILON)


def rms_back(v, r, gain, c):
    gc = gain * c
    return r * gc - v * (r * r * r) * jnp.mean(v * gc, axis=-1, keepdims=True)


def places_and_tables(at, dp, zs, rows):
    dealt = lax.dynamic_slice_in_dim(at["order"], dp * zs * SEQ_DEV, zs * SEQ_DEV)
    lens = jnp.take(at["lengths"], dealt).reshape(zs, SEQ_DEV)
    ends = jnp.cumsum(lens, axis=1)
    places = jnp.arange(rows, dtype=jnp.int32)
    segment = jnp.sum((places[None, :, None] >= ends[:, None, :]).astype(jnp.int32), axis=2)
    starts = ends - lens
    offset = jnp.sum(
        jnp.where(
            segment[:, :, None] == jnp.arange(SEQ_DEV, dtype=jnp.int32), starts[:, None, :], 0
        ),
        axis=2,
    )
    half = HEAD_DIM // 2
    inverse = ROPE_BASE ** (-2.0 * jnp.arange(half, dtype=F32) / HEAD_DIM)
    turned = (places[None] - offset).astype(F32)[..., None] * inverse
    at["cos"] = jnp.tile(jnp.cos(turned), (1, 1, 2)).reshape(zs * rows, HEAD_DIM)
    sin = jnp.sin(turned)
    at["sin"] = jnp.concatenate([-sin, sin], axis=2).reshape(zs * rows, HEAD_DIM)
    at["seg"] = segment.astype(F32)[:, None, :]


def on_device(
    tokens,
    lengths,
    permutation,
    routes,
    norm_gains,
    w_qkv,
    w_out,
    router,
    w_gate_up,
    w_down,
    cotangent,
):
    rows, width = tokens.shape
    zs = lax.axis_size("expert")
    dps = lax.axis_size("dp")
    z = lax.axis_index("expert")
    dp = lax.axis_index("dp")
    local = w_gate_up.shape[1]
    ff = w_down.shape[2]
    experts = router.shape[1]
    own_rows = w_qkv.shape[0]
    e_rows = w_gate_up.shape[0]
    cols = width // zs
    expert = z * local + lax.rem(dp, local)
    own = lax.rem(dp, local)
    top = local // 2
    far_bit = dps // 2
    mid = zs // 2
    laid_out = local == 4 and dps == 8
    me_at = jnp.reshape(dp, (1,)).astype(jnp.int32)
    expert_at = jnp.stack([expert, dp]).astype(jnp.int32)
    at = Flow()

    extra = jnp.concatenate(
        [router, norm_gains, jnp.zeros((own_rows, EXTRA - experts - 4), BF16)], axis=1
    )
    sent = jnp.stack(
        [
            jnp.concatenate(
                [w_qkv[:, i * width + e * cols : i * width + (e + 1) * cols] for i in range(3)]
                + [extra],
                axis=1,
            )
            for e in range(zs)
        ]
    )
    at["mine"] = lax.all_to_all(sent, "expert", split_axis=0, concat_axis=0, tiled=True)
    moved = [(b, (b % dps) * zs + b // dps) for b in range(dps * zs)]

    for e in range(local):
        at["w", 0, e] = jnp.concatenate(
            [pick(w_gate_up, own ^ e, 1), pick(w_down, own ^ e, 1)], axis=1
        )
    at["x0"] = tokens
    at["out"] = w_out
    at.fence("mine", "x0", "out", *at.having("w"))

    at["attn"] = lax.all_gather(
        at["mine"].reshape(zs * own_rows, 3 * cols + EXTRA), "dp", axis=0, tiled=True
    )
    if laid_out:
        at["w", 1, 0] = flip(at["w", 0, 1], 1)
        at["w", 1, 2] = flip(at["w", 0, 3], 1)
    at["lengths"], at["order"], at["routes"], at["cot"] = lengths, permutation, routes, cotangent
    for i in range(1, zs):
        at[f"x{i}"] = hop(at[f"x{i - 1}"])
        if i == 1:
            at.fence("x1", "lengths", "order", "routes", "cot", "out")
            places_and_tables(at, dp, zs, rows)
        elif i == 2:
            at.fence("x2", "cos", "sin", "seg", "routes", "cot")
            at["mask"] = jnp.sum(
                (at["routes"][:, :, None] == jnp.arange(experts, dtype=jnp.int32)).astype(BF16),
                axis=1,
            )
            mask_pad = jnp.concatenate(
                [at["mask"], jnp.zeros((rows, EXTRA - experts), BF16)], axis=1
            )
            at["g0"] = jnp.concatenate([at["cot"], mask_pad], axis=1)
            at["out"] = lax.ppermute(at["out"], ("dp", "expert"), moved)
        else:
            at.fence(f"x{i}")
    xs = [f"x{i}" for i in range(zs)]
    at.fence("attn", "out", "g0", "mask", *xs, *at.having("w"))

    cut = e_rows // 4
    if laid_out:
        at["w", 2, 0] = flip(at["w", 0, 2], 2)
        at["w", 4, 0] = flip(at["w", 0, 0], 4)
        at["wa", 5] = flip(at["w", 1, 0][:cut], 4)
    at["g1"] = hop(at["g0"])
    out_w = lax.all_gather(at["out"], "dp", axis=0, tiled=True)
    attn_w = at["attn"]
    qkv_w = attn_w[:, : 3 * cols]
    router_full = attn_w[:, 3 * cols : 3 * cols + experts]
    gains = attn_w[:, 3 * cols + experts : 3 * cols + experts + 4].astype(F32).T
    router_t = router_full.T
    x_all = by_line([at[key] for key in xs])
    xf = x_all.astype(F32)
    r_attn = inv_rms(xf)
    a_all = (xf * r_attn * gains[0]).astype(BF16)
    at["qkv"] = nn(a_all, qkv_w)
    at.fence("qkv", "g1")
    qkv = at["qkv"]
    q, k = qkv[:, :cols], qkv[:, cols : 2 * cols]
    at["squares"] = lax.psum(
        jnp.stack([jnp.sum(q * q, axis=1), jnp.sum(k * k, axis=1)]), "expert"
    )
    at.fence("squares", "g1")
    at["g2"] = hop(at["g1"])
    by_block = lambda v: v.reshape(2, zs, rows).transpose(1, 0, 2)
    r_qk = by_block(lax.rsqrt(at["squares"] / width + EPSILON))
    gain_qk = lax.dynamic_slice_in_dim(gains[1:3], z * cols, cols, axis=1)
    cos, sin, seg = at["cos"], at["sin"], at["seg"]
    qr, kr, vb, o = attend(qkv, r_qk, gain_qk, cos, sin, seg)
    at["added"] = nn(o, out_w, BF16)
    at.fence("added", "g2", *(w for w in at.having("w") + at.having("wa") if laid_out))
    at["added"] = lax.psum_scatter(at["added"], "expert", scatter_dimension=0, tiled=True)
    for i in range(3, zs):
        at[f"g{i}"] = hop(at[f"g{i - 1}"])
    if laid_out:
        at["w", 3, 0] = flip(at["w", 1, 2], 2)
        at["wb", 5] = flip(at["w", 1, 0][cut:], 4)
        at["wa", 6] = flip(at["w", 2, 0][: 3 * cut], 4)
    first_g = [f"g{i}" for i in range(mid)]
    last_g = [f"g{i}" for i in range(mid, zs)]
    at["far ga"] = flip(jnp.concatenate([at[key] for key in first_g], axis=0), top)
    weight_keys = at.having("w") + at.having("wa") + at.having("wb")
    at.fence("added", "far ga", f"g{zs - 1}", *(w for w in weight_keys if laid_out))
    at["far gb"] = flip(jnp.concatenate([at[key] for key in last_g], axis=0), top)
    if laid_out:
        at["wb", 6] = flip(at["w", 2, 0][3 * cut :], 4)
        at["w", 7, 0] = flip(at["w", 3, 0], 4)
    hid = tokens.astype(F32) + at["added"].astype(F32)
    r_ffn = inv_rms(hid)
    m = (hid * r_ffn * gains[3]).astype(BF16)

    at["m0"] = m
    at["far m0"] = flip(m, top)
    for i in range(1, zs):
        at[f"m{i}"] = hop(at[f"m{i - 1}"])
        at.fence(f"m{i}")
        at[f"far m{i}"] = flip(at[f"m{i}"], top)
    mine_e = (jnp.arange(experts) == expert).astype(F32)
    g_near = [jnp.concatenate([at[key] for key in first_g + last_g], axis=0)]
    near_parts = [x for xs in fan(g_near, top) for x in xs]
    far_parts = [x for xs in fan([at["far ga"], at["far gb"]], top) for x in xs]
    if laid_out:
        keys = [("w", r, 0) for r in range(5)] + [(h, r) for r in (5, 6) for h in ("wa", "wb")]
        weights = jnp.concatenate([at[key] for key in [*keys, ("w", 7, 0)]], axis=0)
    else:
        weights = spread({e: at["w", 0, e] for e in range(local)}, dps)

    def chunk_front(parts):
        masks = jnp.concatenate([x[:, width : width + experts] for x in parts], axis=0)
        masks = masks.astype(F32).reshape(-1, rows, experts)
        on = jnp.sum(masks * mine_e, axis=2)
        pos = jnp.where(on > 0, jnp.cumsum(on, axis=1) - 1.0, -1.0).astype(jnp.int32)
        gs, gw = front(parts, pos, weights, ff, me_at)
        return pos, pos.T, masks.transpose(0, 2, 1), gs, gw

    def chunk_expert(blocks, pieces, fronted):
        pos, pos_t, named, gs, gw = fronted
        parts = [blocks] + fan(pieces, top)[1:]
        flat = [x for xs in parts for x in xs]
        backs, outs = run_expert(flat, pos, pos_t, named, router_t, weights, gw, expert_at, ff)
        back = []
        for xs in parts:
            back.append(backs[: len(xs)])
            backs = backs[len(xs) :]
        return back, (outs[0], gs, outs[1], outs[2], outs[3])

    ms = [at[f"m{i}"] for i in range(zs)]
    near = chunk_front(near_parts)
    near_back, near_outs = chunk_expert(ms, [jnp.concatenate(ms, axis=0)], near)
    far = chunk_front(far_parts)
    far_ms = [f"far m{i}" for i in range(zs)]
    at["near gact"] = near_outs[4]
    at.fence("near gact", *far_ms)
    ms = [at[key] for key in far_ms]
    pieces = [jnp.concatenate(ms[:mid], axis=0), jnp.concatenate(ms[mid:], axis=0)]
    far_back, far_outs = chunk_expert(ms, pieces, far)
    near_outs = (*near_outs[:4], at["near gact"])

    quarter = dps // 4
    near_sum = fold(near_back)
    far_sum = fold(far_back)
    chunk_keys = [("c", n) for n in range(10)]
    for key, v in zip(chunk_keys, (*near_outs, *far_outs), strict=True):
        at[key] = v
    for i, v in enumerate(far_sum):
        at["far", i] = v
    at.fence(*at.having("far"), *chunk_keys)

    def chunk_grads(first):
        c = [at[key] for key in chunk_keys]
        return grads([c[:5], c[5:]], first, quarter, e_rows)

    last = zs - 1
    highs = [("got", 3 * quarter + i) for i in range(quarter)]
    at["there"] = flip(at["far", last], top)
    at["send high"] = chunk_grads(3 * quarter)
    at.fence("there", "send high", *chunk_keys)
    for i in reversed(range(zs)):
        here = near_sum[i].astype(F32) + at["there"].astype(F32)
        if i < last:
            here = here + at["acc"].astype(F32)
        at["acc"] = here.astype(BF16)
        if not i:
            break
        at["acc"] = hop(at["acc"], -1)
        at["there"] = flip(at["far", i - 1], top)
        beside = []
        if i == last:
            for n in range(quarter):
                at["got", 3 * quarter + n] = flip(at["send high"][n], far_bit)
            for n, y in enumerate(result(at["c", 9], far[1], weights, top, me_at)):
                at["y part", n] = y
            beside = at.having("y part")
        if i == last - 1:
            at["send low"] = chunk_grads(2 * quarter)
            at["y far"] = fold([[at[key]] for key in at.having("y part")])[0]
            beside = ["send low", "y far", *highs[: quarter // 2]]
        if i == last - 2:
            at["keep high"] = chunk_grads(quarter)
            beside = ["keep high", *highs[quarter // 2 :]]
        at.fence("acc", "there", *beside, *chunk_keys)
    dm = at["acc"].astype(F32)
    at["y far"] = flip(at["y far"], top)
    at["got", 2 * quarter] = flip(at["send low"][0], far_bit)

    own_mask = at["mask"].astype(F32)
    own_logits = jnp.where(own_mask > 0, nn(m, router_full), -1e30)
    own_e = jnp.where(
        own_mask > 0, jnp.exp(own_logits - jnp.max(own_logits, axis=1, keepdims=True)), 0.0
    )
    gate_own = own_e / jnp.sum(own_e, axis=1, keepdims=True)
    dgates = dm[:, width : width + experts] + dm[:, width + experts : width + 2 * experts]
    dz = (
        gate_own * (dgates - jnp.sum(gate_own * dgates, axis=1, keepdims=True))
    ).astype(BF16)
    dmt = nt(dz, router_full) + dm[:, :width]
    grad_out = cotangent.astype(F32)
    dh = grad_out + rms_back(hid, r_ffn, gains[3], dmt)
    at["dhb"] = lax.all_gather(dh.astype(BF16), "expert", axis=0, tiled=True)
    router_part = tn(m, dz)
    gain_ffn = jnp.sum(dmt * hid * r_ffn, axis=0)
    at["keep low"] = chunk_grads(0)
    at["y near"] = fold([[x] for x in result(at["c", 4], near[1], weights, top, me_at)])[0]
    at["router"], at["gain ffn"] = router_part, gain_ffn
    at.fence(
        "dhb", "y far", "y near", "keep low", "send low", "router", "gain ffn",
        ("got", 2 * quarter),
    )
    dhb = at["dhb"]
    for i in range(1, quarter):
        at["got", 2 * quarter + i] = flip(at["send low"][i], far_bit)
    for i in range(quarter):
        at["tail", quarter + i, 0] = add(at["keep high"][i], at["got", 3 * quarter + i])
    if laid_out:
        at["tail", 0, 2] = flip(at["tail", 2, 0], 2)
    y_own = add(at["y near"], at["y far"])
    at["y"] = lax.psum_scatter(
        by_line([y_own[i * rows : (i + 1) * rows] for i in range(zs)]),
        "expert",
        scatter_dimension=0,
        tiled=True,
    )

    dqn, dkn, dv, sums = attend_back(dhb, out_w, qkv, qr, kr, vb, gain_qk, cos, sin, seg)
    means = lax.psum(sums.transpose(1, 0, 2).reshape(2, zs * rows), "expert") / width
    dqkv, gains_qk = join_back(qkv, dqn, dkn, dv, r_qk, by_block(means), gain_qk)
    at["dqkv"] = dqkv
    lows = [("got", 2 * quarter + i) for i in range(quarter)]
    at.fence("dqkv", "dhb", "y", *lows, *at.having("tail"))
    if laid_out:
        at["tail", 1, 2] = flip(at["tail", 3, 0], 2)

    at["odd"] = attn_grads(a_all, at["dqkv"], [], me_at, 1, 2)
    at.fence("odd", "dqkv", "dhb")
    at["odd"] = flip(at["odd"], 1)
    at["da"], at["gain attn"] = first_back(at["dqkv"], attn_w, x_all, r_attn, rows)
    at.fence("odd", "dqkv", "da", "gain attn")
    at["da"] = lax.psum_scatter(at["da"], "expert", scatter_dimension=0, tiled=True)
    at["held"] = add(attn_grads(a_all, at["dqkv"], [], me_at, 0, 2), at["odd"])
    at.fence("held", "dhb")
    sides = halves(at["held"], zs * own_rows)
    stage(at, sides, 0)
    out_blocks = tn(o, at["dhb"], BF16).reshape(dps, own_rows, width)
    at["out grad"] = jnp.concatenate([pick(out_blocks, dp ^ r, 0) for r in range(dps)], axis=0)
    for i in range(quarter):
        at["tail", i, 0] = add(at["keep low"][i], at["got", 2 * quarter + i])
    for turn_ in range(1, len(bits_of(2, dps))):
        at.fence(*at.having("side"), "out grad", *at.having("tail"))
        sides = unstage(at, sides, turn_ - 1)
        stage(at, sides, turn_)
        if laid_out:
            for e in (0, 2):
                at["tail", 0, e ^ 1] = flip(at["tail", 1, e], 1)
    at.fence(*at.having("side"), "out grad", "gain attn", "da", *at.having("tail"))
    sides = unstage(at, sides, len(bits_of(2, dps)) - 1)
    at["back"] = lax.all_to_all(
        jnp.concatenate([sides[0][0][0], sides[1][0][0]], axis=1).reshape(zs, own_rows, 3 * cols),
        "expert",
        split_axis=0,
        concat_axis=0,
        tiled=True,
    )
    if laid_out:
        blocks = {e: at["tail", 0, e] for e in range(local)}
    else:
        blocks = gather_back({k[1]: at[k] for k in at.having("tail")}, local, dps)
    stacked = jnp.stack([blocks[e] for e in range(local)])
    blocks = [pick(stacked, own ^ e, 0) for e in range(local)]
    at["gu"] = jnp.stack([b[:, : 2 * ff] for b in blocks], axis=1).astype(F32)
    at["dn"] = jnp.stack([b[:, 2 * ff :] for b in blocks], axis=1).astype(F32)
    zero = jnp.zeros((2, width), F32)
    gain_rows = jnp.concatenate(
        [
            at["gain attn"],
            lax.dynamic_update_slice_in_dim(zero, gains_qk, z * cols, 1),
            at["gain ffn"][None],
            jnp.zeros((EXTRA - experts - 4, width), F32),
        ],
        axis=0,
    )
    extra_part = jnp.concatenate([at["router"], gain_rows.T], axis=1).astype(BF16)
    at["extra"] = lax.psum_scatter(extra_part, "dp", scatter_dimension=0, tiled=True)
    at["out grad"] = scatter_dp(at["out grad"], own_rows)
    at.fence("back", "extra", "gu", "dn", "out grad")
    grad_w_out = lax.ppermute(
        at["out grad"], ("dp", "expert"), [(b, a) for a, b in moved]
    ).astype(F32)
    back = at["back"].astype(F32)
    grad_w_qkv = jnp.concatenate(
        [back[e, :, i * cols : (i + 1) * cols] for i in range(3) for e in range(zs)], axis=1
    )
    extra_back = lax.all_to_all(
        at["extra"].reshape(zs, own_rows, EXTRA), "expert", split_axis=0, concat_axis=0, tiled=True
    )
    extra_sum = jnp.sum(extra_back.astype(F32), axis=0)
    grad_router = extra_sum[:, :experts]
    grad_gains = extra_sum[:, experts : experts + 4]
    da = at["da"].astype(F32)

    output = hid + at["y"].astype(F32)
    x_own = tokens.astype(F32)
    grad_tokens = dh + rms_back(x_own, inv_rms(x_own), gains[0], da)
    return (
        output,
        grad_tokens,
        grad_gains,
        grad_w_qkv,
        grad_w_out,
        grad_router,
        at["gu"],
        at["dn"],
    )


def solution(mesh):
    both = P(("dp", "expert"), None)
    experts = P("dp", "expert", None)
    return jax.shard_map(
        on_device,
        mesh=mesh,
        in_specs=(both, P(), P(), both, both, both, both, both, experts, experts, both),
        out_specs=(both, both, both, both, both, both, experts, experts),
        check_vma=False,
    )
```

```python
import functools

import jax
import jax.numpy as jnp
from jax import lax
from jax.experimental import pallas as pl
from jax.experimental.pallas import tpu as pltpu
from jax.sharding import PartitionSpec as P

HEADS = 16
HEAD_DIM = 128
SEQ_DEV = 2
EPSILON = 1e-06
ROPE_BASE = 50000.0
CAP = 80
EXTRA = 128
VMEM = 56 * 2**20
COST = pl.CostEstimate(flops=10**6, bytes_accessed=10**5, transcendentals=0)

F32 = jnp.float32
BF16 = jnp.bfloat16


def dot(a, b, dims, out=F32):
    return lax.dot_general(a, b, (dims, ((), ())), preferred_element_type=F32).astype(out)


def nn(a, b, out=F32):
    return dot(a, b, ((1,), (0,)), out)


def nt(a, b, out=F32):
    return dot(a, b, ((1,), (1,)), out)


def tn(a, b, out=F32):
    return dot(a, b, ((0,), (0,)), out)


def flip(v, bit):
    return lax.ppermute(v, "dp", [(i, i ^ bit) for i in range(lax.axis_size("dp"))])


def ring(n):
    return [*range(0, n, 2), *reversed(range(1, n, 2))]


def hop(v, step=1):
    order = ring(lax.axis_size("expert"))
    n = len(order)
    pairs = [(order[i], order[(i + step) % n]) for i in range(n)]
    return lax.ppermute(v, "expert", pairs)


def gather_ring(v):
    return [v] + [hop(v, i) for i in range(1, lax.axis_size("expert"))]


def places_in_ring():
    n = lax.axis_size("expert")
    at = [ring(n).index(i) for i in range(n)]
    at = jnp.asarray(at, jnp.int32)
    return lax.rem(at[lax.axis_index("expert")] - at + n, n)


def by_line(blocks):
    where = places_in_ring()
    stacked = jnp.stack(blocks)
    return jnp.concatenate([pick(stacked, where[i], 0) for i in range(len(blocks))], axis=0)


def bits_of(low, high):
    out = []
    while low < high:
        out.append(low)
        low *= 2
    return out


def pick(v, index, axis):
    return lax.dynamic_index_in_dim(v, index, axis, keepdims=False)


def tie(*values):
    return lax.optimization_barrier(values)


(
    ORDER,
    LENGTHS,
    COS,
    SIN,
    SEG,
    MINE,
    W,
    X,
    OUT,
    ATTN,
    ROUTES,
    COT,
    MASK,
    G,
    QKV,
    SQUARES,
    ADDED,
    WA,
    FAR_GA,
    WB,
    M,
    NEAR_GACT,
    C,
    FAR,
    THERE,
    SEND_HIGH,
    ACC,
    Y_PART,
    NEAR_PART,
    SEND_LOW,
    Y_FAR,
    Y_NEAR,
    DHB,
    KEEP_HIGH,
    KEEP_LOW,
    ROUTER,
    GAIN_FFN,
    TAIL,
    Y,
    DQKV,
    ODD,
    DA,
    GAIN_ATTN,
    HELD,
    OUT_GRAD,
    BESIDE,
    SIDE,
    BACK,
    GU,
    DN,
    NEAR,
    DISTANT,
    PIECE,
    BACKS,
    ROWS,
    HALF,
) = range(56)


class Flow:
    def __init__(self):
        self.of = {}

    def fence(self, *keys):
        out = tie(*[self.of[key] for key in keys])
        for key, v in zip(keys, out, strict=True):
            self.of[key] = v

    def __getitem__(self, key):
        return self.of[key]

    def __setitem__(self, key, value):
        self.of[key] = value

    def having(self, kind):
        return [key for key in self.of if isinstance(key, tuple) and key[0] == kind]


def fan(pieces, low):
    out = [list(pieces)]
    for bit in bits_of(1, low):
        out = out + [[flip(x, bit) for x in xs] for xs in out]
    return out


def add(a, b):
    return (a.astype(F32) + b.astype(F32)).astype(BF16)


def match(pieces, like):
    if len(pieces) == len(like):
        return pieces
    step = like[0].shape[0]
    return [x[i : i + step] for x in pieces for i in range(0, x.shape[0], step)]


def fold(parts):
    parts = list(parts)
    while len(parts) > 1:
        half = len(parts) // 2
        for i in range(half):
            got = match([flip(x, half) for x in reversed(parts[half + i])][::-1], parts[i])
            parts[i] = [add(a, b) for a, b in zip(parts[i], got, strict=True)]
        parts = parts[:half]
    return parts[0]


def scatter_step(at, bit):
    keys = sorted(key for key in at.having(OUT_GRAD) if key[1] & bit)
    v = [at.of.pop(key) for key in keys]
    got = flip(jnp.concatenate(v, axis=0) if len(v) > 1 else v[0], bit)
    rows = v[0].shape[0]
    for i, (_, r) in enumerate(keys):
        to = OUT_GRAD, r ^ bit
        at[to] = add(at[to], got[i * rows : (i + 1) * rows])


def blocks_of(parts, tok):
    return [(i, at) for i, p in enumerate(parts) for at in range(0, p.shape[0], tok)]


def onehot_back(pos_t, b):
    slot = lax.broadcasted_iota(jnp.int32, (pos_t.shape[0], CAP), 1)
    return (slot == pos_t[:, b : b + 1]).astype(BF16)


def onehot(pos_ref, b):
    slot = lax.broadcasted_iota(jnp.int32, (CAP, pos_ref.shape[1]), 0)
    return slot == pos_ref[b : b + 1, :]


def mm(a, b, dims):
    return lax.dot_general(a, b, (dims, ((), ())), preferred_element_type=F32)


def to_distance(ref, rows, value, me):
    n = lax.axis_size("dp")
    wide = value.shape[1] // n
    for c in range(n):
        at = pl.multiple_of((me ^ c) * wide, wide)
        ref[rows, pl.ds(at, wide)] = value[:, c * wide : (c + 1) * wide]


def gather_kernel(count, g_count, expert, *refs):
    parts, refs = refs[:count], refs[count:]
    g_parts, refs = refs[:g_count], refs[g_count:]
    pos, named, router, rows_out, gs_out, gate = refs
    tok = pos.shape[1]
    width = rows_out.shape[1]
    for b, (i, first) in enumerate(blocks_of(parts, tok)):
        at = slice(b * CAP, (b + 1) * CAP)
        part = parts[i][first : first + tok, :]
        hot = onehot(pos, b)
        found = mm(hot.astype(BF16), part, ((1,), (0,))).astype(BF16)
        to_distance(rows_out, at, found, expert[1])
        chosen = named[b] > 0
        logits = jnp.where(chosen, mm(router[...], part, ((1,), (1,))), -1e30)
        e = jnp.where(chosen, jnp.exp(logits - jnp.max(logits, axis=0, keepdims=True)), 0.0)
        gates = e / jnp.sum(e, axis=0, keepdims=True)
        mine = lax.broadcasted_iota(jnp.int32, gates.shape, 0) == expert[0]
        row = jnp.sum(jnp.where(mine, gates, 0.0), axis=0, keepdims=True)
        gate[at, :] = jnp.sum(jnp.where(hot, row, 0.0), axis=1, keepdims=True)
    for b, (i, first) in enumerate(blocks_of(g_parts, tok)):
        part = g_parts[i][first : first + tok, :width]
        found = mm(onehot(pos, b).astype(BF16), part, ((1,), (0,))).astype(BF16)
        to_distance(gs_out, slice(b * CAP, (b + 1) * CAP), found, expert[1])


def gather(parts, g_parts, pos, named, router, expert):
    slots, width = pos.shape[0] * CAP, parts[0].shape[1]
    ins = [*parts, *g_parts, pos, named, router]
    whole = lambda x: pl.BlockSpec(x.shape, lambda n, e: (0,) * len(x.shape))
    outs = [
        jax.ShapeDtypeStruct((slots, width), BF16),
        jax.ShapeDtypeStruct((slots, width), BF16),
        jax.ShapeDtypeStruct((slots, 1), F32),
    ]
    return pl.pallas_call(
        functools.partial(gather_kernel, len(parts), len(g_parts)),
        grid_spec=pltpu.PrefetchScalarGridSpec(
            num_scalar_prefetch=1,
            grid=(1,),
            in_specs=[whole(x) for x in ins],
            out_specs=[whole(x) for x in outs],
        ),
        out_shape=outs,
        compiler_params=pltpu.CompilerParams(vmem_limit_bytes=VMEM),
        cost_estimate=COST,
        name="gather",
    )(expert, *ins)


def spans(pieces):
    out, at = [], 0
    for p in pieces:
        out.append(slice(at, at + p.shape[0]))
        at += p.shape[0]
    return out


def expert_kernel(count, pieces, expert, *refs):
    rows_in, gs_in, gate, pos_t = refs[:4]
    parts = [refs[4 + i * pieces : 4 + (i + 1) * pieces] for i in range(3)]
    refs = refs[4 + 3 * pieces :]
    backs, refs = refs[:count], refs[count:]
    dg_out, du_out, gact_out, acc, dgate, wg, wu, wd = refs
    n = pl.program_id(0)
    tok = pos_t.shape[0]
    width = rows_in.shape[1]
    for at, a, b, c in zip(spans(parts[0]), *parts, strict=True):
        wg[at, :] = a[...]
        wu[at, :] = b[...]
        wd[at, :] = c[...]

    rows = rows_in[...]
    g = mm(rows, wg[...], ((1,), (0,)))
    u = mm(rows, wu[...], ((1,), (0,)))
    gw = mm(gs_in[...], wd[...], ((1,), (0,)))
    sg = 1.0 / (1.0 + jnp.exp(-g))
    silu = g * sg
    act = (silu * u).astype(BF16).astype(F32)
    part = jnp.sum(act * gw, axis=1, keepdims=True)
    gate_v = gate[...]
    gact_out[...] = (gate_v * act).astype(BF16)
    dact = gate_v * gw
    dg = (dact * u * (sg * (1.0 + g * (1.0 - sg)))).astype(BF16)
    du = (dact * silu).astype(BF16)
    dg_out[...] = dg
    du_out[...] = du
    back = mm(dg, wg[...], ((1,), (1,))) + mm(du, wu[...], ((1,), (1,)))

    @pl.when(n == 0)
    def _():
        acc[...] = back
        dgate[...] = part

    @pl.when(n > 0)
    def _():
        acc[...] += back
        dgate[...] += part

    @pl.when(n == pl.num_programs(0) - 1)
    def _():
        lane = lax.broadcasted_iota(jnp.int32, (CAP, EXTRA), 1)
        for b, (i, first) in enumerate(blocks_of(backs, tok)):
            at = slice(b * CAP, (b + 1) * CAP)
            to = slice(first, first + tok)
            hot = onehot_back(pos_t, b)
            out = backs[i]
            found = mm(hot, acc[at, :].astype(BF16), ((1,), (0,))).astype(BF16)
            to_distance(out, to, found, expert[1])
            d = dgate[at, :]
            hi = d.astype(BF16).astype(F32)
            beside = jnp.where(
                lane == expert[0], hi, jnp.where(lane == expert[2] + expert[0], d - hi, 0.0)
            ).astype(BF16)
            out[to, width:] = mm(hot, beside, ((1,), (0,))).astype(BF16)


def run_expert(rows, gs, gate, pos_t, pieces, expert, heights, ff):
    slots, width = rows.shape
    tile = min(512, ff)
    steps = ff // tile
    whole = lambda x: pl.BlockSpec(x.shape, lambda n, e: (0,) * len(x.shape))
    column = pl.BlockSpec((slots, tile), lambda n, e: (0, n))
    backs = [jax.ShapeDtypeStruct((h, width + EXTRA), BF16) for h in heights]
    thin = jax.ShapeDtypeStruct((slots, ff), BF16)
    outs = pl.pallas_call(
        functools.partial(expert_kernel, len(heights), len(pieces)),
        grid_spec=pltpu.PrefetchScalarGridSpec(
            num_scalar_prefetch=1,
            grid=(steps,),
            in_specs=[whole(x) for x in (rows, gs, gate, pos_t)]
            + [pl.BlockSpec((p.shape[0], tile), lambda n, e: (0, n)) for p in pieces]
            + [pl.BlockSpec((p.shape[0], tile), lambda n, e: (0, steps + n)) for p in pieces]
            + [pl.BlockSpec((p.shape[0], tile), lambda n, e: (0, 2 * steps + n)) for p in pieces],
            out_specs=[whole(x) for x in backs] + [column, column, column],
            scratch_shapes=[pltpu.VMEM((slots, width), F32), pltpu.VMEM((slots, 1), F32)]
            + [pltpu.VMEM((width, tile), BF16)] * 3,
        ),
        out_shape=backs + [thin, thin, thin],
        compiler_params=pltpu.CompilerParams(vmem_limit_bytes=VMEM),
        cost_estimate=COST,
        name="expert",
    )(expert, rows, gs, gate, pos_t, *pieces, *pieces, *pieces)
    return outs[: len(heights)], outs[len(heights) :]


def result_kernel(count, pieces, wide, me, gact, pos_t, *refs):
    parts, outs, wd = refs[:pieces], refs[pieces : pieces + count], refs[-1]
    tok = pos_t.shape[0]
    n = pl.program_id(0)
    blocks = wd.shape[0] // wide // pl.num_programs(0)

    @pl.when(n == 0)
    def _():
        for at, w in zip(spans(parts), parts, strict=True):
            wd[at, :] = w[...]

    step = blocks * wide
    here = wd[pl.ds(pl.multiple_of(n * step, step), step), :]
    y = mm(gact[...], here, ((1,), (1,))).astype(BF16)
    for b, (i, at) in enumerate(blocks_of(outs, tok)):
        part = y[b * CAP : (b + 1) * CAP, :]
        part = mm(onehot_back(pos_t, b), part, ((1,), (0,))).astype(BF16)
        for k in range(blocks):
            to = pl.multiple_of((me[0] ^ (blocks * n + k)) * wide, wide)
            outs[i][at : at + tok, pl.ds(to, wide)] = part[:, k * wide : (k + 1) * wide]


def result(gact, pos_t, pieces, count, me):
    slots, ff = gact.shape
    width = sum(p.shape[0] for p in pieces)
    wide = width // lax.axis_size("dp")
    tile = max(wide, min(512, width))
    last = (pieces[0].shape[1] - ff) // ff
    out = jax.ShapeDtypeStruct((pos_t.shape[1] // count * pos_t.shape[0], width), BF16)
    return pl.pallas_call(
        functools.partial(result_kernel, count, len(pieces), wide),
        grid_spec=pltpu.PrefetchScalarGridSpec(
            num_scalar_prefetch=1,
            grid=(width // tile,),
            in_specs=[
                pl.BlockSpec((slots, ff), lambda n, me: (0, 0)),
                pl.BlockSpec(pos_t.shape, lambda n, me: (0, 0)),
            ]
            + [pl.BlockSpec((p.shape[0], ff), lambda n, me: (0, last)) for p in pieces],
            out_specs=[pl.BlockSpec(out.shape, lambda n, me: (0, 0))] * count,
            scratch_shapes=[pltpu.VMEM((width, ff), BF16)],
        ),
        out_shape=[out] * count,
        compiler_params=pltpu.CompilerParams(vmem_limit_bytes=VMEM),
        cost_estimate=COST,
        name="result",
    )(me, gact, pos_t, *pieces)


def grads_kernel(count, *refs):
    out = refs[-1]
    ff = refs[2].shape[1]
    gate = up = down = 0.0
    for c in range(count):
        rows, gs, dg, du, gact = refs[5 * c : 5 * c + 5]
        gate = gate + mm(rows[...], dg[...], ((0,), (0,)))
        up = up + mm(rows[...], du[...], ((0,), (0,)))
        down = down + mm(gs[...], gact[...], ((0,), (0,)))
    out[0, :, :ff] = gate.astype(BF16)
    out[0, :, ff : 2 * ff] = up.astype(BF16)
    out[0, :, 2 * ff :] = down.astype(BF16)


def grads(chunks, first, blocks, rows):
    ff = chunks[0][2].shape[1]
    specs, ins = [], []
    for chunk in chunks:
        slots = chunk[0].shape[0]
        tall = pl.BlockSpec((slots, rows), lambda i: (0, first + i))
        flat = pl.BlockSpec((slots, ff), lambda i: (0, 0))
        specs += [tall, tall, flat, flat, flat]
        ins += list(chunk)
    slots = sum(chunk[0].shape[0] for chunk in chunks)
    return pl.pallas_call(
        functools.partial(grads_kernel, len(chunks)),
        grid=(blocks,),
        in_specs=specs,
        out_specs=pl.BlockSpec((1, rows, 3 * ff), lambda i: (i, 0, 0)),
        out_shape=jax.ShapeDtypeStruct((blocks, rows, 3 * ff), BF16),
        compiler_params=pltpu.CompilerParams(vmem_limit_bytes=VMEM),
        cost_estimate=COST,
        name="grads",
    )(*ins)


def attn_grads_kernel(me, a, d, *rest):
    k = d.shape[1]
    out = rest[-1]
    out[:, :k] = mm(a[...], d[...], ((0,), (0,))).astype(BF16)
    if len(rest) > 1:
        out[:, k:] = rest[0][...]


def attn_grads(a, d, extra, me, first, stride):
    rows, width = a.shape
    n = lax.axis_size("dp")
    tile = width // n
    count = n // stride
    at = lambda i, me: me[0] ^ (first + stride * i)
    k = d.shape[1] + sum(e.shape[1] for e in extra)
    return pl.pallas_call(
        attn_grads_kernel,
        grid_spec=pltpu.PrefetchScalarGridSpec(
            num_scalar_prefetch=1,
            grid=(count,),
            in_specs=[
                pl.BlockSpec((rows, tile), lambda i, me: (0, at(i, me))),
                pl.BlockSpec(d.shape, lambda i, me: (0, 0)),
            ]
            + [pl.BlockSpec((tile, e.shape[1]), lambda i, me: (at(i, me), 0)) for e in extra],
            out_specs=pl.BlockSpec((tile, k), lambda i, me: (i, 0)),
        ),
        out_shape=jax.ShapeDtypeStruct((count * tile, k), BF16),
        compiler_params=pltpu.CompilerParams(vmem_limit_bytes=VMEM),
        cost_estimate=COST,
        name="attn_grads",
    )(me, a, d, *extra)


def halves(held, rows):
    n = lax.axis_size("dp")
    wide = held.shape[1] // 256 * 128
    out = []
    for left, right, order in (
        (0, wide, bits_of(2, n)),
        (wide, held.shape[1], bits_of(2, n)[::-1]),
    ):
        side = {2 * i: held[i * rows : (i + 1) * rows, left:right] for i in range(n // 2)}
        out.append((side, order))
    return out


def stage(at, sides, step):
    for s, (side, order) in enumerate(sides):
        keys = sorted(r for r in side if r & order[step])
        v = [side[r] for r in keys]
        at[SIDE, s] = flip(jnp.concatenate(v, axis=0) if len(v) > 1 else v[0], order[step])


def unstage(at, sides, step):
    out = []
    for s, (side, order) in enumerate(sides):
        bit = order[step]
        keys = sorted(r for r in side if r & bit)
        rows = side[0].shape[0]
        got = at[SIDE, s]
        kept = {r: v for r, v in side.items() if not r & bit}
        for i, r in enumerate(keys):
            kept[r ^ bit] = add(kept[r ^ bit], got[i * rows : (i + 1) * rows])
        out.append((kept, order))
    return out


def spread(first, n):
    local = len(first)
    have = {(0, e): v for e, v in first.items()}
    for bit in bits_of(1, local):
        for key in sorted(key for key in have if key[1] & bit):
            have[(key[0] ^ bit, key[1] ^ bit)] = flip(have.pop(key), bit)
    for bit in bits_of(local, n):
        for key in sorted(have):
            have[(key[0] ^ bit, 0)] = flip(have[key], bit)
    return [have[key] for key in sorted(have)]


def gather_back(held, local, n):
    held = dict(held)
    for bit in reversed(bits_of(local, n // 2)):
        for r in sorted(r for r in held if r & bit):
            held[r ^ bit] = add(held[r ^ bit], flip(held.pop(r), bit))
    have = {(r, 0): v for r, v in held.items()}
    for bit in reversed(bits_of(1, local)):
        for key in sorted(key for key in have if key[0] & bit):
            have[(key[0] ^ bit, key[1] ^ bit)] = flip(have.pop(key), bit)
    return {e: v for (_, e), v in have.items()}


def per_row(row):
    return jnp.broadcast_to(row, (row.shape[1], row.shape[1])).T


def turn(v, cos, sin):
    return v * cos + pltpu.roll(v, v.shape[1] // 2, 1) * sin


def softmax_rows(qr, kr, same, scale):
    s = jnp.where(same, mm(qr, kr, ((1,), (1,))) * scale, -1e30)
    e = jnp.exp(s - jnp.max(s, axis=1, keepdims=True))
    return e / jnp.sum(e, axis=1, keepdims=True)


def attend_kernel(scale, qkv, r, gains, cos, sin, seg, qr_out, kr_out, vb_out, o_out):
    cols = o_out.shape[1]
    rq, rk = per_row(r[0, 0:1, :]), per_row(r[0, 1:2, :])
    seg_row = seg[0]
    same = per_row(seg_row) == seg_row
    for h in range(cols // HEAD_DIM):
        at = slice(h * HEAD_DIM, (h + 1) * HEAD_DIM)
        k_at = slice(cols + h * HEAD_DIM, cols + (h + 1) * HEAD_DIM)
        v_at = slice(2 * cols + h * HEAD_DIM, 2 * cols + (h + 1) * HEAD_DIM)
        qr = turn(qkv[:, at] * rq * gains[0:1, at], cos[...], sin[...]).astype(BF16)
        kr = turn(qkv[:, k_at] * rk * gains[1:2, at], cos[...], sin[...]).astype(BF16)
        vb = qkv[:, v_at].astype(BF16)
        p = softmax_rows(qr, kr, same, scale)
        qr_out[:, at] = qr
        kr_out[:, at] = kr
        vb_out[:, at] = vb
        o_out[:, at] = mm(p.astype(BF16), vb, ((1,), (0,))).astype(BF16)


def attend(qkv, r, gains, cos, sin, seg):
    total, cols = qkv.shape[0], qkv.shape[1] // 3
    zs, tok = seg.shape[0], seg.shape[2]
    tall = lambda w: pl.BlockSpec((tok, w), lambda b: (b, 0))
    fixed = lambda x: pl.BlockSpec(x.shape, lambda b: (0, 0))
    thin = jax.ShapeDtypeStruct((total, cols), BF16)
    return pl.pallas_call(
        functools.partial(attend_kernel, HEAD_DIM ** (-0.5)),
        grid=(zs,),
        in_specs=[
            tall(qkv.shape[1]),
            pl.BlockSpec((1, 2, tok), lambda b: (b, 0, 0)),
            fixed(gains),
            tall(HEAD_DIM),
            tall(HEAD_DIM),
            pl.BlockSpec((1, 1, tok), lambda b: (b, 0, 0)),
        ],
        out_specs=[tall(cols)] * 4,
        out_shape=[thin] * 4,
        compiler_params=pltpu.CompilerParams(vmem_limit_bytes=VMEM),
        cost_estimate=COST,
        name="attend",
    )(qkv, r, gains, cos, sin, seg)


def attend_back_kernel(
    scale, dhb, wo, q, k, qr, kr, vb, gains, cos, sin, seg, dq_out, dk_out, dv_out, sums
):
    cols = wo.shape[0]
    seg_row = seg[0]
    same = per_row(seg_row) == seg_row
    do_all = mm(dhb[...], wo[...], ((1,), (1,))).astype(BF16)
    sum_q = sum_k = 0.0
    for h in range(cols // HEAD_DIM):
        at = slice(h * HEAD_DIM, (h + 1) * HEAD_DIM)
        do = do_all[:, at]
        p = softmax_rows(qr[:, at], kr[:, at], same, scale)
        dp = mm(do, vb[:, at], ((1,), (1,)))
        ds = (p * (dp - jnp.sum(p * dp, axis=1, keepdims=True))).astype(BF16)
        dv_out[:, at] = mm(p.astype(BF16), do, ((0,), (0,))).astype(BF16)
        dq = turn(mm(ds, kr[:, at], ((1,), (0,))) * scale, cos[...], -sin[...])
        dk = turn(mm(ds, qr[:, at], ((0,), (0,))) * scale, cos[...], -sin[...])
        dq_out[:, at] = dq
        dk_out[:, at] = dk
        sum_q = sum_q + jnp.sum(q[:, at] * gains[0:1, at] * dq, axis=1, keepdims=True)
        sum_k = sum_k + jnp.sum(k[:, at] * gains[1:2, at] * dk, axis=1, keepdims=True)
    tok = dhb.shape[0]
    sums[0, 0:1, :] = jnp.broadcast_to(sum_q, (tok, tok)).T[0:1, :]
    sums[0, 1:2, :] = jnp.broadcast_to(sum_k, (tok, tok)).T[0:1, :]


def attend_back(dhb, wo, qkv, qr, kr, vb, gains, cos, sin, seg):
    total, cols = qkv.shape[0], wo.shape[0]
    zs, tok = seg.shape[0], seg.shape[2]
    tall = lambda w, at=0: pl.BlockSpec((tok, w), lambda b: (b, at))
    fixed = lambda x: pl.BlockSpec(x.shape, lambda b: (0, 0))
    wide = jax.ShapeDtypeStruct((total, cols), F32)
    return pl.pallas_call(
        functools.partial(attend_back_kernel, HEAD_DIM ** (-0.5)),
        grid=(zs,),
        in_specs=[
            tall(dhb.shape[1]),
            fixed(wo),
            tall(cols, 0),
            tall(cols, 1),
            tall(cols),
            tall(cols),
            tall(cols),
            fixed(gains),
            tall(HEAD_DIM),
            tall(HEAD_DIM),
            pl.BlockSpec((1, 1, tok), lambda b: (b, 0, 0)),
        ],
        out_specs=[tall(cols)] * 3 + [pl.BlockSpec((1, 2, tok), lambda b: (b, 0, 0))],
        out_shape=[
            wide,
            wide,
            jax.ShapeDtypeStruct((total, cols), BF16),
            jax.ShapeDtypeStruct((zs, 2, tok), F32),
        ],
        compiler_params=pltpu.CompilerParams(vmem_limit_bytes=VMEM),
        cost_estimate=COST,
        name="attend_back",
    )(dhb, wo, qkv, qkv, qr, kr, vb, gains, cos, sin, seg)


def join_back_kernel(q, k, dqn, dkn, dv, r, means, gains, out, gain_out):
    cols = dv.shape[1]
    for at, v, d in ((0, q, dqn), (1, k, dkn)):
        rr = per_row(r[0, at : at + 1, :])
        mean = per_row(means[0, at : at + 1, :])
        part = []
        for h in range(cols // HEAD_DIM):
            to = slice(h * HEAD_DIM, (h + 1) * HEAD_DIM)
            vr = v[:, to] * rr
            out[:, at * cols + h * HEAD_DIM : at * cols + (h + 1) * HEAD_DIM] = (
                rr * (gains[at : at + 1, to] * d[:, to]) - vr * (rr * rr) * mean
            ).astype(BF16)
            part.append(jnp.sum(d[:, to] * vr, axis=0, keepdims=True))
        row = jnp.concatenate(part, axis=1)

        @pl.when(pl.program_id(0) == 0)
        def _():
            gain_out[at : at + 1, :] = row

        @pl.when(pl.program_id(0) > 0)
        def _():
            gain_out[at : at + 1, :] += row

    out[:, 2 * cols :] = dv[...]


def join_back(qkv, dqn, dkn, dv, r, means, gains):
    total, cols = dv.shape
    zs, tok = r.shape[0], r.shape[2]
    tall = lambda w, at=0: pl.BlockSpec((tok, w), lambda b: (b, at))
    row = pl.BlockSpec((1, 2, tok), lambda b: (b, 0, 0))
    return pl.pallas_call(
        join_back_kernel,
        grid=(zs,),
        in_specs=[tall(cols, 0), tall(cols, 1), tall(cols), tall(cols), tall(cols), row, row]
        + [pl.BlockSpec(gains.shape, lambda b: (0, 0))],
        out_specs=[tall(3 * cols), pl.BlockSpec((2, cols), lambda b: (0, 0))],
        out_shape=[
            jax.ShapeDtypeStruct((total, 3 * cols), BF16),
            jax.ShapeDtypeStruct((2, cols), F32),
        ],
        compiler_params=pltpu.CompilerParams(vmem_limit_bytes=VMEM),
        cost_estimate=COST,
        name="join_back",
    )(qkv, qkv, dqn, dkn, dv, r, means, gains)


def first_back_kernel(d, w, x, r, da, gain):
    back = mm(d[...], w[...], ((1,), (1,)))
    da[...] = back.astype(BF16)
    row = jnp.sum(back * (x[...].astype(F32) * r[...]), axis=0, keepdims=True)

    @pl.when(pl.program_id(0) == 0)
    def _():
        gain[...] = row

    @pl.when(pl.program_id(0) > 0)
    def _():
        gain[...] += row


def first_back(d, w, x, r, tok):
    total, width = x.shape
    k = d.shape[1]
    return pl.pallas_call(
        first_back_kernel,
        grid=(total // tok,),
        in_specs=[
            pl.BlockSpec((tok, k), lambda b: (b, 0)),
            pl.BlockSpec((width, k), lambda b: (0, 0)),
            pl.BlockSpec((tok, width), lambda b: (b, 0)),
            pl.BlockSpec((tok, 1), lambda b: (b, 0)),
        ],
        out_specs=[
            pl.BlockSpec((tok, width), lambda b: (b, 0)),
            pl.BlockSpec((1, width), lambda b: (0, 0)),
        ],
        out_shape=[
            jax.ShapeDtypeStruct((total, width), BF16),
            jax.ShapeDtypeStruct((1, width), F32),
        ],
        compiler_params=pltpu.CompilerParams(vmem_limit_bytes=VMEM),
        cost_estimate=COST,
        name="first_back",
    )(d, w, x, r)


def form_kernel(count, own, *refs):
    ins, (gate_up, down) = refs[:count], refs[count:]
    wide = gate_up.shape[2]
    for o in range(count):

        @pl.when(own[0] == o)
        def _():
            for e in range(count):
                gate_up[:, e, :] = ins[o ^ e][:, :wide].astype(F32)
                down[:, e, :] = ins[o ^ e][:, wide:].astype(F32)


def form(blocks, own):
    rows, k = blocks[0].shape
    count, ff, tile = len(blocks), k // 3, 32
    return pl.pallas_call(
        functools.partial(form_kernel, count),
        grid_spec=pltpu.PrefetchScalarGridSpec(
            num_scalar_prefetch=1,
            grid=(rows // tile,),
            in_specs=[pl.BlockSpec((tile, k), lambda i, o: (i, 0))] * count,
            out_specs=[
                pl.BlockSpec((tile, count, 2 * ff), lambda i, o: (i, 0, 0)),
                pl.BlockSpec((tile, count, ff), lambda i, o: (i, 0, 0)),
            ],
        ),
        out_shape=[
            jax.ShapeDtypeStruct((rows, count, 2 * ff), F32),
            jax.ShapeDtypeStruct((rows, count, ff), F32),
        ],
        compiler_params=pltpu.CompilerParams(vmem_limit_bytes=VMEM),
        cost_estimate=COST,
        name="form",
    )(own, *blocks)


def inv_rms(v):
    return lax.rsqrt(jnp.mean(v * v, axis=-1, keepdims=True) + EPSILON)


def rms_back(v, r, gain, c):
    gc = gain * c
    return r * gc - v * (r * r * r) * jnp.mean(v * gc, axis=-1, keepdims=True)


def places_and_tables(at, dp, zs, rows):
    dealt = lax.dynamic_slice_in_dim(at[ORDER], dp * zs * SEQ_DEV, zs * SEQ_DEV)
    lens = jnp.take(at[LENGTHS], dealt).reshape(zs, SEQ_DEV)
    ends = jnp.cumsum(lens, axis=1)
    places = jnp.arange(rows, dtype=jnp.int32)
    segment = jnp.sum((places[None, :, None] >= ends[:, None, :]).astype(jnp.int32), axis=2)
    starts = ends - lens
    offset = jnp.sum(
        jnp.where(
            segment[:, :, None] == jnp.arange(SEQ_DEV, dtype=jnp.int32), starts[:, None, :], 0
        ),
        axis=2,
    )
    half = HEAD_DIM // 2
    inverse = ROPE_BASE ** (-2.0 * jnp.arange(half, dtype=F32) / HEAD_DIM)
    turned = (places[None] - offset).astype(F32)[..., None] * inverse
    at[COS] = jnp.tile(jnp.cos(turned), (1, 1, 2)).reshape(zs * rows, HEAD_DIM)
    sin = jnp.sin(turned)
    at[SIN] = jnp.concatenate([-sin, sin], axis=2).reshape(zs * rows, HEAD_DIM)
    at[SEG] = segment.astype(F32)[:, None, :]


def on_device(
    tokens,
    lengths,
    permutation,
    routes,
    norm_gains,
    w_qkv,
    w_out,
    router,
    w_gate_up,
    w_down,
    cotangent,
):
    rows, width = tokens.shape
    zs = lax.axis_size("expert")
    dps = lax.axis_size("dp")
    z = lax.axis_index("expert")
    dp = lax.axis_index("dp")
    local = w_gate_up.shape[1]
    ff = w_down.shape[2]
    experts = router.shape[1]
    own_rows = w_qkv.shape[0]
    e_rows = w_gate_up.shape[0]
    cols = width // zs
    expert = z * local + lax.rem(dp, local)
    own = lax.rem(dp, local)
    top = local // 2
    far_bit = dps // 2
    mid = zs // 2
    laid_out = local == 4 and dps == 8
    me_at = jnp.reshape(dp, (1,)).astype(jnp.int32)
    expert_at = jnp.stack([expert, dp, jnp.int32(experts)]).astype(jnp.int32)
    at = Flow()

    extra = jnp.concatenate(
        [router, norm_gains, jnp.zeros((own_rows, EXTRA - experts - 4), BF16)], axis=1
    )
    sent = jnp.stack(
        [
            jnp.concatenate(
                [w_qkv[:, i * width + e * cols : i * width + (e + 1) * cols] for i in range(3)]
                + [extra],
                axis=1,
            )
            for e in range(zs)
        ]
    )
    at[MINE] = lax.all_to_all(sent, "expert", split_axis=0, concat_axis=0, tiled=True)
    moved = [(b, (b % dps) * zs + b // dps) for b in range(dps * zs)]

    for e in range(local):
        at[W, 0, e] = jnp.concatenate(
            [pick(w_gate_up, own ^ e, 1), pick(w_down, own ^ e, 1)], axis=1
        )
    at[X, 0] = tokens
    at[OUT] = w_out
    at.fence(MINE, (X, 0), OUT, *at.having(W))

    at[ATTN] = lax.all_gather(
        at[MINE].reshape(zs * own_rows, 3 * cols + EXTRA), "dp", axis=0, tiled=True
    )
    if laid_out:
        at[W, 1, 0] = flip(at[W, 0, 1], 1)
        at[W, 1, 2] = flip(at[W, 0, 3], 1)
    at[LENGTHS], at[ORDER], at[ROUTES], at[COT] = lengths, permutation, routes, cotangent
    for i in range(1, zs):
        at[X, i] = hop(at[X, i - 1])
        if i == 1:
            at.fence((X, 1), LENGTHS, ORDER, ROUTES, COT, OUT)
            places_and_tables(at, dp, zs, rows)
        elif i == 2:
            at.fence((X, 2), COS, SIN, SEG, ROUTES, COT)
            at[MASK] = jnp.sum(
                (at[ROUTES][:, :, None] == jnp.arange(experts, dtype=jnp.int32)).astype(BF16),
                axis=1,
            )
            mask_pad = jnp.concatenate(
                [at[MASK], jnp.zeros((rows, EXTRA - experts), BF16)], axis=1
            )
            at[G, 0] = jnp.concatenate([at[COT], mask_pad], axis=1)
            at[OUT] = lax.ppermute(at[OUT], ("dp", "expert"), moved)
        else:
            at.fence((X, i))
    xs = [(X, i) for i in range(zs)]
    at.fence(ATTN, OUT, (G, 0), MASK, *xs, *at.having(W))

    cut = e_rows // 4
    if laid_out:
        at[W, 2, 0] = flip(at[W, 0, 2], 2)
        at[W, 4, 0] = flip(at[W, 0, 0], 4)
    at[G, 1] = hop(at[G, 0])
    out_w = lax.all_gather(at[OUT], "dp", axis=0, tiled=True)
    attn_w = at[ATTN]
    qkv_w = attn_w[:, : 3 * cols]
    router_full = attn_w[:, 3 * cols : 3 * cols + experts]
    gains = attn_w[:, 3 * cols + experts : 3 * cols + experts + 4].astype(F32).T
    router_t = router_full.T
    x_all = by_line([at[key] for key in xs])
    xf = x_all.astype(F32)
    r_attn = inv_rms(xf)
    a_all = (xf * r_attn * gains[0]).astype(BF16)
    at[QKV] = nn(a_all, qkv_w)
    at.fence(QKV, (G, 1))
    qkv = at[QKV]
    q, k = qkv[:, :cols], qkv[:, cols : 2 * cols]
    at[SQUARES] = lax.psum(
        jnp.stack([jnp.sum(q * q, axis=1), jnp.sum(k * k, axis=1)]), "expert"
    )
    at.fence(SQUARES, (G, 1))
    at[G, 2] = hop(at[G, 1])
    by_block = lambda v: v.reshape(2, zs, rows).transpose(1, 0, 2)
    r_qk = by_block(lax.rsqrt(at[SQUARES] / width + EPSILON))
    gain_qk = lax.dynamic_slice_in_dim(gains[1:3], z * cols, cols, axis=1)
    cos, sin, seg = at[COS], at[SIN], at[SEG]
    qr, kr, vb, o = attend(qkv, r_qk, gain_qk, cos, sin, seg)
    at[ADDED] = nn(o, out_w, BF16)
    at.fence(ADDED, (G, 2), *(w for w in at.having(W) if laid_out))
    at[ADDED] = lax.psum_scatter(at[ADDED], "expert", scatter_dimension=0, tiled=True)
    for i in range(3, zs):
        at[G, i] = hop(at[G, i - 1])
    if laid_out:
        at[W, 3, 0] = flip(at[W, 1, 2], 2)
        at[W, 5, 0] = flip(at[W, 1, 0], 4)
        at[WA, 6] = flip(at[W, 2, 0][: 2 * cut], 4)
    first_g = [(G, i) for i in range(mid)]
    last_g = [(G, i) for i in range(mid, zs)]
    at[FAR_GA] = flip(jnp.concatenate([at[key] for key in first_g], axis=0), top)
    weight_keys = at.having(W) + at.having(WA)
    at.fence(ADDED, FAR_GA, (G, zs - 1), *(w for w in weight_keys if laid_out))
    later = {1: lambda: flip(at[W, 2, 0][2 * cut :], 4)}
    later[2] = lambda: flip(at[W, 3, 0][: 2 * cut], 4)
    later[3] = lambda: flip(at[W, 3, 0][2 * cut :], 4)
    hid = tokens.astype(F32) + at[ADDED].astype(F32)
    r_ffn = inv_rms(hid)
    m = (hid * r_ffn * gains[3]).astype(BF16)

    at[M, 0] = m
    mine_e = (jnp.arange(experts) == expert).astype(F32)

    def chunk_places(kind, parts):
        masks = jnp.concatenate([x[:, width : width + experts] for x in parts], axis=0)
        masks = masks.astype(F32).reshape(-1, rows, experts)
        on = jnp.sum(masks * mine_e, axis=2)
        pos = jnp.where(on > 0, jnp.cumsum(on, axis=1) - 1.0, -1.0).astype(jnp.int32)
        at[kind, 0], at[kind, 1], at[kind, 2] = pos, pos.T, masks.transpose(0, 2, 1)

    waiting = [(G, key) for key in last_g] + [(M, (M, i)) for i in range(zs)]
    for i in range(1, zs):
        at[M, i] = hop(at[M, i - 1])
        kind, key = waiting.pop(0)
        at[FAR, *key] = flip(at[key], top)
        beside = [(FAR, *key)]
        if laid_out:
            at[WB, i] = later[i]()
            beside.append((WB, i))
        if i == 2:
            g_near = [jnp.concatenate([at[key] for key in first_g + last_g], axis=0)]
            near_parts = [x for xs in fan(g_near, top) for x in xs]
            chunk_places(NEAR, near_parts)
        if i == zs - 1:
            beside += at.having(NEAR)
        at.fence((M, i), *beside)
    key = waiting.pop(0)[1]
    at[FAR, *key] = flip(at[key], top)
    g_far = [at[FAR_GA], *[at[FAR, *k] for k in last_g]]
    far_parts = [x for xs in fan(g_far, top) for x in xs]
    chunk_places(DISTANT, far_parts)

    def chunk_gather(kind, blocks, pieces, g_parts):
        parts = [blocks] + fan(pieces, top)[1:]
        flat = [x for xs in parts for x in xs]
        got = gather(flat, g_parts, at[kind, 0], at[kind, 2], router_t, expert_at)
        return parts, got

    def chunk_expert(kind, parts, got):
        heights = [x.shape[0] for xs in parts for x in xs]
        backs, outs = run_expert(*got, at[kind, 1], weights, expert_at, heights, ff)
        back = []
        for xs in parts:
            back.append(backs[: len(xs)])
            backs = backs[len(xs) :]
        return back, (got[0], got[1], *outs)

    ms = [at[M, i] for i in range(zs)]
    near_parts, near_rows = chunk_gather(NEAR, ms, [jnp.concatenate(ms, axis=0)], near_parts)
    for i, v in enumerate(near_rows):
        at[ROWS, i] = v
    at.fence(*at.having(ROWS), *at.having(DISTANT), (FAR, *key))
    while waiting:
        key = waiting.pop(0)[1]
        at[FAR, *key] = flip(at[key], top)
    if laid_out:
        keys = [(W, r, 0) for r in range(6)] + [(WA, 6), (WB, 1), (WB, 2), (WB, 3)]
        weights = [at[key] for key in keys]
    else:
        weights = spread({e: at[W, 0, e] for e in range(local)}, dps)
    near_back, near_outs = chunk_expert(NEAR, near_parts, [at[ROWS, i] for i in range(3)])
    far_ms = [(FAR, M, i) for i in range(zs)]
    at[NEAR_GACT] = near_outs[4]
    at.fence(NEAR_GACT, *far_ms)
    ms = [at[key] for key in far_ms]
    pieces = [jnp.concatenate(ms[:mid], axis=0), jnp.concatenate(ms[mid:], axis=0)]
    far_parts, far_rows = chunk_gather(DISTANT, ms, pieces, far_parts)
    far_back, far_outs = chunk_expert(DISTANT, far_parts, far_rows)
    near_outs = (*near_outs[:4], at[NEAR_GACT])

    quarter = dps // 4
    near_sum = fold(near_back)
    far_sum = fold(far_back)
    chunk_keys = [(C, n) for n in range(10)]
    for key, v in zip(chunk_keys, (*near_outs, *far_outs), strict=True):
        at[key] = v
    for i, v in enumerate(far_sum):
        at[BACKS, i] = v
    at.fence(*at.having(BACKS), *chunk_keys)

    def chunk_grads(first):
        c = [at[key] for key in chunk_keys]
        return grads([c[:5], c[5:]], first, quarter, e_rows)

    last = zs - 1

    unit = e_rows // 16

    def send_part(key, row, start, stop):
        at[PIECE, key, row, start] = flip(at[key][row][start * unit : stop * unit], far_bit)

    def got_row(key, row):
        if not laid_out:
            return flip(at[key][row], far_bit)
        parts = sorted(k for k in at.having(PIECE) if k[1:3] == (key, row))
        return jnp.concatenate([at[k] for k in parts], axis=0)

    at[THERE] = flip(at[BACKS, last], top)
    at[SEND_HIGH] = chunk_grads(3 * quarter)
    at.fence(THERE, SEND_HIGH, *chunk_keys)
    for i in reversed(range(zs)):
        here = near_sum[i].astype(F32) + at[THERE].astype(F32)
        if i < last:
            here = here + at[ACC].astype(F32)
        at[ACC] = here.astype(BF16)
        if not i:
            break
        at[ACC] = hop(at[ACC], -1)
        at[THERE] = flip(at[BACKS, i - 1], top)
        beside = []
        if i == last:
            if laid_out:
                send_part(SEND_HIGH, 0, 0, 8)
            for n, y in enumerate(result(at[C, 9], at[DISTANT, 1], weights, top, me_at)):
                at[Y_PART, n] = y
            beside = [*at.having(Y_PART), *at.having(PIECE)]
        if i == last - 1:
            for n, y in enumerate(result(at[C, 4], at[NEAR, 1], weights, top, me_at)):
                at[NEAR_PART, n] = y
            if laid_out:
                send_part(SEND_HIGH, 0, 8, 16)
            beside = [*at.having(NEAR_PART), *at.having(PIECE)]
        if i == last - 2:
            if laid_out:
                send_part(SEND_HIGH, 1, 0, 8)
            at[SEND_LOW] = chunk_grads(2 * quarter)
            at[Y_FAR] = fold([[at[key]] for key in at.having(Y_PART)])[0]
            at[Y_NEAR] = fold([[at[key]] for key in at.having(NEAR_PART)])[0]
            beside = [SEND_LOW, Y_FAR, Y_NEAR, *at.having(PIECE)]
        at.fence(ACC, THERE, *beside, *chunk_keys)
    dm = at[ACC].astype(F32)
    at[Y_FAR] = flip(at[Y_FAR], top)
    if laid_out:
        send_part(SEND_HIGH, 1, 8, 16)
        send_part(SEND_LOW, 0, 0, 8)

    own_mask = at[MASK].astype(F32)
    own_logits = jnp.where(own_mask > 0, nn(m, router_full), -1e30)
    own_e = jnp.where(
        own_mask > 0, jnp.exp(own_logits - jnp.max(own_logits, axis=1, keepdims=True)), 0.0
    )
    gate_own = own_e / jnp.sum(own_e, axis=1, keepdims=True)
    dgates = dm[:, width : width + experts] + dm[:, width + experts : width + 2 * experts]
    dz = (
        gate_own * (dgates - jnp.sum(gate_own * dgates, axis=1, keepdims=True))
    ).astype(BF16)
    dmt = nt(dz, router_full) + dm[:, :width]
    grad_out = cotangent.astype(F32)
    dh = grad_out + rms_back(hid, r_ffn, gains[3], dmt)
    at[DHB] = lax.all_gather(dh.astype(BF16), "expert", axis=0, tiled=True)
    router_part = tn(m, dz)
    gain_ffn = jnp.sum(dmt * hid * r_ffn, axis=0)
    at[KEEP_HIGH] = chunk_grads(quarter)
    at[KEEP_LOW] = chunk_grads(0)
    at[ROUTER], at[GAIN_FFN] = router_part, gain_ffn
    at.fence(
        DHB, Y_FAR, Y_NEAR, KEEP_LOW, KEEP_HIGH, SEND_LOW, ROUTER, GAIN_FFN, *at.having(PIECE)
    )
    dhb = at[DHB]
    if laid_out:
        send_part(SEND_LOW, 0, 8, 16)
        send_part(SEND_LOW, 1, 0, 10)
    for i in range(quarter):
        at[TAIL, quarter + i, 0] = add(at[KEEP_HIGH][i], got_row(SEND_HIGH, i))
    if laid_out:
        at[TAIL, 0, 2] = flip(at[TAIL, 2, 0], 2)
        at[HALF, 0] = flip(at[TAIL, 3, 0][: 4 * unit], 2)
    y_own = add(at[Y_NEAR], at[Y_FAR])
    at[Y] = lax.psum_scatter(
        by_line([y_own[i * rows : (i + 1) * rows] for i in range(zs)]),
        "expert",
        scatter_dimension=0,
        tiled=True,
    )

    dqn, dkn, dv, sums = attend_back(dhb, out_w, qkv, qr, kr, vb, gain_qk, cos, sin, seg)
    means = lax.psum(sums.reshape(-1, rows), "expert").reshape(zs, 2, rows) / width
    dqkv, gains_qk = join_back(qkv, dqn, dkn, dv, r_qk, means, gain_qk)
    at[DQKV] = dqkv
    at.fence(DQKV, DHB, Y, SEND_LOW, *at.having(PIECE), *at.having(TAIL), *at.having(HALF))
    if laid_out:
        send_part(SEND_LOW, 1, 10, 16)
        at[HALF, 4] = flip(at[TAIL, 3, 0][4 * unit : 11 * unit], 2)

    at[ODD] = attn_grads(a_all, at[DQKV], [], me_at, 1, 2)
    at.fence(ODD, DQKV)
    at[ODD] = flip(at[ODD], 1)
    at[DA], at[GAIN_ATTN] = first_back(at[DQKV], attn_w, x_all, r_attn, rows)
    at.fence(ODD, DQKV, DA, GAIN_ATTN, *at.having(HALF), *at.having(PIECE), *at.having(TAIL))
    if laid_out:
        at[HALF, 11] = flip(at[TAIL, 3, 0][11 * unit :], 2)
    at[DA] = lax.psum_scatter(at[DA], "expert", scatter_dimension=0, tiled=True)
    at[HELD] = add(attn_grads(a_all, at[DQKV], [], me_at, 0, 2), at[ODD])
    at.fence(HELD, DHB, GAIN_ATTN, *at.having(HALF))
    sides = halves(at[HELD], zs * own_rows)
    stage(at, sides, 0)
    out_blocks = tn(o, at[DHB], BF16).reshape(dps, own_rows, width)
    for r in range(dps):
        at[OUT_GRAD, r] = pick(out_blocks, dp ^ r, 0)
    zero = jnp.zeros((2, width), F32)
    gain_rows = jnp.concatenate(
        [
            at[GAIN_ATTN],
            lax.dynamic_update_slice_in_dim(zero, gains_qk, z * cols, 1),
            at[GAIN_FFN][None],
            jnp.zeros((EXTRA - experts - 4, width), F32),
        ],
        axis=0,
    )
    at[BESIDE] = jnp.concatenate([at[ROUTER], gain_rows.T], axis=1).astype(BF16)
    for turn_ in range(1, len(bits_of(2, dps))):
        at.fence(*at.having(SIDE), BESIDE, DA, *at.having(OUT_GRAD))
        sides = unstage(at, sides, turn_ - 1)
        stage(at, sides, turn_)
        if turn_ == 1 and laid_out:
            scatter_step(at, 1)
    at[BESIDE] = lax.psum_scatter(at[BESIDE], "dp", scatter_dimension=0, tiled=True)
    at.fence(*at.having(SIDE), *at.having(OUT_GRAD))
    sides = unstage(at, sides, len(bits_of(2, dps)) - 1)
    at[BACK] = jnp.concatenate([sides[0][0][0], sides[1][0][0]], axis=1)
    at.fence(BACK, KEEP_LOW, *at.having(OUT_GRAD), *at.having(TAIL), *at.having(HALF))
    for i in range(quarter):
        at[TAIL, i, 0] = add(at[KEEP_LOW][i], got_row(SEND_LOW, i))
    if laid_out:
        at[TAIL, 1, 2] = jnp.concatenate([at[HALF, 0], at[HALF, 4], at[HALF, 11]], axis=0)
        for e in (0, 2):
            at[TAIL, 0, e ^ 1] = flip(at[TAIL, 1, e], 1)
    at[BACK] = lax.all_to_all(
        at[BACK].reshape(zs, own_rows, 3 * cols),
        "expert",
        split_axis=0,
        concat_axis=0,
        tiled=True,
    )
    if laid_out:
        blocks = {e: at[TAIL, 0, e] for e in range(local)}
    else:
        blocks = gather_back({k[1]: at[k] for k in at.having(TAIL)}, local, dps)
    at[GU], at[DN] = form([blocks[e] for e in range(local)], jnp.reshape(own, (1,)))
    for bit in bits_of(2 if laid_out else 1, dps):
        scatter_step(at, bit)
    at.fence(BACK, GU, DN, BESIDE, *at.having(OUT_GRAD))
    grad_w_out = lax.ppermute(
        at[OUT_GRAD, 0], ("dp", "expert"), [(b, a) for a, b in moved]
    ).astype(F32)
    back = at[BACK].astype(F32)
    grad_w_qkv = jnp.concatenate(
        [back[e, :, i * cols : (i + 1) * cols] for i in range(3) for e in range(zs)], axis=1
    )
    line = ring(zs)
    place = jnp.asarray([line.index(i) for i in range(zs)], jnp.int32)[z]
    blocks = at[BESIDE].reshape(zs, own_rows, EXTRA)
    extra_sum = pick(blocks, z, 0).astype(F32)
    for i in range(1, zs):
        to = jnp.asarray(line, jnp.int32)[lax.rem(place + i, zs)]
        extra_sum = extra_sum + hop(pick(blocks, to, 0), i).astype(F32)
    grad_router = extra_sum[:, :experts]
    grad_gains = extra_sum[:, experts : experts + 4]
    da = at[DA].astype(F32)

    output = hid + at[Y].astype(F32)
    x_own = tokens.astype(F32)
    grad_tokens = dh + rms_back(x_own, inv_rms(x_own), gains[0], da)
    return (
        output,
        grad_tokens,
        grad_gains,
        grad_w_qkv,
        grad_w_out,
        grad_router,
        at[GU],
        at[DN],
    )


def solution(mesh):
    both = P(("dp", "expert"), None)
    experts = P("dp", "expert", None)
    return jax.shard_map(
        on_device,
        mesh=mesh,
        in_specs=(both, P(), P(), both, both, both, both, both, experts, experts, both),
        out_specs=(both, both, both, both, both, both, experts, experts),
        check_vma=False,
    )
```

```python
import functools

import jax
import jax.numpy as jnp
from jax import lax
from jax.experimental import pallas as pl
from jax.experimental.pallas import tpu as pltpu
from jax.sharding import PartitionSpec as P

HEADS = 16
HEAD_DIM = 128
SEQ_DEV = 2
EPSILON = 1e-06
ROPE_BASE = 50000.0
CAP = 80
EXTRA = 128
VMEM = 56 * 2**20
COST = pl.CostEstimate(flops=10**6, bytes_accessed=10**5, transcendentals=0)

F32 = jnp.float32
BF16 = jnp.bfloat16


def dot(a, b, dims, out=F32):
    return lax.dot_general(a, b, (dims, ((), ())), preferred_element_type=F32).astype(out)


def nn(a, b, out=F32):
    return dot(a, b, ((1,), (0,)), out)


def nt(a, b, out=F32):
    return dot(a, b, ((1,), (1,)), out)


def tn(a, b, out=F32):
    return dot(a, b, ((0,), (0,)), out)


def flip(v, bit):
    return lax.ppermute(v, "dp", [(i, i ^ bit) for i in range(lax.axis_size("dp"))])


def ring(n):
    return [*range(0, n, 2), *reversed(range(1, n, 2))]


def hop(v, step=1):
    order = ring(lax.axis_size("expert"))
    n = len(order)
    pairs = [(order[i], order[(i + step) % n]) for i in range(n)]
    return lax.ppermute(v, "expert", pairs)


def gather_ring(v):
    return [v] + [hop(v, i) for i in range(1, lax.axis_size("expert"))]


def places_in_ring():
    n = lax.axis_size("expert")
    at = [ring(n).index(i) for i in range(n)]
    at = jnp.asarray(at, jnp.int32)
    return lax.rem(at[lax.axis_index("expert")] - at + n, n)


def by_line(blocks):
    where = places_in_ring()
    stacked = jnp.stack(blocks)
    return jnp.concatenate([pick(stacked, where[i], 0) for i in range(len(blocks))], axis=0)


def bits_of(low, high):
    out = []
    while low < high:
        out.append(low)
        low *= 2
    return out


def pick(v, index, axis):
    return lax.dynamic_index_in_dim(v, index, axis, keepdims=False)


def tie(*values):
    return lax.optimization_barrier(values)


(
    ORDER,
    LENGTHS,
    COS,
    SIN,
    SEG,
    MINE,
    W,
    X,
    OUT,
    ATTN,
    ROUTES,
    COT,
    MASK,
    G,
    QKV,
    SQUARES,
    ADDED,
    WA,
    FAR_GA,
    WB,
    M,
    NEAR_GACT,
    C,
    FAR,
    THERE,
    SEND_HIGH,
    ACC,
    Y_PART,
    NEAR_PART,
    SEND_LOW,
    Y_FAR,
    Y_NEAR,
    DHB,
    KEEP_HIGH,
    KEEP_LOW,
    ROUTER,
    GAIN_FFN,
    TAIL,
    Y,
    DQKV,
    ODD,
    DA,
    GAIN_ATTN,
    HELD,
    OUT_GRAD,
    BESIDE,
    SIDE,
    BACK,
    GU,
    DN,
    NEAR,
    DISTANT,
    PIECE,
    BACKS,
    ROWS,
    HALF,
    SMALL,
) = range(57)


class Flow:
    def __init__(self):
        self.of = {}

    def fence(self, *keys):
        out = tie(*[self.of[key] for key in keys])
        for key, v in zip(keys, out, strict=True):
            self.of[key] = v

    def __getitem__(self, key):
        return self.of[key]

    def __setitem__(self, key, value):
        self.of[key] = value

    def having(self, kind):
        return [key for key in self.of if isinstance(key, tuple) and key[0] == kind]


def fan(pieces, low):
    out = [list(pieces)]
    for bit in bits_of(1, low):
        out = out + [[flip(x, bit) for x in xs] for xs in out]
    return out


def add(a, b):
    return (a.astype(F32) + b.astype(F32)).astype(BF16)


def match(pieces, like):
    if len(pieces) == len(like):
        return pieces
    step = like[0].shape[0]
    return [x[i : i + step] for x in pieces for i in range(0, x.shape[0], step)]


def fold(parts):
    parts = list(parts)
    while len(parts) > 1:
        half = len(parts) // 2
        for i in range(half):
            got = match([flip(x, half) for x in reversed(parts[half + i])][::-1], parts[i])
            parts[i] = [add(a, b) for a, b in zip(parts[i], got, strict=True)]
        parts = parts[:half]
    return parts[0]


def scatter_step(at, kind, bit):
    keys = sorted(key for key in at.having(kind) if key[1] & bit)
    v = [at.of.pop(key) for key in keys]
    got = flip(jnp.concatenate(v, axis=0) if len(v) > 1 else v[0], bit)
    rows = v[0].shape[0]
    for i, (_, r) in enumerate(keys):
        at[kind, r ^ bit] = add(at[kind, r ^ bit], got[i * rows : (i + 1) * rows])


def blocks_of(parts, tok):
    return [(i, at) for i, p in enumerate(parts) for at in range(0, p.shape[0], tok)]


def onehot_back(pos_t, b):
    slot = lax.broadcasted_iota(jnp.int32, (pos_t.shape[0], CAP), 1)
    return (slot == pos_t[:, b : b + 1]).astype(BF16)


def onehot(pos_ref, b):
    slot = lax.broadcasted_iota(jnp.int32, (CAP, pos_ref.shape[1]), 0)
    return slot == pos_ref[b : b + 1, :]


def mm(a, b, dims):
    return lax.dot_general(a, b, (dims, ((), ())), preferred_element_type=F32)


def to_distance(ref, rows, value, me):
    n = lax.axis_size("dp")
    wide = value.shape[1] // n
    for c in range(n):
        at = pl.multiple_of((me ^ c) * wide, wide)
        ref[rows, pl.ds(at, wide)] = value[:, c * wide : (c + 1) * wide]


def gather_kernel(count, expert, *refs):
    parts, (pos, named, router, rows_out, gate) = refs[:count], refs[count:]
    tok = pos.shape[1]
    for b, (i, first) in enumerate(blocks_of(parts, tok)):
        at = slice(b * CAP, (b + 1) * CAP)
        part = parts[i][first : first + tok, :]
        hot = onehot(pos, b)
        found = mm(hot.astype(BF16), part, ((1,), (0,))).astype(BF16)
        to_distance(rows_out, at, found, expert[1])
        chosen = named[b] > 0
        logits = jnp.where(chosen, mm(router[...], part, ((1,), (1,))), -1e30)
        e = jnp.where(chosen, jnp.exp(logits - jnp.max(logits, axis=0, keepdims=True)), 0.0)
        gates = e / jnp.sum(e, axis=0, keepdims=True)
        mine = lax.broadcasted_iota(jnp.int32, gates.shape, 0) == expert[0]
        row = jnp.sum(jnp.where(mine, gates, 0.0), axis=0, keepdims=True)
        gate[at, :] = jnp.sum(jnp.where(hot, row, 0.0), axis=1, keepdims=True)


def gather_cot_kernel(count, expert, *refs):
    parts, (pos, rows_out) = refs[:count], refs[count:]
    tok = pos.shape[1]
    width = rows_out.shape[1]
    for b, (i, first) in enumerate(blocks_of(parts, tok)):
        part = parts[i][first : first + tok, :width]
        found = mm(onehot(pos, b).astype(BF16), part, ((1,), (0,))).astype(BF16)
        to_distance(rows_out, slice(b * CAP, (b + 1) * CAP), found, expert[1])


def pick_rows(kernel, name, parts, others, outs, expert):
    ins = [*parts, *others]
    whole = lambda x: pl.BlockSpec(x.shape, lambda n, e: (0,) * len(x.shape))
    return pl.pallas_call(
        functools.partial(kernel, len(parts)),
        grid_spec=pltpu.PrefetchScalarGridSpec(
            num_scalar_prefetch=1,
            grid=(1,),
            in_specs=[whole(x) for x in ins],
            out_specs=[whole(x) for x in outs],
        ),
        out_shape=outs,
        compiler_params=pltpu.CompilerParams(vmem_limit_bytes=VMEM),
        cost_estimate=COST,
        name=name,
    )(expert, *ins)


def spans(pieces):
    out, at = [], 0
    for p in pieces:
        out.append(slice(at, at + p.shape[0]))
        at += p.shape[0]
    return out


def expert_kernel(count, pieces, expert, *refs):
    rows_in, gs_in, gate, pos_t = refs[:4]
    parts = [refs[4 + i * pieces : 4 + (i + 1) * pieces] for i in range(3)]
    refs = refs[4 + 3 * pieces :]
    backs, refs = refs[:count], refs[count:]
    dg_out, du_out, gact_out, acc, dgate, wg, wu, wd = refs
    n = pl.program_id(0)
    tok = pos_t.shape[0]
    width = rows_in.shape[1]
    for at, a, b, c in zip(spans(parts[0]), *parts, strict=True):
        wg[at, :] = a[...]
        wu[at, :] = b[...]
        wd[at, :] = c[...]

    rows = rows_in[...]
    g = mm(rows, wg[...], ((1,), (0,)))
    u = mm(rows, wu[...], ((1,), (0,)))
    gw = mm(gs_in[...], wd[...], ((1,), (0,)))
    sg = 1.0 / (1.0 + jnp.exp(-g))
    silu = g * sg
    act = (silu * u).astype(BF16).astype(F32)
    part = jnp.sum(act * gw, axis=1, keepdims=True)
    gate_v = gate[...]
    gact_out[...] = (gate_v * act).astype(BF16)
    dact = gate_v * gw
    dg = (dact * u * (sg * (1.0 + g * (1.0 - sg)))).astype(BF16)
    du = (dact * silu).astype(BF16)
    dg_out[...] = dg
    du_out[...] = du
    back = mm(dg, wg[...], ((1,), (1,))) + mm(du, wu[...], ((1,), (1,)))

    @pl.when(n == 0)
    def _():
        acc[...] = back
        dgate[...] = part

    @pl.when(n > 0)
    def _():
        acc[...] += back
        dgate[...] += part

    @pl.when(n == pl.num_programs(0) - 1)
    def _():
        lane = lax.broadcasted_iota(jnp.int32, (CAP, EXTRA), 1)
        for b, (i, first) in enumerate(blocks_of(backs, tok)):
            at = slice(b * CAP, (b + 1) * CAP)
            to = slice(first, first + tok)
            hot = onehot_back(pos_t, b)
            out = backs[i]
            found = mm(hot, acc[at, :].astype(BF16), ((1,), (0,))).astype(BF16)
            to_distance(out, to, found, expert[1])
            d = dgate[at, :]
            hi = d.astype(BF16).astype(F32)
            beside = jnp.where(
                lane == expert[0], hi, jnp.where(lane == expert[2] + expert[0], d - hi, 0.0)
            ).astype(BF16)
            out[to, width:] = mm(hot, beside, ((1,), (0,))).astype(BF16)


def run_expert(rows, gs, gate, pos_t, pieces, expert, heights, ff):
    slots, width = rows.shape
    tile = min(512, ff)
    steps = ff // tile
    whole = lambda x: pl.BlockSpec(x.shape, lambda n, e: (0,) * len(x.shape))
    column = pl.BlockSpec((slots, tile), lambda n, e: (0, n))
    backs = [jax.ShapeDtypeStruct((h, width + EXTRA), BF16) for h in heights]
    thin = jax.ShapeDtypeStruct((slots, ff), BF16)
    outs = pl.pallas_call(
        functools.partial(expert_kernel, len(heights), len(pieces)),
        grid_spec=pltpu.PrefetchScalarGridSpec(
            num_scalar_prefetch=1,
            grid=(steps,),
            in_specs=[whole(x) for x in (rows, gs, gate, pos_t)]
            + [pl.BlockSpec((p.shape[0], tile), lambda n, e: (0, n)) for p in pieces]
            + [pl.BlockSpec((p.shape[0], tile), lambda n, e: (0, steps + n)) for p in pieces]
            + [pl.BlockSpec((p.shape[0], tile), lambda n, e: (0, 2 * steps + n)) for p in pieces],
            out_specs=[whole(x) for x in backs] + [column, column, column],
            scratch_shapes=[pltpu.VMEM((slots, width), F32), pltpu.VMEM((slots, 1), F32)]
            + [pltpu.VMEM((width, tile), BF16)] * 3,
        ),
        out_shape=backs + [thin, thin, thin],
        compiler_params=pltpu.CompilerParams(vmem_limit_bytes=VMEM),
        cost_estimate=COST,
        name="expert",
    )(expert, rows, gs, gate, pos_t, *pieces, *pieces, *pieces)
    return outs[: len(heights)], outs[len(heights) :]


def result_kernel(count, pieces, wide, me, gact, pos_t, *refs):
    parts, outs, wd = refs[:pieces], refs[pieces : pieces + count], refs[-1]
    tok = pos_t.shape[0]
    n = pl.program_id(0)
    blocks = wd.shape[0] // wide // pl.num_programs(0)

    @pl.when(n == 0)
    def _():
        for at, w in zip(spans(parts), parts, strict=True):
            wd[at, :] = w[...]

    step = blocks * wide
    here = wd[pl.ds(pl.multiple_of(n * step, step), step), :]
    y = mm(gact[...], here, ((1,), (1,))).astype(BF16)
    for b, (i, at) in enumerate(blocks_of(outs, tok)):
        part = y[b * CAP : (b + 1) * CAP, :]
        part = mm(onehot_back(pos_t, b), part, ((1,), (0,))).astype(BF16)
        for k in range(blocks):
            to = pl.multiple_of((me[0] ^ (blocks * n + k)) * wide, wide)
            outs[i][at : at + tok, pl.ds(to, wide)] = part[:, k * wide : (k + 1) * wide]


def result(gact, pos_t, pieces, count, me):
    slots, ff = gact.shape
    width = sum(p.shape[0] for p in pieces)
    wide = width // lax.axis_size("dp")
    tile = max(wide, min(512, width))
    last = (pieces[0].shape[1] - ff) // ff
    out = jax.ShapeDtypeStruct((pos_t.shape[1] // count * pos_t.shape[0], width), BF16)
    return pl.pallas_call(
        functools.partial(result_kernel, count, len(pieces), wide),
        grid_spec=pltpu.PrefetchScalarGridSpec(
            num_scalar_prefetch=1,
            grid=(width // tile,),
            in_specs=[
                pl.BlockSpec((slots, ff), lambda n, me: (0, 0)),
                pl.BlockSpec(pos_t.shape, lambda n, me: (0, 0)),
            ]
            + [pl.BlockSpec((p.shape[0], ff), lambda n, me: (0, last)) for p in pieces],
            out_specs=[pl.BlockSpec(out.shape, lambda n, me: (0, 0))] * count,
            scratch_shapes=[pltpu.VMEM((width, ff), BF16)],
        ),
        out_shape=[out] * count,
        compiler_params=pltpu.CompilerParams(vmem_limit_bytes=VMEM),
        cost_estimate=COST,
        name="result",
    )(me, gact, pos_t, *pieces)


def grads_kernel(count, rows, cuts, *refs):
    ins, outs = refs[: 5 * count], list(refs[5 * count :])
    ff = ins[2].shape[1]
    for b, cut in enumerate(cuts):
        at = slice(b * rows, (b + 1) * rows)
        gate = up = down = 0.0
        for c in range(count):
            tall, gs, dg, du, gact = ins[5 * c : 5 * c + 5]
            gate = gate + mm(tall[:, at], dg[...], ((0,), (0,)))
            up = up + mm(tall[:, at], du[...], ((0,), (0,)))
            down = down + mm(gs[:, at], gact[...], ((0,), (0,)))
        for start, stop in zip(cut[:-1], cut[1:], strict=True):
            out = outs.pop(0)
            out[:, :ff] = gate[start:stop].astype(BF16)
            out[:, ff : 2 * ff] = up[start:stop].astype(BF16)
            out[:, 2 * ff :] = down[start:stop].astype(BF16)


def grads(chunks, first, rows, cuts):
    ff = chunks[0][2].shape[1]
    blocks = len(cuts)
    specs, ins = [], []
    for chunk in chunks:
        slots = chunk[0].shape[0]
        tall = pl.BlockSpec((slots, blocks * rows), lambda i: (0, first // blocks))
        flat = pl.BlockSpec((slots, ff), lambda i: (0, 0))
        specs += [tall, tall, flat, flat, flat]
        ins += list(chunk)
    heights = [b - a for cut in cuts for a, b in zip(cut[:-1], cut[1:], strict=True)]
    return pl.pallas_call(
        functools.partial(grads_kernel, len(chunks), rows, cuts),
        grid=(1,),
        in_specs=specs,
        out_specs=[pl.BlockSpec((h, 3 * ff), lambda i: (0, 0)) for h in heights],
        out_shape=[jax.ShapeDtypeStruct((h, 3 * ff), BF16) for h in heights],
        compiler_params=pltpu.CompilerParams(vmem_limit_bytes=VMEM),
        cost_estimate=COST,
        name="grads",
    )(*ins)


def add_pieces_kernel(keep, *refs):
    pieces, out = refs[:-1], refs[-1]
    for at, p in zip(spans(pieces), pieces, strict=True):
        out[at, :] = (keep[at, :].astype(F32) + p[...].astype(F32)).astype(BF16)


def add_pieces(keep, pieces):
    whole = lambda x: pl.BlockSpec(x.shape, lambda i: (0, 0))
    return pl.pallas_call(
        add_pieces_kernel,
        grid=(1,),
        in_specs=[whole(x) for x in (keep, *pieces)],
        out_specs=whole(keep),
        out_shape=jax.ShapeDtypeStruct(keep.shape, BF16),
        compiler_params=pltpu.CompilerParams(vmem_limit_bytes=VMEM),
        cost_estimate=COST,
        name="add_pieces",
    )(keep, *pieces)


def attn_grads_kernel(me, a, d, *rest):
    k = d.shape[1]
    out = rest[-1]
    out[:, :k] = mm(a[...], d[...], ((0,), (0,))).astype(BF16)
    if len(rest) > 1:
        out[:, k:] = rest[0][...]


def attn_grads(a, d, extra, me, first, stride):
    rows, width = a.shape
    n = lax.axis_size("dp")
    tile = width // n
    count = n // stride
    at = lambda i, me: me[0] ^ (first + stride * i)
    k = d.shape[1] + sum(e.shape[1] for e in extra)
    return pl.pallas_call(
        attn_grads_kernel,
        grid_spec=pltpu.PrefetchScalarGridSpec(
            num_scalar_prefetch=1,
            grid=(count,),
            in_specs=[
                pl.BlockSpec((rows, tile), lambda i, me: (0, at(i, me))),
                pl.BlockSpec(d.shape, lambda i, me: (0, 0)),
            ]
            + [pl.BlockSpec((tile, e.shape[1]), lambda i, me: (at(i, me), 0)) for e in extra],
            out_specs=pl.BlockSpec((tile, k), lambda i, me: (i, 0)),
        ),
        out_shape=jax.ShapeDtypeStruct((count * tile, k), BF16),
        compiler_params=pltpu.CompilerParams(vmem_limit_bytes=VMEM),
        cost_estimate=COST,
        name="attn_grads",
    )(me, a, d, *extra)


def halves(held, rows):
    n = lax.axis_size("dp")
    wide = held.shape[1] // 256 * 128
    out = []
    for left, right, order in (
        (0, wide, bits_of(2, n)),
        (wide, held.shape[1], bits_of(2, n)[::-1]),
    ):
        side = {2 * i: held[i * rows : (i + 1) * rows, left:right] for i in range(n // 2)}
        out.append((side, order))
    return out


def stage(at, sides, step):
    for s, (side, order) in enumerate(sides):
        keys = sorted(r for r in side if r & order[step])
        v = [side[r] for r in keys]
        at[SIDE, s] = flip(jnp.concatenate(v, axis=0) if len(v) > 1 else v[0], order[step])


def unstage(at, sides, step):
    out = []
    for s, (side, order) in enumerate(sides):
        bit = order[step]
        keys = sorted(r for r in side if r & bit)
        rows = side[0].shape[0]
        got = at[SIDE, s]
        kept = {r: v for r, v in side.items() if not r & bit}
        for i, r in enumerate(keys):
            kept[r ^ bit] = add(kept[r ^ bit], got[i * rows : (i + 1) * rows])
        out.append((kept, order))
    return out


def spread(first, n):
    local = len(first)
    have = {(0, e): v for e, v in first.items()}
    for bit in bits_of(1, local):
        for key in sorted(key for key in have if key[1] & bit):
            have[(key[0] ^ bit, key[1] ^ bit)] = flip(have.pop(key), bit)
    for bit in bits_of(local, n):
        for key in sorted(have):
            have[(key[0] ^ bit, 0)] = flip(have[key], bit)
    return [have[key] for key in sorted(have)]


def gather_back(held, local, n):
    held = dict(held)
    for bit in reversed(bits_of(local, n // 2)):
        for r in sorted(r for r in held if r & bit):
            held[r ^ bit] = add(held[r ^ bit], flip(held.pop(r), bit))
    have = {(r, 0): v for r, v in held.items()}
    for bit in reversed(bits_of(1, local)):
        for key in sorted(key for key in have if key[0] & bit):
            have[(key[0] ^ bit, key[1] ^ bit)] = flip(have.pop(key), bit)
    return {e: v for (_, e), v in have.items()}


def per_row(row):
    return jnp.broadcast_to(row, (row.shape[1], row.shape[1])).T


def turn(v, cos, sin):
    return v * cos + pltpu.roll(v, v.shape[1] // 2, 1) * sin


def softmax_rows(qr, kr, same, scale):
    s = jnp.where(same, mm(qr, kr, ((1,), (1,))) * scale, -1e30)
    e = jnp.exp(s - jnp.max(s, axis=1, keepdims=True))
    return e / jnp.sum(e, axis=1, keepdims=True)


def attend_kernel(scale, qkv, r, gains, cos, sin, seg, qr_out, kr_out, vb_out, o_out):
    cols = o_out.shape[1]
    rq, rk = per_row(r[0, 0:1, :]), per_row(r[0, 1:2, :])
    seg_row = seg[0]
    same = per_row(seg_row) == seg_row
    for h in range(cols // HEAD_DIM):
        at = slice(h * HEAD_DIM, (h + 1) * HEAD_DIM)
        k_at = slice(cols + h * HEAD_DIM, cols + (h + 1) * HEAD_DIM)
        v_at = slice(2 * cols + h * HEAD_DIM, 2 * cols + (h + 1) * HEAD_DIM)
        qr = turn(qkv[:, at] * rq * gains[0:1, at], cos[...], sin[...]).astype(BF16)
        kr = turn(qkv[:, k_at] * rk * gains[1:2, at], cos[...], sin[...]).astype(BF16)
        vb = qkv[:, v_at].astype(BF16)
        p = softmax_rows(qr, kr, same, scale)
        qr_out[:, at] = qr
        kr_out[:, at] = kr
        vb_out[:, at] = vb
        o_out[:, at] = mm(p.astype(BF16), vb, ((1,), (0,))).astype(BF16)


def attend(qkv, r, gains, cos, sin, seg):
    total, cols = qkv.shape[0], qkv.shape[1] // 3
    zs, tok = seg.shape[0], seg.shape[2]
    tall = lambda w: pl.BlockSpec((tok, w), lambda b: (b, 0))
    fixed = lambda x: pl.BlockSpec(x.shape, lambda b: (0, 0))
    thin = jax.ShapeDtypeStruct((total, cols), BF16)
    return pl.pallas_call(
        functools.partial(attend_kernel, HEAD_DIM ** (-0.5)),
        grid=(zs,),
        in_specs=[
            tall(qkv.shape[1]),
            pl.BlockSpec((1, 2, tok), lambda b: (b, 0, 0)),
            fixed(gains),
            tall(HEAD_DIM),
            tall(HEAD_DIM),
            pl.BlockSpec((1, 1, tok), lambda b: (b, 0, 0)),
        ],
        out_specs=[tall(cols)] * 4,
        out_shape=[thin] * 4,
        compiler_params=pltpu.CompilerParams(vmem_limit_bytes=VMEM),
        cost_estimate=COST,
        name="attend",
    )(qkv, r, gains, cos, sin, seg)


def attend_back_kernel(
    scale, dhb, wo, q, k, qr, kr, vb, gains, cos, sin, seg, dq_out, dk_out, dv_out, sums
):
    cols = wo.shape[0]
    seg_row = seg[0]
    same = per_row(seg_row) == seg_row
    do_all = mm(dhb[...], wo[...], ((1,), (1,))).astype(BF16)
    sum_q = sum_k = 0.0
    for h in range(cols // HEAD_DIM):
        at = slice(h * HEAD_DIM, (h + 1) * HEAD_DIM)
        do = do_all[:, at]
        p = softmax_rows(qr[:, at], kr[:, at], same, scale)
        dp = mm(do, vb[:, at], ((1,), (1,)))
        ds = (p * (dp - jnp.sum(p * dp, axis=1, keepdims=True))).astype(BF16)
        dv_out[:, at] = mm(p.astype(BF16), do, ((0,), (0,))).astype(BF16)
        dq = turn(mm(ds, kr[:, at], ((1,), (0,))) * scale, cos[...], -sin[...])
        dk = turn(mm(ds, qr[:, at], ((0,), (0,))) * scale, cos[...], -sin[...])
        dq_out[:, at] = dq
        dk_out[:, at] = dk
        sum_q = sum_q + jnp.sum(q[:, at] * gains[0:1, at] * dq, axis=1, keepdims=True)
        sum_k = sum_k + jnp.sum(k[:, at] * gains[1:2, at] * dk, axis=1, keepdims=True)
    tok = dhb.shape[0]
    sums[0, 0:1, :] = jnp.broadcast_to(sum_q, (tok, tok)).T[0:1, :]
    sums[0, 1:2, :] = jnp.broadcast_to(sum_k, (tok, tok)).T[0:1, :]


def attend_back(dhb, wo, qkv, qr, kr, vb, gains, cos, sin, seg):
    total, cols = qkv.shape[0], wo.shape[0]
    zs, tok = seg.shape[0], seg.shape[2]
    tall = lambda w, at=0: pl.BlockSpec((tok, w), lambda b: (b, at))
    fixed = lambda x: pl.BlockSpec(x.shape, lambda b: (0, 0))
    wide = jax.ShapeDtypeStruct((total, cols), F32)
    return pl.pallas_call(
        functools.partial(attend_back_kernel, HEAD_DIM ** (-0.5)),
        grid=(zs,),
        in_specs=[
            tall(dhb.shape[1]),
            fixed(wo),
            tall(cols, 0),
            tall(cols, 1),
            tall(cols),
            tall(cols),
            tall(cols),
            fixed(gains),
            tall(HEAD_DIM),
            tall(HEAD_DIM),
            pl.BlockSpec((1, 1, tok), lambda b: (b, 0, 0)),
        ],
        out_specs=[tall(cols)] * 3 + [pl.BlockSpec((1, 2, tok), lambda b: (b, 0, 0))],
        out_shape=[
            wide,
            wide,
            jax.ShapeDtypeStruct((total, cols), BF16),
            jax.ShapeDtypeStruct((zs, 2, tok), F32),
        ],
        compiler_params=pltpu.CompilerParams(vmem_limit_bytes=VMEM),
        cost_estimate=COST,
        name="attend_back",
    )(dhb, wo, qkv, qkv, qr, kr, vb, gains, cos, sin, seg)


def join_back_kernel(q, k, dqn, dkn, dv, r, means, gains, out, gain_out):
    cols = dv.shape[1]
    for at, v, d in ((0, q, dqn), (1, k, dkn)):
        rr = per_row(r[0, at : at + 1, :])
        mean = per_row(means[0, at : at + 1, :])
        part = []
        for h in range(cols // HEAD_DIM):
            to = slice(h * HEAD_DIM, (h + 1) * HEAD_DIM)
            vr = v[:, to] * rr
            out[:, at * cols + h * HEAD_DIM : at * cols + (h + 1) * HEAD_DIM] = (
                rr * (gains[at : at + 1, to] * d[:, to]) - vr * (rr * rr) * mean
            ).astype(BF16)
            part.append(jnp.sum(d[:, to] * vr, axis=0, keepdims=True))
        row = jnp.concatenate(part, axis=1)

        @pl.when(pl.program_id(0) == 0)
        def _():
            gain_out[at : at + 1, :] = row

        @pl.when(pl.program_id(0) > 0)
        def _():
            gain_out[at : at + 1, :] += row

    out[:, 2 * cols :] = dv[...]


def join_back(qkv, dqn, dkn, dv, r, means, gains):
    total, cols = dv.shape
    zs, tok = r.shape[0], r.shape[2]
    tall = lambda w, at=0: pl.BlockSpec((tok, w), lambda b: (b, at))
    row = pl.BlockSpec((1, 2, tok), lambda b: (b, 0, 0))
    return pl.pallas_call(
        join_back_kernel,
        grid=(zs,),
        in_specs=[tall(cols, 0), tall(cols, 1), tall(cols), tall(cols), tall(cols), row, row]
        + [pl.BlockSpec(gains.shape, lambda b: (0, 0))],
        out_specs=[tall(3 * cols), pl.BlockSpec((2, cols), lambda b: (0, 0))],
        out_shape=[
            jax.ShapeDtypeStruct((total, 3 * cols), BF16),
            jax.ShapeDtypeStruct((2, cols), F32),
        ],
        compiler_params=pltpu.CompilerParams(vmem_limit_bytes=VMEM),
        cost_estimate=COST,
        name="join_back",
    )(qkv, qkv, dqn, dkn, dv, r, means, gains)


def first_back_kernel(d, w, x, r, da, gain):
    back = mm(d[...], w[...], ((1,), (1,)))
    da[...] = back.astype(BF16)
    row = jnp.sum(back * (x[...].astype(F32) * r[...]), axis=0, keepdims=True)

    @pl.when(pl.program_id(0) == 0)
    def _():
        gain[...] = row

    @pl.when(pl.program_id(0) > 0)
    def _():
        gain[...] += row


def first_back(d, w, x, r, tok):
    total, width = x.shape
    k = d.shape[1]
    return pl.pallas_call(
        first_back_kernel,
        grid=(total // tok,),
        in_specs=[
            pl.BlockSpec((tok, k), lambda b: (b, 0)),
            pl.BlockSpec((width, k), lambda b: (0, 0)),
            pl.BlockSpec((tok, width), lambda b: (b, 0)),
            pl.BlockSpec((tok, 1), lambda b: (b, 0)),
        ],
        out_specs=[
            pl.BlockSpec((tok, width), lambda b: (b, 0)),
            pl.BlockSpec((1, width), lambda b: (0, 0)),
        ],
        out_shape=[
            jax.ShapeDtypeStruct((total, width), BF16),
            jax.ShapeDtypeStruct((1, width), F32),
        ],
        compiler_params=pltpu.CompilerParams(vmem_limit_bytes=VMEM),
        cost_estimate=COST,
        name="first_back",
    )(d, w, x, r)


def form_kernel(count, own, *refs):
    ins, (gate_up, down) = refs[:count], refs[-2:]
    wide = gate_up.shape[2]
    for o in range(count):

        @pl.when(own[0] == o)
        def _():
            for e in range(count):
                gate_up[:, e, :] = ins[o ^ e][:, :wide].astype(F32)
                down[:, e, :] = ins[o ^ e][:, wide:].astype(F32)


def form(blocks, own, rows, start, stop, before=()):
    k = blocks[0][0].shape[1]
    count, ff, tile = len(blocks), k // 3, 32

    def spec(at):
        return pl.BlockSpec((tile, k), lambda i, o: (i + (start - at) // tile, 0))

    shapes = [
        jax.ShapeDtypeStruct((rows, count, 2 * ff), F32),
        jax.ShapeDtypeStruct((rows, count, ff), F32),
    ]
    outs = [
        pl.BlockSpec((tile, *s.shape[1:]), lambda i, o: (i + start // tile, 0, 0)) for s in shapes
    ]
    return pl.pallas_call(
        functools.partial(form_kernel, count),
        grid_spec=pltpu.PrefetchScalarGridSpec(
            num_scalar_prefetch=1,
            grid=((stop - start) // tile,),
            in_specs=[spec(at) for _, at in blocks]
            + [pl.BlockSpec(memory_space=pl.ANY)] * len(before),
            out_specs=outs,
        ),
        out_shape=shapes,
        input_output_aliases={1 + count + n: n for n in range(len(before))},
        compiler_params=pltpu.CompilerParams(vmem_limit_bytes=VMEM),
        cost_estimate=COST,
        name="form",
    )(own, *[v for v, _ in blocks], *before)


def inv_rms(v):
    return lax.rsqrt(jnp.mean(v * v, axis=-1, keepdims=True) + EPSILON)


def rms_back(v, r, gain, c):
    gc = gain * c
    return r * gc - v * (r * r * r) * jnp.mean(v * gc, axis=-1, keepdims=True)


def places_and_tables(at, dp, zs, rows):
    dealt = lax.dynamic_slice_in_dim(at[ORDER], dp * zs * SEQ_DEV, zs * SEQ_DEV)
    lens = jnp.take(at[LENGTHS], dealt).reshape(zs, SEQ_DEV)
    ends = jnp.cumsum(lens, axis=1)
    places = jnp.arange(rows, dtype=jnp.int32)
    segment = jnp.sum((places[None, :, None] >= ends[:, None, :]).astype(jnp.int32), axis=2)
    starts = ends - lens
    offset = jnp.sum(
        jnp.where(
            segment[:, :, None] == jnp.arange(SEQ_DEV, dtype=jnp.int32), starts[:, None, :], 0
        ),
        axis=2,
    )
    half = HEAD_DIM // 2
    inverse = ROPE_BASE ** (-2.0 * jnp.arange(half, dtype=F32) / HEAD_DIM)
    turned = (places[None] - offset).astype(F32)[..., None] * inverse
    at[COS] = jnp.tile(jnp.cos(turned), (1, 1, 2)).reshape(zs * rows, HEAD_DIM)
    sin = jnp.sin(turned)
    at[SIN] = jnp.concatenate([-sin, sin], axis=2).reshape(zs * rows, HEAD_DIM)
    at[SEG] = segment.astype(F32)[:, None, :]


def on_device(
    tokens,
    lengths,
    permutation,
    routes,
    norm_gains,
    w_qkv,
    w_out,
    router,
    w_gate_up,
    w_down,
    cotangent,
):
    rows, width = tokens.shape
    zs = lax.axis_size("expert")
    dps = lax.axis_size("dp")
    z = lax.axis_index("expert")
    dp = lax.axis_index("dp")
    local = w_gate_up.shape[1]
    ff = w_down.shape[2]
    experts = router.shape[1]
    own_rows = w_qkv.shape[0]
    e_rows = w_gate_up.shape[0]
    cols = width // zs
    expert = z * local + lax.rem(dp, local)
    own = lax.rem(dp, local)
    top = local // 2
    far_bit = dps // 2
    mid = zs // 2
    laid_out = local == 4 and dps == 8
    me_at = jnp.reshape(dp, (1,)).astype(jnp.int32)
    expert_at = jnp.stack([expert, dp, jnp.int32(experts)]).astype(jnp.int32)
    at = Flow()

    extra = jnp.concatenate(
        [router, norm_gains, jnp.zeros((own_rows, EXTRA - experts - 4), BF16)], axis=1
    )
    sent = jnp.stack(
        [
            jnp.concatenate(
                [w_qkv[:, i * width + e * cols : i * width + (e + 1) * cols] for i in range(3)]
                + [extra],
                axis=1,
            )
            for e in range(zs)
        ]
    )
    at[MINE] = lax.all_to_all(sent, "expert", split_axis=0, concat_axis=0, tiled=True)
    moved = [(b, (b % dps) * zs + b // dps) for b in range(dps * zs)]

    for e in range(local):
        at[W, 0, e] = jnp.concatenate(
            [pick(w_gate_up, own ^ e, 1), pick(w_down, own ^ e, 1)], axis=1
        )
    at[X, 0] = tokens
    at[OUT] = w_out
    at.fence(MINE, (X, 0), OUT, *at.having(W))

    at[ATTN] = lax.all_gather(
        at[MINE].reshape(zs * own_rows, 3 * cols + EXTRA), "dp", axis=0, tiled=True
    )
    if laid_out:
        at[W, 1, 0] = flip(at[W, 0, 1], 1)
        at[W, 1, 2] = flip(at[W, 0, 3], 1)
    at[LENGTHS], at[ORDER], at[ROUTES], at[COT] = lengths, permutation, routes, cotangent
    for i in range(1, zs):
        at[X, i] = hop(at[X, i - 1])
        if i == 1:
            at.fence((X, 1), LENGTHS, ORDER, ROUTES, COT, OUT)
            places_and_tables(at, dp, zs, rows)
        elif i == 2:
            at.fence((X, 2), COS, SIN, SEG, ROUTES, COT)
            at[MASK] = jnp.sum(
                (at[ROUTES][:, :, None] == jnp.arange(experts, dtype=jnp.int32)).astype(BF16),
                axis=1,
            )
            mask_pad = jnp.concatenate(
                [at[MASK], jnp.zeros((rows, EXTRA - experts), BF16)], axis=1
            )
            at[G, 0] = jnp.concatenate([at[COT], mask_pad], axis=1)
            at[OUT] = lax.ppermute(at[OUT], ("dp", "expert"), moved)
        else:
            at.fence((X, i))
    xs = [(X, i) for i in range(zs)]
    at.fence(ATTN, OUT, (G, 0), MASK, *xs, *at.having(W))

    cut = e_rows // 4
    if laid_out:
        at[W, 2, 0] = flip(at[W, 0, 2], 2)
        at[W, 4, 0] = flip(at[W, 0, 0], 4)
    at[G, 1] = hop(at[G, 0])
    out_w = lax.all_gather(at[OUT], "dp", axis=0, tiled=True)
    attn_w = at[ATTN]
    qkv_w = attn_w[:, : 3 * cols]
    router_full = attn_w[:, 3 * cols : 3 * cols + experts]
    gains = attn_w[:, 3 * cols + experts : 3 * cols + experts + 4].astype(F32).T
    router_t = router_full.T
    x_all = by_line([at[key] for key in xs])
    xf = x_all.astype(F32)
    r_attn = inv_rms(xf)
    a_all = (xf * r_attn * gains[0]).astype(BF16)
    at[QKV] = nn(a_all, qkv_w)
    at.fence(QKV, (G, 1))
    qkv = at[QKV]
    q, k = qkv[:, :cols], qkv[:, cols : 2 * cols]
    at[SQUARES] = lax.psum(
        jnp.stack([jnp.sum(q * q, axis=1), jnp.sum(k * k, axis=1)]), "expert"
    )
    at.fence(SQUARES, (G, 1))
    at[G, 2] = hop(at[G, 1])
    by_block = lambda v: v.reshape(2, zs, rows).transpose(1, 0, 2)
    r_qk = by_block(lax.rsqrt(at[SQUARES] / width + EPSILON))
    gain_qk = lax.dynamic_slice_in_dim(gains[1:3], z * cols, cols, axis=1)
    cos, sin, seg = at[COS], at[SIN], at[SEG]
    qr, kr, vb, o = attend(qkv, r_qk, gain_qk, cos, sin, seg)
    at[ADDED] = nn(o, out_w, BF16)
    at.fence(ADDED, (G, 2), *(w for w in at.having(W) if laid_out))
    at[ADDED] = lax.psum_scatter(at[ADDED], "expert", scatter_dimension=0, tiled=True)
    for i in range(3, zs):
        at[G, i] = hop(at[G, i - 1])
    if laid_out:
        at[W, 3, 0] = flip(at[W, 1, 2], 2)
        at[W, 5, 0] = flip(at[W, 1, 0], 4)
        at[WA, 6] = flip(at[W, 2, 0][: 11 * cut // 4], 4)
    first_g = [(G, i) for i in range(mid)]
    last_g = [(G, i) for i in range(mid, zs)]
    at[FAR_GA] = flip(jnp.concatenate([at[key] for key in first_g], axis=0), top)
    weight_keys = at.having(W) + at.having(WA)
    at.fence(ADDED, FAR_GA, (G, zs - 1), *(w for w in weight_keys if laid_out))
    marks = (0, 3 * cut // 4, 9 * cut // 4, e_rows)
    hid = tokens.astype(F32) + at[ADDED].astype(F32)
    r_ffn = inv_rms(hid)
    m = (hid * r_ffn * gains[3]).astype(BF16)

    at[M, 0] = m
    mine_e = (jnp.arange(experts) == expert).astype(F32)

    def chunk_places(kind, parts):
        masks = jnp.concatenate([x[:, width : width + experts] for x in parts], axis=0)
        masks = masks.astype(F32).reshape(-1, rows, experts)
        on = jnp.sum(masks * mine_e, axis=2)
        pos = jnp.where(on > 0, jnp.cumsum(on, axis=1) - 1.0, -1.0).astype(jnp.int32)
        at[kind, 0], at[kind, 1], at[kind, 2] = pos, pos.T, masks.transpose(0, 2, 1)
        out = jax.ShapeDtypeStruct((pos.shape[0] * CAP, width), BF16)
        (at[kind, 3],) = pick_rows(gather_cot_kernel, "gather_cot", parts, [pos], [out], expert_at)

    waiting = [(G, key) for key in last_g] + [(M, (M, i)) for i in range(zs)]
    near_cores = [fan([m], top)[1:]]
    for i in range(1, zs):
        at[M, i] = hop(at[M, i - 1])
        kind, key = waiting.pop(0)
        at[FAR, *key] = flip(at[key], top)
        beside = [(FAR, *key)]
        if laid_out:
            at[WB, i] = flip(at[W, 3, 0][marks[i - 1] : marks[i]], 4)
            beside.append((WB, i))
            if i == 1:
                at[WA, 7] = flip(at[W, 2, 0][11 * cut // 4 :], 4)
                beside.append((WA, 7))
        if i == 1:
            g_near = [jnp.concatenate([at[key] for key in first_g + last_g], axis=0)]
            chunk_places(NEAR, [x for xs in fan(g_near, top) for x in xs])
        if i == 2:
            beside += at.having(NEAR)
        if i == zs - 1:
            g_far = [at[FAR_GA], *[at[FAR, *k] for k in last_g]]
            chunk_places(DISTANT, [x for xs in fan(g_far, top) for x in xs])
            beside += at.having(DISTANT)
        at.fence((M, i), *beside)
        near_cores.append(fan([at[M, i]], top)[1:])
    key = waiting.pop(0)[1]
    at[FAR, *key] = flip(at[key], top)

    def chunk_gather(kind, blocks, cores):
        flat = [*blocks, *(x[0] for d in range(top - 1) for x in (c[d] for c in cores))]
        slots = at[kind, 0].shape[0] * CAP
        outs = [
            jax.ShapeDtypeStruct((slots, width), BF16),
            jax.ShapeDtypeStruct((slots, 1), F32),
        ]
        others = [at[kind, 0], at[kind, 2], router_t]
        picked, gate = pick_rows(gather_kernel, "gather", flat, others, outs, expert_at)
        return picked, at[kind, 3], gate

    def chunk_expert(kind, groups, got):
        heights = [h for group in groups for h in group]
        backs, outs = run_expert(*got, at[kind, 1], weights, expert_at, heights, ff)
        back = []
        for group in groups:
            back.append(backs[: len(group)])
            backs = backs[len(group) :]
        return back, (got[0], got[1], *outs)

    ms = [at[M, i] for i in range(zs)]
    near_rows = chunk_gather(NEAR, ms, near_cores)
    for i, v in enumerate(near_rows):
        at[ROWS, i] = v
    at.fence(*at.having(ROWS), (FAR, *key))
    while waiting:
        key = waiting.pop(0)[1]
        at[FAR, *key] = flip(at[key], top)
    if laid_out:
        keys = [(W, r, 0) for r in range(6)] + [(WA, 6), (WA, 7), (WB, 1), (WB, 2), (WB, 3)]
        weights = [at[key] for key in keys]
    else:
        weights = spread({e: at[W, 0, e] for e in range(local)}, dps)
    own_heights = [rows] * zs
    near_back, near_outs = chunk_expert(
        NEAR, [own_heights] + [[zs * rows]] * (top - 1), [at[ROWS, i] for i in range(3)]
    )
    far_ms = [(FAR, M, i) for i in range(zs)]
    at[NEAR_GACT] = near_outs[4]
    at.fence(NEAR_GACT, *far_ms)
    ms = [at[key] for key in far_ms]
    far_rows = chunk_gather(DISTANT, ms, [fan([v], top)[1:] for v in ms])
    far_back, far_outs = chunk_expert(
        DISTANT, [own_heights] + [[mid * rows, (zs - mid) * rows]] * (top - 1), far_rows
    )
    near_outs = (*near_outs[:4], at[NEAR_GACT])

    quarter = dps // 4
    near_sum = fold(near_back)
    far_sum = fold(far_back)
    chunk_keys = [(C, n) for n in range(10)]
    for key, v in zip(chunk_keys, (*near_outs, *far_outs), strict=True):
        at[key] = v
    for i, v in enumerate(far_sum):
        at[BACKS, i] = v
    at.fence(*at.having(BACKS), *chunk_keys)

    halves_cut = [(0, e_rows // 2, e_rows) if laid_out else (0, e_rows)] * quarter

    def chunk_grads(kind, first, cuts):
        c = [at[key] for key in chunk_keys]
        made = list(grads([c[:5], c[5:]], first, e_rows, cuts))
        for row, cut in enumerate(cuts):
            for start in cut[:-1]:
                at[kind, row, start] = made.pop(0)

    def send_part(key, row, start):
        at[PIECE, key, row, start] = flip(at[key, row, start], far_bit)

    def sum_row(keep, key, row):
        starts = sorted(k[2] for k in at.having(key) if k[1] == row)
        if not laid_out:
            send_part(key, row, 0)
        return add_pieces(at[keep, row, 0], [at[PIECE, key, row, start] for start in starts])

    whole_cut = [(0, e_rows)] * quarter
    last = zs - 1

    at[THERE] = flip(at[BACKS, last], top)
    chunk_grads(SEND_HIGH, 3 * quarter, halves_cut)
    at.fence(THERE, *at.having(SEND_HIGH), *chunk_keys)
    half = e_rows // 2
    early = 3 * e_rows // 8
    for i in reversed(range(zs)):
        here = near_sum[i].astype(F32) + at[THERE].astype(F32)
        if i < last:
            here = here + at[ACC].astype(F32)
        at[ACC] = here.astype(BF16)
        if not i:
            break
        at[ACC] = hop(at[ACC], -1)
        at[THERE] = flip(at[BACKS, i - 1], top)
        beside = []
        if i == last:
            if laid_out:
                send_part(SEND_HIGH, 0, 0)
            for n, y in enumerate(result(at[C, 9], at[DISTANT, 1], weights, top, me_at)):
                at[Y_PART, n] = y
            beside = [*at.having(Y_PART), *at.having(PIECE)]
        if i == last - 1:
            for n, y in enumerate(result(at[C, 4], at[NEAR, 1], weights, top, me_at)):
                at[NEAR_PART, n] = y
            if laid_out:
                send_part(SEND_HIGH, 0, half)
            beside = [*at.having(NEAR_PART), *at.having(PIECE)]
        if i == last - 2:
            if laid_out:
                send_part(SEND_HIGH, 1, 0)
            low_cut = halves_cut
            if laid_out:
                low_cut = [halves_cut[0], (0, e_rows - early, e_rows)]
            chunk_grads(SEND_LOW, 2 * quarter, low_cut)
            at[Y_FAR] = fold([[at[key]] for key in at.having(Y_PART)])[0]
            at[Y_NEAR] = fold([[at[key]] for key in at.having(NEAR_PART)])[0]
            beside = [Y_FAR, Y_NEAR, *at.having(SEND_LOW), *at.having(PIECE)]
        at.fence(ACC, THERE, *beside, *chunk_keys)
    dm = at[ACC].astype(F32)
    at[Y_FAR] = flip(at[Y_FAR], top)
    if laid_out:
        send_part(SEND_HIGH, 1, half)
        send_part(SEND_LOW, 0, 0)

    own_mask = at[MASK].astype(F32)
    own_logits = jnp.where(own_mask > 0, nn(m, router_full), -1e30)
    own_e = jnp.where(
        own_mask > 0, jnp.exp(own_logits - jnp.max(own_logits, axis=1, keepdims=True)), 0.0
    )
    gate_own = own_e / jnp.sum(own_e, axis=1, keepdims=True)
    dgates = dm[:, width : width + experts] + dm[:, width + experts : width + 2 * experts]
    dz = (
        gate_own * (dgates - jnp.sum(gate_own * dgates, axis=1, keepdims=True))
    ).astype(BF16)
    dmt = nt(dz, router_full) + dm[:, :width]
    grad_out = cotangent.astype(F32)
    dh = grad_out + rms_back(hid, r_ffn, gains[3], dmt)
    at[DHB] = lax.all_gather(dh.astype(BF16), "expert", axis=0, tiled=True)
    router_part = tn(m, dz)
    gain_ffn = jnp.sum(dmt * hid * r_ffn, axis=0)
    chunk_grads(KEEP_HIGH, quarter, whole_cut)
    if laid_out:
        at[TAIL, quarter, 0] = sum_row(KEEP_HIGH, SEND_HIGH, 0)
    chunk_grads(KEEP_LOW, 0, whole_cut)
    at[ROUTER], at[GAIN_FFN] = router_part, gain_ffn
    tails = at.having(TAIL)
    keeps = at.having(KEEP_LOW) + at.having(KEEP_HIGH) + at.having(SEND_LOW)
    at.fence(DHB, Y_FAR, Y_NEAR, ROUTER, GAIN_FFN, *keeps, *at.having(PIECE), *tails)
    dhb = at[DHB]
    if laid_out:
        at[TAIL, 0, 2] = flip(at[TAIL, 2, 0], 2)
        send_part(SEND_LOW, 0, half)
        send_part(SEND_LOW, 1, 0)
    for i in range(1 if laid_out else 0, quarter):
        at[TAIL, quarter + i, 0] = sum_row(KEEP_HIGH, SEND_HIGH, i)
    y_own = add(at[Y_NEAR], at[Y_FAR])
    at[Y] = lax.psum_scatter(
        by_line([y_own[i * rows : (i + 1) * rows] for i in range(zs)]),
        "expert",
        scatter_dimension=0,
        tiled=True,
    )

    dqn, dkn, dv, sums = attend_back(dhb, out_w, qkv, qr, kr, vb, gain_qk, cos, sin, seg)
    means = lax.psum(sums.reshape(-1, rows), "expert").reshape(zs, 2, rows) / width
    at[OUT_GRAD] = tn(o, dhb, BF16)
    dqkv, gains_qk = join_back(qkv, dqn, dkn, dv, r_qk, means, gain_qk)
    at[DQKV] = dqkv
    at.fence(DQKV, OUT_GRAD, Y, *at.having(PIECE), *at.having(TAIL))
    at[OUT_GRAD] = lax.psum_scatter(at[OUT_GRAD], "dp", scatter_dimension=0, tiled=True)

    at[ODD] = attn_grads(a_all, at[DQKV], [], me_at, 1, 2)
    at.fence(ODD, DQKV, *at.having(TAIL), *at.having(SEND_LOW))
    at[ODD] = flip(at[ODD], 1)
    if laid_out:
        at[HALF, 0] = flip(at[TAIL, 3, 0][:early], 2)
        send_part(SEND_LOW, 1, e_rows - early)
    even = attn_grads(a_all, at[DQKV], [], me_at, 0, 2)
    at[HELD] = add(even, at[ODD])
    at.fence(HELD, DQKV, *at.having(HALF), *at.having(PIECE))
    sides = halves(at[HELD], zs * own_rows)
    stage(at, sides, 0)
    at[DA], at[GAIN_ATTN] = first_back(at[DQKV], attn_w, x_all, r_attn, rows)
    zero = jnp.zeros((2, width), F32)
    gain_rows = jnp.concatenate(
        [
            at[GAIN_ATTN],
            lax.dynamic_update_slice_in_dim(zero, gains_qk, z * cols, 1),
            at[GAIN_FFN][None],
            jnp.zeros((EXTRA - experts - 4, width), F32),
        ],
        axis=0,
    )
    at[BESIDE] = jnp.concatenate([at[ROUTER], gain_rows.T], axis=1).astype(BF16)
    for turn_ in range(1, len(bits_of(2, dps))):
        at.fence(*at.having(SIDE), BESIDE, DA, OUT_GRAD, *at.having(KEEP_LOW), *at.having(PIECE))
        if turn_ == 1:
            at[DA] = lax.psum_scatter(at[DA], "expert", scatter_dimension=0, tiled=True)
            stacked = at[BESIDE].reshape(dps, e_rows, EXTRA)
            for r in range(dps):
                at[SMALL, r] = pick(stacked, dp ^ r, 0)
            scatter_step(at, SMALL, 1)
            for i in range(quarter):
                at[TAIL, i, 0] = sum_row(KEEP_LOW, SEND_LOW, i)
        sides = unstage(at, sides, turn_ - 1)
        stage(at, sides, turn_)
    at.fence(*at.having(SIDE), *at.having(SMALL), *at.having(TAIL))
    sides = unstage(at, sides, len(bits_of(2, dps)) - 1)
    at[BACK] = jnp.concatenate([sides[0][0][0], sides[1][0][0]], axis=1)
    at.fence(BACK, OUT_GRAD, *at.having(SMALL), *at.having(HALF), *at.having(TAIL))
    at[BACK] = lax.all_to_all(
        at[BACK].reshape(zs, own_rows, 3 * cols),
        "expert",
        split_axis=0,
        concat_axis=0,
        tiled=True,
    )
    at[OUT_GRAD] = lax.ppermute(
        at[OUT_GRAD], ("dp", "expert"), [(b, a) for a, b in moved]
    )
    for bit in bits_of(2, dps):
        scatter_step(at, SMALL, bit)
    own_at = jnp.reshape(own, (1,))
    if laid_out:
        at[HALF, early] = flip(at[TAIL, 3, 0][early:], 2)
        at[TAIL, 0, 1] = flip(at[TAIL, 1, 0], 1)
        blocks = [(at[TAIL, 0, e], 0) for e in range(local - 1)]
        at[HALF, 0], at[HALF, early] = flip(at[HALF, 0], 1), flip(at[HALF, early], 1)
        first = form([*blocks, (at[HALF, 0], 0)], own_at, e_rows, 0, early)
        blocks += [(at[HALF, early], early)]
        at[GU], at[DN] = form(blocks, own_at, e_rows, early, e_rows, first)
    else:
        rest = gather_back({k[1]: at[k] for k in at.having(TAIL)}, local, dps)
        at[GU], at[DN] = form([(rest[e], 0) for e in range(local)], own_at, e_rows, 0, e_rows)
    at.fence(BACK, OUT_GRAD, DA, GU, DN, *at.having(SMALL))
    grad_w_out = at[OUT_GRAD].astype(F32)
    back = at[BACK].astype(F32)
    grad_w_qkv = jnp.concatenate(
        [back[e, :, i * cols : (i + 1) * cols] for i in range(3) for e in range(zs)], axis=1
    )
    line = ring(zs)
    place = jnp.asarray([line.index(i) for i in range(zs)], jnp.int32)[z]
    blocks = at[SMALL, 0].reshape(zs, own_rows, EXTRA)
    extra_sum = pick(blocks, z, 0).astype(F32)
    for i in range(1, zs):
        to = jnp.asarray(line, jnp.int32)[lax.rem(place + i, zs)]
        extra_sum = extra_sum + hop(pick(blocks, to, 0), i).astype(F32)
    grad_router = extra_sum[:, :experts]
    grad_gains = extra_sum[:, experts : experts + 4]
    da = at[DA].astype(F32)

    output = hid + at[Y].astype(F32)
    x_own = tokens.astype(F32)
    grad_tokens = dh + rms_back(x_own, inv_rms(x_own), gains[0], da)
    return (
        output,
        grad_tokens,
        grad_gains,
        grad_w_qkv,
        grad_w_out,
        grad_router,
        at[GU],
        at[DN],
    )


def solution(mesh):
    both = P(("dp", "expert"), None)
    experts = P("dp", "expert", None)
    return jax.shard_map(
        on_device,
        mesh=mesh,
        in_specs=(both, P(), P(), both, both, both, both, both, experts, experts, both),
        out_specs=(both, both, both, both, both, both, experts, experts),
        check_vma=False,
    )
```

```python
import functools

import jax
import jax.numpy as jnp
from jax import lax
from jax.experimental import pallas as pl
from jax.experimental.pallas import tpu as pltpu
from jax.sharding import PartitionSpec as P

HEADS = 16
HEAD_DIM = 128
SEQ_DEV = 2
EPSILON = 1e-06
ROPE_BASE = 50000.0
CAP = 80
EXTRA = 128
VMEM = 56 * 2**20
COST = pl.CostEstimate(flops=10**6, bytes_accessed=10**5, transcendentals=0)

F32 = jnp.float32
BF16 = jnp.bfloat16


def dot(a, b, dims, out=F32):
    return lax.dot_general(a, b, (dims, ((), ())), preferred_element_type=F32).astype(out)


def nn(a, b, out=F32):
    return dot(a, b, ((1,), (0,)), out)


def nt(a, b, out=F32):
    return dot(a, b, ((1,), (1,)), out)


def tn(a, b, out=F32):
    return dot(a, b, ((0,), (0,)), out)


def flip(v, bit):
    return lax.ppermute(v, "dp", [(i, i ^ bit) for i in range(lax.axis_size("dp"))])


def ring(n):
    return [*range(0, n, 2), *reversed(range(1, n, 2))]


def hop(v, step=1):
    order = ring(lax.axis_size("expert"))
    n = len(order)
    pairs = [(order[i], order[(i + step) % n]) for i in range(n)]
    return lax.ppermute(v, "expert", pairs)


def gather_ring(v):
    return [v] + [hop(v, i) for i in range(1, lax.axis_size("expert"))]


def place_in_ring(i, n):
    half = i // 2
    return jnp.where(i % 2 == 0, half, n - 1 - half) if not isinstance(i, int) else (
        half if i % 2 == 0 else n - 1 - half
    )


def at_place(p, n):
    return jnp.where(p < (n + 1) // 2, 2 * p, 2 * (n - 1 - p) + 1)


def by_line(blocks):
    n = len(blocks)
    mine = place_in_ring(lax.axis_index("expert"), n)
    stacked = jnp.stack(blocks)
    return jnp.concatenate(
        [pick(stacked, lax.rem(mine - place_in_ring(i, n) + n, n), 0) for i in range(n)], axis=0
    )


def bits_of(low, high):
    out = []
    while low < high:
        out.append(low)
        low *= 2
    return out


def pick(v, index, axis):
    return lax.dynamic_index_in_dim(v, index, axis, keepdims=False)


def tie(*values):
    return lax.optimization_barrier(values)


(
    ORDER,
    LENGTHS,
    COS,
    SIN,
    SEG,
    MINE,
    W,
    X,
    OUT,
    ATTN,
    ROUTES,
    COT,
    MASK,
    G,
    QKV,
    SQUARES,
    ADDED,
    WA,
    FAR_GA,
    WB,
    M,
    NEAR_GACT,
    C,
    FAR,
    THERE,
    SEND_HIGH,
    ACC,
    Y_PART,
    NEAR_PART,
    SEND_LOW,
    Y_FAR,
    Y_NEAR,
    DHB,
    KEEP_HIGH,
    KEEP_LOW,
    ROUTER,
    GAIN_FFN,
    TAIL,
    Y,
    DQKV,
    ODD,
    DA,
    GAIN_ATTN,
    HELD,
    OUT_GRAD,
    BESIDE,
    SIDE,
    BACK,
    GU,
    DN,
    NEAR,
    DISTANT,
    PIECE,
    BACKS,
    ROWS,
    HALF,
    SMALL,
) = range(57)


class Flow:
    def __init__(self):
        self.of = {}

    def fence(self, *keys):
        out = tie(*[self.of[key] for key in keys])
        for key, v in zip(keys, out, strict=True):
            self.of[key] = v

    def __getitem__(self, key):
        return self.of[key]

    def __setitem__(self, key, value):
        self.of[key] = value

    def having(self, kind):
        return [key for key in self.of if isinstance(key, tuple) and key[0] == kind]


def fan(pieces, low):
    out = [list(pieces)]
    for bit in bits_of(1, low):
        out = out + [[flip(x, bit) for x in xs] for xs in out]
    return out


def add(a, b):
    return (a.astype(F32) + b.astype(F32)).astype(BF16)


def match(pieces, like):
    if len(pieces) == len(like):
        return pieces
    step = like[0].shape[0]
    return [x[i : i + step] for x in pieces for i in range(0, x.shape[0], step)]


def fold(parts):
    parts = list(parts)
    while len(parts) > 1:
        half = len(parts) // 2
        for i in range(half):
            got = match([flip(x, half) for x in reversed(parts[half + i])][::-1], parts[i])
            parts[i] = [add(a, b) for a, b in zip(parts[i], got, strict=True)]
        parts = parts[:half]
    return parts[0]


class Halving:
    def __init__(self, at, kind, value):
        self.at, self.kind, self.dp = at, kind, lax.axis_index("dp")
        n = lax.axis_size("dp")
        self.left = bits_of(1, n)[::-1]
        shape = (2,) * len(self.left) + (value.shape[0] // n, value.shape[1])
        at[kind, 0] = value.reshape(shape)

    def begin(self, bit):
        at, axis = self.at, self.left.index(bit)
        mine = lax.rem(self.dp // bit, 2)
        v = at[self.kind, 0]
        at[self.kind, 1] = flip(pick(v, 1 - mine, axis), bit)
        at[self.kind, 0] = pick(v, mine, axis)
        self.left.remove(bit)

    def end(self):
        at = self.at
        at[self.kind, 0] = add(at[self.kind, 0], at.of.pop((self.kind, 1)))


def blocks_of(parts, tok):
    return [(i, at) for i, p in enumerate(parts) for at in range(0, p.shape[0], tok)]


def onehot_back(pos_t, b):
    slot = lax.broadcasted_iota(jnp.int32, (pos_t.shape[0], CAP), 1)
    return (slot == pos_t[:, b : b + 1]).astype(BF16)


def onehot(pos_ref, b):
    slot = lax.broadcasted_iota(jnp.int32, (CAP, pos_ref.shape[1]), 0)
    return slot == pos_ref[b : b + 1, :]


def mm(a, b, dims):
    return lax.dot_general(a, b, (dims, ((), ())), preferred_element_type=F32)


def to_distance(ref, rows, value, me):
    n = lax.axis_size("dp")
    wide = value.shape[1] // n
    for c in range(n):
        at = pl.multiple_of((me ^ c) * wide, wide)
        ref[rows, pl.ds(at, wide)] = value[:, c * wide : (c + 1) * wide]


def gather_kernel(count, expert, *refs):
    parts, (pos, named, router, rows_out, gate) = refs[:count], refs[count:]
    tok = pos.shape[1]
    for b, (i, first) in enumerate(blocks_of(parts, tok)):
        at = slice(b * CAP, (b + 1) * CAP)
        part = parts[i][first : first + tok, :]
        hot = onehot(pos, b)
        found = mm(hot.astype(BF16), part, ((1,), (0,))).astype(BF16)
        to_distance(rows_out, at, found, expert[1])
        chosen = named[b] > 0
        logits = jnp.where(chosen, mm(router[...], part, ((1,), (1,))), -1e30)
        e = jnp.where(chosen, jnp.exp(logits - jnp.max(logits, axis=0, keepdims=True)), 0.0)
        gates = e / jnp.sum(e, axis=0, keepdims=True)
        mine = lax.broadcasted_iota(jnp.int32, gates.shape, 0) == expert[0]
        row = jnp.sum(jnp.where(mine, gates, 0.0), axis=0, keepdims=True)
        gate[at, :] = jnp.sum(jnp.where(hot, row, 0.0), axis=1, keepdims=True)


def gather_cot_kernel(count, expert, *refs):
    parts, (pos, rows_out) = refs[:count], refs[count:]
    tok = pos.shape[1]
    width = rows_out.shape[1]
    for b, (i, first) in enumerate(blocks_of(parts, tok)):
        part = parts[i][first : first + tok, :width]
        found = mm(onehot(pos, b).astype(BF16), part, ((1,), (0,))).astype(BF16)
        to_distance(rows_out, slice(b * CAP, (b + 1) * CAP), found, expert[1])


def pick_rows(kernel, name, parts, others, outs, expert):
    ins = [*parts, *others]
    whole = lambda x: pl.BlockSpec(x.shape, lambda n, e: (0,) * len(x.shape))
    return pl.pallas_call(
        functools.partial(kernel, len(parts)),
        grid_spec=pltpu.PrefetchScalarGridSpec(
            num_scalar_prefetch=1,
            grid=(1,),
            in_specs=[whole(x) for x in ins],
            out_specs=[whole(x) for x in outs],
        ),
        out_shape=outs,
        compiler_params=pltpu.CompilerParams(vmem_limit_bytes=VMEM),
        cost_estimate=COST,
        name=name,
    )(expert, *ins)


def spans(pieces):
    out, at = [], 0
    for p in pieces:
        out.append(slice(at, at + p.shape[0]))
        at += p.shape[0]
    return out


def expert_kernel(count, pieces, expert, *refs):
    rows_in, gs_in, gate, pos_t = refs[:4]
    parts = [refs[4 + i * pieces : 4 + (i + 1) * pieces] for i in range(3)]
    refs = refs[4 + 3 * pieces :]
    backs, refs = refs[:count], refs[count:]
    dg_out, du_out, gact_out, acc, dgate, wg, wu, wd = refs
    n = pl.program_id(0)
    tok = pos_t.shape[0]
    width = rows_in.shape[1]
    for at, a, b, c in zip(spans(parts[0]), *parts, strict=True):
        wg[at, :] = a[...]
        wu[at, :] = b[...]
        wd[at, :] = c[...]

    rows = rows_in[...]
    g = mm(rows, wg[...], ((1,), (0,)))
    u = mm(rows, wu[...], ((1,), (0,)))
    gw = mm(gs_in[...], wd[...], ((1,), (0,)))
    sg = 1.0 / (1.0 + jnp.exp(-g))
    silu = g * sg
    act = (silu * u).astype(BF16).astype(F32)
    part = jnp.sum(act * gw, axis=1, keepdims=True)
    gate_v = gate[...]
    gact_out[...] = (gate_v * act).astype(BF16)
    dact = gate_v * gw
    dg = (dact * u * (sg * (1.0 + g * (1.0 - sg)))).astype(BF16)
    du = (dact * silu).astype(BF16)
    dg_out[...] = dg
    du_out[...] = du
    back = mm(dg, wg[...], ((1,), (1,))) + mm(du, wu[...], ((1,), (1,)))

    @pl.when(n == 0)
    def _():
        acc[...] = back
        dgate[...] = part

    @pl.when(n > 0)
    def _():
        acc[...] += back
        dgate[...] += part

    @pl.when(n == pl.num_programs(0) - 1)
    def _():
        lane = lax.broadcasted_iota(jnp.int32, (CAP, EXTRA), 1)
        for b, (i, first) in enumerate(blocks_of(backs, tok)):
            at = slice(b * CAP, (b + 1) * CAP)
            to = slice(first, first + tok)
            hot = onehot_back(pos_t, b)
            out = backs[i]
            found = mm(hot, acc[at, :].astype(BF16), ((1,), (0,))).astype(BF16)
            to_distance(out, to, found, expert[1])
            d = dgate[at, :]
            hi = d.astype(BF16).astype(F32)
            beside = jnp.where(
                lane == expert[0], hi, jnp.where(lane == expert[2] + expert[0], d - hi, 0.0)
            ).astype(BF16)
            out[to, width:] = mm(hot, beside, ((1,), (0,))).astype(BF16)


def run_expert(rows, gs, gate, pos_t, pieces, expert, heights, ff):
    slots, width = rows.shape
    tile = min(512, ff)
    steps = ff // tile
    whole = lambda x: pl.BlockSpec(x.shape, lambda n, e: (0,) * len(x.shape))
    column = pl.BlockSpec((slots, tile), lambda n, e: (0, n))
    backs = [jax.ShapeDtypeStruct((h, width + EXTRA), BF16) for h in heights]
    thin = jax.ShapeDtypeStruct((slots, ff), BF16)
    outs = pl.pallas_call(
        functools.partial(expert_kernel, len(heights), len(pieces)),
        grid_spec=pltpu.PrefetchScalarGridSpec(
            num_scalar_prefetch=1,
            grid=(steps,),
            in_specs=[whole(x) for x in (rows, gs, gate, pos_t)]
            + [pl.BlockSpec((p.shape[0], tile), lambda n, e: (0, n)) for p in pieces]
            + [pl.BlockSpec((p.shape[0], tile), lambda n, e: (0, steps + n)) for p in pieces]
            + [pl.BlockSpec((p.shape[0], tile), lambda n, e: (0, 2 * steps + n)) for p in pieces],
            out_specs=[whole(x) for x in backs] + [column, column, column],
            scratch_shapes=[pltpu.VMEM((slots, width), F32), pltpu.VMEM((slots, 1), F32)]
            + [pltpu.VMEM((width, tile), BF16)] * 3,
        ),
        out_shape=backs + [thin, thin, thin],
        compiler_params=pltpu.CompilerParams(vmem_limit_bytes=VMEM),
        cost_estimate=COST,
        name="expert",
    )(expert, rows, gs, gate, pos_t, *pieces, *pieces, *pieces)
    return outs[: len(heights)], outs[len(heights) :]


def result_kernel(count, pieces, wide, me, gact, pos_t, *refs):
    parts, outs, wd = refs[:pieces], refs[pieces : pieces + count], refs[-1]
    tok = pos_t.shape[0]
    n = pl.program_id(0)
    blocks = wd.shape[0] // wide // pl.num_programs(0)

    @pl.when(n == 0)
    def _():
        for at, w in zip(spans(parts), parts, strict=True):
            wd[at, :] = w[...]

    step = blocks * wide
    here = wd[pl.ds(pl.multiple_of(n * step, step), step), :]
    y = mm(gact[...], here, ((1,), (1,))).astype(BF16)
    for b, (i, at) in enumerate(blocks_of(outs, tok)):
        part = y[b * CAP : (b + 1) * CAP, :]
        part = mm(onehot_back(pos_t, b), part, ((1,), (0,))).astype(BF16)
        for k in range(blocks):
            to = pl.multiple_of((me[0] ^ (blocks * n + k)) * wide, wide)
            outs[i][at : at + tok, pl.ds(to, wide)] = part[:, k * wide : (k + 1) * wide]


def result(gact, pos_t, pieces, count, me):
    slots, ff = gact.shape
    width = sum(p.shape[0] for p in pieces)
    wide = width // lax.axis_size("dp")
    tile = max(wide, min(512, width))
    last = (pieces[0].shape[1] - ff) // ff
    out = jax.ShapeDtypeStruct((pos_t.shape[1] // count * pos_t.shape[0], width), BF16)
    return pl.pallas_call(
        functools.partial(result_kernel, count, len(pieces), wide),
        grid_spec=pltpu.PrefetchScalarGridSpec(
            num_scalar_prefetch=1,
            grid=(width // tile,),
            in_specs=[
                pl.BlockSpec((slots, ff), lambda n, me: (0, 0)),
                pl.BlockSpec(pos_t.shape, lambda n, me: (0, 0)),
            ]
            + [pl.BlockSpec((p.shape[0], ff), lambda n, me: (0, last)) for p in pieces],
            out_specs=[pl.BlockSpec(out.shape, lambda n, me: (0, 0))] * count,
            scratch_shapes=[pltpu.VMEM((width, ff), BF16)],
        ),
        out_shape=[out] * count,
        compiler_params=pltpu.CompilerParams(vmem_limit_bytes=VMEM),
        cost_estimate=COST,
        name="result",
    )(me, gact, pos_t, *pieces)


def grads_kernel(count, rows, cuts, *refs):
    ins, outs = refs[: 5 * count], list(refs[5 * count :])
    ff = ins[2].shape[1]
    for b, cut in enumerate(cuts):
        at = slice(b * rows, (b + 1) * rows)
        gate = up = down = 0.0
        for c in range(count):
            tall, gs, dg, du, gact = ins[5 * c : 5 * c + 5]
            gate = gate + mm(tall[:, at], dg[...], ((0,), (0,)))
            up = up + mm(tall[:, at], du[...], ((0,), (0,)))
            down = down + mm(gs[:, at], gact[...], ((0,), (0,)))
        for start, stop in zip(cut[:-1], cut[1:], strict=True):
            out = outs.pop(0)
            out[:, :ff] = gate[start:stop].astype(BF16)
            out[:, ff : 2 * ff] = up[start:stop].astype(BF16)
            out[:, 2 * ff :] = down[start:stop].astype(BF16)


def grads(chunks, first, rows, cuts):
    ff = chunks[0][2].shape[1]
    blocks = len(cuts)
    specs, ins = [], []
    for chunk in chunks:
        slots = chunk[0].shape[0]
        tall = pl.BlockSpec((slots, blocks * rows), lambda i: (0, first // blocks))
        flat = pl.BlockSpec((slots, ff), lambda i: (0, 0))
        specs += [tall, tall, flat, flat, flat]
        ins += list(chunk)
    heights = [b - a for cut in cuts for a, b in zip(cut[:-1], cut[1:], strict=True)]
    return pl.pallas_call(
        functools.partial(grads_kernel, len(chunks), rows, cuts),
        grid=(1,),
        in_specs=specs,
        out_specs=[pl.BlockSpec((h, 3 * ff), lambda i: (0, 0)) for h in heights],
        out_shape=[jax.ShapeDtypeStruct((h, 3 * ff), BF16) for h in heights],
        compiler_params=pltpu.CompilerParams(vmem_limit_bytes=VMEM),
        cost_estimate=COST,
        name="grads",
    )(*ins)


def add_pieces_kernel(keep, *refs):
    pieces, out = refs[:-1], refs[-1]
    for at, p in zip(spans(pieces), pieces, strict=True):
        out[at, :] = (keep[at, :].astype(F32) + p[...].astype(F32)).astype(BF16)


def add_pieces(keep, pieces):
    whole = lambda x: pl.BlockSpec(x.shape, lambda i: (0, 0))
    return pl.pallas_call(
        add_pieces_kernel,
        grid=(1,),
        in_specs=[whole(x) for x in (keep, *pieces)],
        out_specs=whole(keep),
        out_shape=jax.ShapeDtypeStruct(keep.shape, BF16),
        compiler_params=pltpu.CompilerParams(vmem_limit_bytes=VMEM),
        cost_estimate=COST,
        name="add_pieces",
    )(keep, *pieces)


def attn_grads_kernel(me, a, d, *rest):
    k = d.shape[1]
    out = rest[-1]
    out[:, :k] = mm(a[...], d[...], ((0,), (0,))).astype(BF16)
    if len(rest) > 1:
        out[:, k:] = rest[0][...]


def attn_grads(a, d, extra, me, first, stride):
    rows, width = a.shape
    n = lax.axis_size("dp")
    tile = width // n
    count = n // stride
    at = lambda i, me: me[0] ^ (first + stride * i)
    k = d.shape[1] + sum(e.shape[1] for e in extra)
    return pl.pallas_call(
        attn_grads_kernel,
        grid_spec=pltpu.PrefetchScalarGridSpec(
            num_scalar_prefetch=1,
            grid=(count,),
            in_specs=[
                pl.BlockSpec((rows, tile), lambda i, me: (0, at(i, me))),
                pl.BlockSpec(d.shape, lambda i, me: (0, 0)),
            ]
            + [pl.BlockSpec((tile, e.shape[1]), lambda i, me: (at(i, me), 0)) for e in extra],
            out_specs=pl.BlockSpec((tile, k), lambda i, me: (i, 0)),
        ),
        out_shape=jax.ShapeDtypeStruct((count * tile, k), BF16),
        compiler_params=pltpu.CompilerParams(vmem_limit_bytes=VMEM),
        cost_estimate=COST,
        name="attn_grads",
    )(me, a, d, *extra)


def halves(held, rows):
    n = lax.axis_size("dp")
    wide = held.shape[1] // 256 * 128
    out = []
    for left, right, order in (
        (0, wide, bits_of(2, n)),
        (wide, held.shape[1], bits_of(2, n)[::-1]),
    ):
        side = {2 * i: held[i * rows : (i + 1) * rows, left:right] for i in range(n // 2)}
        out.append((side, order))
    return out


def stage(at, sides, step):
    for s, (side, order) in enumerate(sides):
        keys = sorted(r for r in side if r & order[step])
        v = [side[r] for r in keys]
        at[SIDE, s] = flip(jnp.concatenate(v, axis=0) if len(v) > 1 else v[0], order[step])


def unstage(at, sides, step):
    out = []
    for s, (side, order) in enumerate(sides):
        bit = order[step]
        keys = sorted(r for r in side if r & bit)
        rows = side[0].shape[0]
        got = at[SIDE, s]
        kept = {r: v for r, v in side.items() if not r & bit}
        for i, r in enumerate(keys):
            kept[r ^ bit] = add(kept[r ^ bit], got[i * rows : (i + 1) * rows])
        out.append((kept, order))
    return out


def spread(first, n):
    local = len(first)
    have = {(0, e): v for e, v in first.items()}
    for bit in bits_of(1, local):
        for key in sorted(key for key in have if key[1] & bit):
            have[(key[0] ^ bit, key[1] ^ bit)] = flip(have.pop(key), bit)
    for bit in bits_of(local, n):
        for key in sorted(have):
            have[(key[0] ^ bit, 0)] = flip(have[key], bit)
    return [have[key] for key in sorted(have)]


def gather_back(held, local, n):
    held = dict(held)
    for bit in reversed(bits_of(local, n // 2)):
        for r in sorted(r for r in held if r & bit):
            held[r ^ bit] = add(held[r ^ bit], flip(held.pop(r), bit))
    have = {(r, 0): v for r, v in held.items()}
    for bit in reversed(bits_of(1, local)):
        for key in sorted(key for key in have if key[0] & bit):
            have[(key[0] ^ bit, key[1] ^ bit)] = flip(have.pop(key), bit)
    return {e: v for (_, e), v in have.items()}


def per_row(row):
    return jnp.broadcast_to(row, (row.shape[1], row.shape[1])).T


def turn(v, cos, sin):
    return v * cos + pltpu.roll(v, v.shape[1] // 2, 1) * sin


def softmax_rows(qr, kr, same, scale):
    s = jnp.where(same, mm(qr, kr, ((1,), (1,))) * scale, -1e30)
    e = jnp.exp(s - jnp.max(s, axis=1, keepdims=True))
    return e / jnp.sum(e, axis=1, keepdims=True)


def attend_kernel(scale, qkv, r, gains, cos, sin, seg, qr_out, kr_out, vb_out, o_out):
    cols = o_out.shape[1]
    rq, rk = per_row(r[0, 0:1, :]), per_row(r[0, 1:2, :])
    seg_row = seg[0]
    same = per_row(seg_row) == seg_row
    for h in range(cols // HEAD_DIM):
        at = slice(h * HEAD_DIM, (h + 1) * HEAD_DIM)
        k_at = slice(cols + h * HEAD_DIM, cols + (h + 1) * HEAD_DIM)
        v_at = slice(2 * cols + h * HEAD_DIM, 2 * cols + (h + 1) * HEAD_DIM)
        qr = turn(qkv[:, at] * rq * gains[0:1, at], cos[...], sin[...]).astype(BF16)
        kr = turn(qkv[:, k_at] * rk * gains[1:2, at], cos[...], sin[...]).astype(BF16)
        vb = qkv[:, v_at].astype(BF16)
        p = softmax_rows(qr, kr, same, scale)
        qr_out[:, at] = qr
        kr_out[:, at] = kr
        vb_out[:, at] = vb
        o_out[:, at] = mm(p.astype(BF16), vb, ((1,), (0,))).astype(BF16)


def attend(qkv, r, gains, cos, sin, seg):
    total, cols = qkv.shape[0], qkv.shape[1] // 3
    zs, tok = seg.shape[0], seg.shape[2]
    tall = lambda w: pl.BlockSpec((tok, w), lambda b: (b, 0))
    fixed = lambda x: pl.BlockSpec(x.shape, lambda b: (0, 0))
    thin = jax.ShapeDtypeStruct((total, cols), BF16)
    return pl.pallas_call(
        functools.partial(attend_kernel, HEAD_DIM ** (-0.5)),
        grid=(zs,),
        in_specs=[
            tall(qkv.shape[1]),
            pl.BlockSpec((1, 2, tok), lambda b: (b, 0, 0)),
            fixed(gains),
            tall(HEAD_DIM),
            tall(HEAD_DIM),
            pl.BlockSpec((1, 1, tok), lambda b: (b, 0, 0)),
        ],
        out_specs=[tall(cols)] * 4,
        out_shape=[thin] * 4,
        compiler_params=pltpu.CompilerParams(vmem_limit_bytes=VMEM),
        cost_estimate=COST,
        name="attend",
    )(qkv, r, gains, cos, sin, seg)


def attend_back_kernel(
    scale, dhb, wo, q, k, qr, kr, vb, gains, cos, sin, seg, dq_out, dk_out, dv_out, sums
):
    cols = wo.shape[0]
    seg_row = seg[0]
    same = per_row(seg_row) == seg_row
    do_all = mm(dhb[...], wo[...], ((1,), (1,))).astype(BF16)
    sum_q = sum_k = 0.0
    for h in range(cols // HEAD_DIM):
        at = slice(h * HEAD_DIM, (h + 1) * HEAD_DIM)
        do = do_all[:, at]
        p = softmax_rows(qr[:, at], kr[:, at], same, scale)
        dp = mm(do, vb[:, at], ((1,), (1,)))
        ds = (p * (dp - jnp.sum(p * dp, axis=1, keepdims=True))).astype(BF16)
        dv_out[:, at] = mm(p.astype(BF16), do, ((0,), (0,))).astype(BF16)
        dq = turn(mm(ds, kr[:, at], ((1,), (0,))) * scale, cos[...], -sin[...])
        dk = turn(mm(ds, qr[:, at], ((0,), (0,))) * scale, cos[...], -sin[...])
        dq_out[:, at] = dq
        dk_out[:, at] = dk
        sum_q = sum_q + jnp.sum(q[:, at] * gains[0:1, at] * dq, axis=1, keepdims=True)
        sum_k = sum_k + jnp.sum(k[:, at] * gains[1:2, at] * dk, axis=1, keepdims=True)
    tok = dhb.shape[0]
    sums[0, 0:1, :] = jnp.broadcast_to(sum_q, (tok, tok)).T[0:1, :]
    sums[0, 1:2, :] = jnp.broadcast_to(sum_k, (tok, tok)).T[0:1, :]


def attend_back(dhb, wo, qkv, qr, kr, vb, gains, cos, sin, seg):
    total, cols = qkv.shape[0], wo.shape[0]
    zs, tok = seg.shape[0], seg.shape[2]
    tall = lambda w, at=0: pl.BlockSpec((tok, w), lambda b: (b, at))
    fixed = lambda x: pl.BlockSpec(x.shape, lambda b: (0, 0))
    wide = jax.ShapeDtypeStruct((total, cols), F32)
    return pl.pallas_call(
        functools.partial(attend_back_kernel, HEAD_DIM ** (-0.5)),
        grid=(zs,),
        in_specs=[
            tall(dhb.shape[1]),
            fixed(wo),
            tall(cols, 0),
            tall(cols, 1),
            tall(cols),
            tall(cols),
            tall(cols),
            fixed(gains),
            tall(HEAD_DIM),
            tall(HEAD_DIM),
            pl.BlockSpec((1, 1, tok), lambda b: (b, 0, 0)),
        ],
        out_specs=[tall(cols)] * 3 + [pl.BlockSpec((1, 2, tok), lambda b: (b, 0, 0))],
        out_shape=[
            wide,
            wide,
            jax.ShapeDtypeStruct((total, cols), BF16),
            jax.ShapeDtypeStruct((zs, 2, tok), F32),
        ],
        compiler_params=pltpu.CompilerParams(vmem_limit_bytes=VMEM),
        cost_estimate=COST,
        name="attend_back",
    )(dhb, wo, qkv, qkv, qr, kr, vb, gains, cos, sin, seg)


def join_back_kernel(q, k, dqn, dkn, dv, r, means, gains, out, gain_out):
    cols = dv.shape[1]
    for at, v, d in ((0, q, dqn), (1, k, dkn)):
        rr = per_row(r[0, at : at + 1, :])
        mean = per_row(means[0, at : at + 1, :])
        part = []
        for h in range(cols // HEAD_DIM):
            to = slice(h * HEAD_DIM, (h + 1) * HEAD_DIM)
            vr = v[:, to] * rr
            out[:, at * cols + h * HEAD_DIM : at * cols + (h + 1) * HEAD_DIM] = (
                rr * (gains[at : at + 1, to] * d[:, to]) - vr * (rr * rr) * mean
            ).astype(BF16)
            part.append(jnp.sum(d[:, to] * vr, axis=0, keepdims=True))
        row = jnp.concatenate(part, axis=1)

        @pl.when(pl.program_id(0) == 0)
        def _():
            gain_out[at : at + 1, :] = row

        @pl.when(pl.program_id(0) > 0)
        def _():
            gain_out[at : at + 1, :] += row

    out[:, 2 * cols :] = dv[...]


def join_back(qkv, dqn, dkn, dv, r, means, gains):
    total, cols = dv.shape
    zs, tok = r.shape[0], r.shape[2]
    tall = lambda w, at=0: pl.BlockSpec((tok, w), lambda b: (b, at))
    row = pl.BlockSpec((1, 2, tok), lambda b: (b, 0, 0))
    return pl.pallas_call(
        join_back_kernel,
        grid=(zs,),
        in_specs=[tall(cols, 0), tall(cols, 1), tall(cols), tall(cols), tall(cols), row, row]
        + [pl.BlockSpec(gains.shape, lambda b: (0, 0))],
        out_specs=[tall(3 * cols), pl.BlockSpec((2, cols), lambda b: (0, 0))],
        out_shape=[
            jax.ShapeDtypeStruct((total, 3 * cols), BF16),
            jax.ShapeDtypeStruct((2, cols), F32),
        ],
        compiler_params=pltpu.CompilerParams(vmem_limit_bytes=VMEM),
        cost_estimate=COST,
        name="join_back",
    )(qkv, qkv, dqn, dkn, dv, r, means, gains)


def first_back_kernel(d, w, x, r, da, gain):
    back = mm(d[...], w[...], ((1,), (1,)))
    da[...] = back.astype(BF16)
    row = jnp.sum(back * (x[...].astype(F32) * r[...]), axis=0, keepdims=True)

    @pl.when(pl.program_id(0) == 0)
    def _():
        gain[...] = row

    @pl.when(pl.program_id(0) > 0)
    def _():
        gain[...] += row


def first_back(d, w, x, r, tok):
    total, width = x.shape
    k = d.shape[1]
    return pl.pallas_call(
        first_back_kernel,
        grid=(total // tok,),
        in_specs=[
            pl.BlockSpec((tok, k), lambda b: (b, 0)),
            pl.BlockSpec((width, k), lambda b: (0, 0)),
            pl.BlockSpec((tok, width), lambda b: (b, 0)),
            pl.BlockSpec((tok, 1), lambda b: (b, 0)),
        ],
        out_specs=[
            pl.BlockSpec((tok, width), lambda b: (b, 0)),
            pl.BlockSpec((1, width), lambda b: (0, 0)),
        ],
        out_shape=[
            jax.ShapeDtypeStruct((total, width), BF16),
            jax.ShapeDtypeStruct((1, width), F32),
        ],
        compiler_params=pltpu.CompilerParams(vmem_limit_bytes=VMEM),
        cost_estimate=COST,
        name="first_back",
    )(d, w, x, r)


def form_kernel(count, own, *refs):
    ins, (gate_up, down) = refs[:count], refs[-2:]
    wide = gate_up.shape[2]
    for o in range(count):

        @pl.when(own[0] == o)
        def _():
            for e in range(count):
                gate_up[:, e, :] = ins[o ^ e][:, :wide].astype(F32)
                down[:, e, :] = ins[o ^ e][:, wide:].astype(F32)


def form(blocks, own, rows, start, stop, before=()):
    k = blocks[0][0].shape[1]
    count, ff, tile = len(blocks), k // 3, 32

    def spec(at):
        return pl.BlockSpec((tile, k), lambda i, o: (i + (start - at) // tile, 0))

    shapes = [
        jax.ShapeDtypeStruct((rows, count, 2 * ff), F32),
        jax.ShapeDtypeStruct((rows, count, ff), F32),
    ]
    outs = [
        pl.BlockSpec((tile, *s.shape[1:]), lambda i, o: (i + start // tile, 0, 0)) for s in shapes
    ]
    return pl.pallas_call(
        functools.partial(form_kernel, count),
        grid_spec=pltpu.PrefetchScalarGridSpec(
            num_scalar_prefetch=1,
            grid=((stop - start) // tile,),
            in_specs=[spec(at) for _, at in blocks]
            + [pl.BlockSpec(memory_space=pl.ANY)] * len(before),
            out_specs=outs,
        ),
        out_shape=shapes,
        input_output_aliases={1 + count + n: n for n in range(len(before))},
        compiler_params=pltpu.CompilerParams(vmem_limit_bytes=VMEM),
        cost_estimate=COST,
        name="form",
    )(own, *[v for v, _ in blocks], *before)


def extra_kernel(zat, router, attn, qk, ffn, out, rows):
    experts, cols = router.shape[0], qk.shape[1]
    rows[...] = jnp.zeros_like(rows)
    rows[:experts, :] = router[...]
    rows[experts : experts + 1, :] = attn[...]
    at = pl.ds(pl.multiple_of(zat[0] * cols, cols), cols)
    rows[experts + 1 : experts + 3, at] = qk[...]
    rows[experts + 3 : experts + 4, :] = ffn[...]
    out[...] = rows[...].T.astype(BF16)


def extra_columns(router, attn, qk, ffn, zat):
    width = attn.shape[1]
    whole = lambda x: pl.BlockSpec(x.shape, lambda i, z: (0, 0))
    out = jax.ShapeDtypeStruct((width, EXTRA), BF16)
    return pl.pallas_call(
        extra_kernel,
        grid_spec=pltpu.PrefetchScalarGridSpec(
            num_scalar_prefetch=1,
            grid=(1,),
            in_specs=[whole(x) for x in (router, attn, qk, ffn)],
            out_specs=whole(out),
            scratch_shapes=[pltpu.VMEM((EXTRA, width), F32)],
        ),
        out_shape=out,
        compiler_params=pltpu.CompilerParams(vmem_limit_bytes=VMEM),
        cost_estimate=COST,
        name="extra_columns",
    )(zat, router, attn, qk, ffn)


def inv_rms(v):
    return lax.rsqrt(jnp.mean(v * v, axis=-1, keepdims=True) + EPSILON)


def rms_back(v, r, gain, c):
    gc = gain * c
    return r * gc - v * (r * r * r) * jnp.mean(v * gc, axis=-1, keepdims=True)


def places_and_tables(at, dp, zs, rows):
    dealt = lax.dynamic_slice_in_dim(at[ORDER], dp * zs * SEQ_DEV, zs * SEQ_DEV)
    lens = jnp.take(at[LENGTHS], dealt).reshape(zs, SEQ_DEV)
    ends = jnp.cumsum(lens, axis=1)
    places = jnp.arange(rows, dtype=jnp.int32)
    segment = jnp.sum((places[None, :, None] >= ends[:, None, :]).astype(jnp.int32), axis=2)
    starts = ends - lens
    offset = jnp.sum(
        jnp.where(
            segment[:, :, None] == jnp.arange(SEQ_DEV, dtype=jnp.int32), starts[:, None, :], 0
        ),
        axis=2,
    )
    half = HEAD_DIM // 2
    inverse = ROPE_BASE ** (-2.0 * jnp.arange(half, dtype=F32) / HEAD_DIM)
    turned = (places[None] - offset).astype(F32)[..., None] * inverse
    at[COS] = jnp.tile(jnp.cos(turned), (1, 1, 2)).reshape(zs * rows, HEAD_DIM)
    sin = jnp.sin(turned)
    at[SIN] = jnp.concatenate([-sin, sin], axis=2).reshape(zs * rows, HEAD_DIM)
    at[SEG] = segment.astype(F32)[:, None, :]


def on_device(
    tokens,
    lengths,
    permutation,
    routes,
    norm_gains,
    w_qkv,
    w_out,
    router,
    w_gate_up,
    w_down,
    cotangent,
):
    rows, width = tokens.shape
    zs = lax.axis_size("expert")
    dps = lax.axis_size("dp")
    z = lax.axis_index("expert")
    dp = lax.axis_index("dp")
    local = w_gate_up.shape[1]
    ff = w_down.shape[2]
    experts = router.shape[1]
    own_rows = w_qkv.shape[0]
    e_rows = w_gate_up.shape[0]
    cols = width // zs
    expert = z * local + lax.rem(dp, local)
    own = lax.rem(dp, local)
    top = local // 2
    far_bit = dps // 2
    mid = zs // 2
    laid_out = local == 4 and dps == 8
    me_at = jnp.reshape(dp, (1,)).astype(jnp.int32)
    expert_at = jnp.stack([expert, dp, jnp.int32(experts)]).astype(jnp.int32)
    at = Flow()

    extra = jnp.concatenate(
        [router, norm_gains, jnp.zeros((own_rows, EXTRA - experts - 4), BF16)], axis=1
    )
    sent = jnp.stack(
        [
            jnp.concatenate(
                [w_qkv[:, i * width + e * cols : i * width + (e + 1) * cols] for i in range(3)]
                + [extra],
                axis=1,
            )
            for e in range(zs)
        ]
    )
    at[MINE] = lax.all_to_all(sent, "expert", split_axis=0, concat_axis=0, tiled=True)
    moved = [(b, (b % dps) * zs + b // dps) for b in range(dps * zs)]

    for e in range(local):
        at[W, 0, e] = jnp.concatenate(
            [pick(w_gate_up, own ^ e, 1), pick(w_down, own ^ e, 1)], axis=1
        )
    at[X, 0] = tokens
    at[OUT] = w_out
    at.fence(MINE, (X, 0), OUT, *at.having(W))

    at[ATTN] = lax.all_gather(
        at[MINE].reshape(zs * own_rows, 3 * cols + EXTRA), "dp", axis=0, tiled=True
    )
    if laid_out:
        at[W, 1, 0] = flip(at[W, 0, 1], 1)
        at[W, 1, 2] = flip(at[W, 0, 3], 1)
    at[LENGTHS], at[ORDER], at[ROUTES], at[COT] = lengths, permutation, routes, cotangent
    for i in range(1, zs):
        at[X, i] = hop(at[X, i - 1])
        if i == 1:
            at.fence((X, 1), LENGTHS, ORDER, ROUTES, COT, OUT)
            places_and_tables(at, dp, zs, rows)
        elif i == 2:
            at.fence((X, 2), COS, SIN, SEG, ROUTES, COT)
            at[MASK] = jnp.sum(
                (at[ROUTES][:, :, None] == jnp.arange(experts, dtype=jnp.int32)).astype(BF16),
                axis=1,
            )
            mask_pad = jnp.concatenate(
                [at[MASK], jnp.zeros((rows, EXTRA - experts), BF16)], axis=1
            )
            at[G, 0] = jnp.concatenate([at[COT], mask_pad], axis=1)
            at[OUT] = lax.ppermute(at[OUT], ("dp", "expert"), moved)
        else:
            at.fence((X, i))
    xs = [(X, i) for i in range(zs)]
    at.fence(ATTN, OUT, (G, 0), MASK, *xs, *at.having(W))

    cut = e_rows // 4
    if laid_out:
        at[W, 2, 0] = flip(at[W, 0, 2], 2)
        at[W, 4, 0] = flip(at[W, 0, 0], 4)
    at[G, 1] = hop(at[G, 0])
    out_w = lax.all_gather(at[OUT], "dp", axis=0, tiled=True)
    attn_w = at[ATTN]
    qkv_w = attn_w[:, : 3 * cols]
    router_full = attn_w[:, 3 * cols : 3 * cols + experts]
    gains = attn_w[:, 3 * cols + experts : 3 * cols + experts + 4].astype(F32).T
    router_t = router_full.T
    x_all = by_line([at[key] for key in xs])
    xf = x_all.astype(F32)
    r_attn = inv_rms(xf)
    a_all = (xf * r_attn * gains[0]).astype(BF16)
    at[QKV] = nn(a_all, qkv_w)
    at.fence(QKV, (G, 1))
    qkv = at[QKV]
    q, k = qkv[:, :cols], qkv[:, cols : 2 * cols]
    at[SQUARES] = lax.psum(
        jnp.stack([jnp.sum(q * q, axis=1), jnp.sum(k * k, axis=1)]), "expert"
    )
    at.fence(SQUARES, (G, 1))
    at[G, 2] = hop(at[G, 1])
    by_block = lambda v: v.reshape(2, zs, rows).transpose(1, 0, 2)
    r_qk = by_block(lax.rsqrt(at[SQUARES] / width + EPSILON))
    gain_qk = lax.dynamic_slice_in_dim(gains[1:3], z * cols, cols, axis=1)
    cos, sin, seg = at[COS], at[SIN], at[SEG]
    qr, kr, vb, o = attend(qkv, r_qk, gain_qk, cos, sin, seg)
    at[ADDED] = nn(o, out_w, BF16)
    at.fence(ADDED, (G, 2), *(w for w in at.having(W) if laid_out))
    at[ADDED] = lax.psum_scatter(at[ADDED], "expert", scatter_dimension=0, tiled=True)
    for i in range(3, zs):
        at[G, i] = hop(at[G, i - 1])
    if laid_out:
        at[W, 3, 0] = flip(at[W, 1, 2], 2)
        at[W, 5, 0] = flip(at[W, 1, 0], 4)
        at[WA, 6] = flip(at[W, 2, 0][: 11 * cut // 4], 4)
    first_g = [(G, i) for i in range(mid)]
    last_g = [(G, i) for i in range(mid, zs)]
    at[FAR_GA] = flip(jnp.concatenate([at[key] for key in first_g], axis=0), top)
    weight_keys = at.having(W) + at.having(WA)
    at.fence(ADDED, FAR_GA, (G, zs - 1), *(w for w in weight_keys if laid_out))
    marks = (0, 3 * cut // 4, 9 * cut // 4, e_rows)
    hid = tokens.astype(F32) + at[ADDED].astype(F32)
    r_ffn = inv_rms(hid)
    m = (hid * r_ffn * gains[3]).astype(BF16)

    at[M, 0] = m
    mine_e = (jnp.arange(experts) == expert).astype(F32)

    def chunk_places(kind, parts):
        masks = jnp.concatenate([x[:, width : width + experts] for x in parts], axis=0)
        masks = masks.astype(F32).reshape(-1, rows, experts)
        on = jnp.sum(masks * mine_e, axis=2)
        pos = jnp.where(on > 0, jnp.cumsum(on, axis=1) - 1.0, -1.0).astype(jnp.int32)
        at[kind, 0], at[kind, 1], at[kind, 2] = pos, pos.T, masks.transpose(0, 2, 1)
        out = jax.ShapeDtypeStruct((pos.shape[0] * CAP, width), BF16)
        (at[kind, 3],) = pick_rows(gather_cot_kernel, "gather_cot", parts, [pos], [out], expert_at)

    waiting = [(G, key) for key in last_g] + [(M, (M, i)) for i in range(zs)]
    near_cores = [fan([m], top)[1:]]
    for i in range(1, zs):
        at[M, i] = hop(at[M, i - 1])
        kind, key = waiting.pop(0)
        at[FAR, *key] = flip(at[key], top)
        beside = [(FAR, *key)]
        if laid_out:
            at[WB, i] = flip(at[W, 3, 0][marks[i - 1] : marks[i]], 4)
            beside.append((WB, i))
            if i == 1:
                at[WA, 7] = flip(at[W, 2, 0][11 * cut // 4 :], 4)
                beside.append((WA, 7))
        if i == 1:
            g_near = [jnp.concatenate([at[key] for key in first_g + last_g], axis=0)]
            chunk_places(NEAR, [x for xs in fan(g_near, top) for x in xs])
        if i == 2:
            beside += at.having(NEAR)
        if i == zs - 1:
            g_far = [at[FAR_GA], *[at[FAR, *k] for k in last_g]]
            chunk_places(DISTANT, [x for xs in fan(g_far, top) for x in xs])
            beside += at.having(DISTANT)
        at.fence((M, i), *beside)
        near_cores.append(fan([at[M, i]], top)[1:])
    key = waiting.pop(0)[1]
    at[FAR, *key] = flip(at[key], top)

    def chunk_gather(kind, blocks, cores):
        flat = [*blocks, *(x[0] for d in range(top - 1) for x in (c[d] for c in cores))]
        slots = at[kind, 0].shape[0] * CAP
        outs = [
            jax.ShapeDtypeStruct((slots, width), BF16),
            jax.ShapeDtypeStruct((slots, 1), F32),
        ]
        others = [at[kind, 0], at[kind, 2], router_t]
        picked, gate = pick_rows(gather_kernel, "gather", flat, others, outs, expert_at)
        return picked, at[kind, 3], gate

    def chunk_expert(kind, groups, got):
        heights = [h for group in groups for h in group]
        backs, outs = run_expert(*got, at[kind, 1], weights, expert_at, heights, ff)
        back = []
        for group in groups:
            back.append(backs[: len(group)])
            backs = backs[len(group) :]
        return back, (got[0], got[1], *outs)

    ms = [at[M, i] for i in range(zs)]
    near_rows = chunk_gather(NEAR, ms, near_cores)
    for i, v in enumerate(near_rows):
        at[ROWS, i] = v
    at.fence(*at.having(ROWS), (FAR, *key))
    while waiting:
        key = waiting.pop(0)[1]
        at[FAR, *key] = flip(at[key], top)
    if laid_out:
        keys = [(W, r, 0) for r in range(6)] + [(WA, 6), (WA, 7), (WB, 1), (WB, 2), (WB, 3)]
        weights = [at[key] for key in keys]
    else:
        weights = spread({e: at[W, 0, e] for e in range(local)}, dps)
    own_heights = [rows] * zs
    near_back, near_outs = chunk_expert(
        NEAR, [own_heights] + [[zs * rows]] * (top - 1), [at[ROWS, i] for i in range(3)]
    )
    far_ms = [(FAR, M, i) for i in range(zs)]
    at[NEAR_GACT] = near_outs[4]
    at.fence(NEAR_GACT, *far_ms)
    ms = [at[key] for key in far_ms]
    far_rows = chunk_gather(DISTANT, ms, [fan([v], top)[1:] for v in ms])
    far_back, far_outs = chunk_expert(
        DISTANT, [own_heights] + [[mid * rows, (zs - mid) * rows]] * (top - 1), far_rows
    )
    near_outs = (*near_outs[:4], at[NEAR_GACT])

    quarter = dps // 4
    near_sum = fold(near_back)
    far_sum = fold(far_back)
    chunk_keys = [(C, n) for n in range(10)]
    for key, v in zip(chunk_keys, (*near_outs, *far_outs), strict=True):
        at[key] = v
    for i, v in enumerate(far_sum):
        at[BACKS, i] = v
    at.fence(*at.having(BACKS), *chunk_keys)

    halves_cut = [(0, e_rows // 2, e_rows) if laid_out else (0, e_rows)] * quarter

    def chunk_grads(kind, first, cuts):
        c = [at[key] for key in chunk_keys]
        made = list(grads([c[:5], c[5:]], first, e_rows, cuts))
        for row, cut in enumerate(cuts):
            for start in cut[:-1]:
                at[kind, row, start] = made.pop(0)

    def send_part(key, row, start):
        at[PIECE, key, row, start] = flip(at[key, row, start], far_bit)

    def sum_row(keep, key, row):
        starts = sorted(k[2] for k in at.having(key) if k[1] == row)
        if not laid_out:
            send_part(key, row, 0)
        return add_pieces(at[keep, row, 0], [at[PIECE, key, row, start] for start in starts])

    whole_cut = [(0, e_rows)] * quarter
    last = zs - 1

    at[THERE] = flip(at[BACKS, last], top)
    chunk_grads(SEND_HIGH, 3 * quarter, halves_cut)
    at.fence(THERE, *at.having(SEND_HIGH), *chunk_keys)
    half = e_rows // 2
    early, most = 3 * e_rows // 8, 3 * e_rows // 4
    for i in reversed(range(zs)):
        here = near_sum[i].astype(F32) + at[THERE].astype(F32)
        if i < last:
            here = here + at[ACC].astype(F32)
        at[ACC] = here.astype(BF16)
        if not i:
            break
        at[ACC] = hop(at[ACC], -1)
        at[THERE] = flip(at[BACKS, i - 1], top)
        beside = []
        if i == last:
            if laid_out:
                send_part(SEND_HIGH, 0, 0)
            for n, y in enumerate(result(at[C, 9], at[DISTANT, 1], weights, top, me_at)):
                at[Y_PART, n] = y
            beside = [*at.having(Y_PART), *at.having(PIECE)]
        if i == last - 1:
            for n, y in enumerate(result(at[C, 4], at[NEAR, 1], weights, top, me_at)):
                at[NEAR_PART, n] = y
            if laid_out:
                send_part(SEND_HIGH, 0, half)
            beside = [*at.having(NEAR_PART), *at.having(PIECE)]
        if i == last - 2:
            if laid_out:
                send_part(SEND_HIGH, 1, 0)
            low_cut = halves_cut
            if laid_out:
                low_cut = [halves_cut[0], (0, e_rows - early, e_rows)]
            chunk_grads(SEND_LOW, 2 * quarter, low_cut)
            at[Y_FAR] = fold([[at[key]] for key in at.having(Y_PART)])[0]
            beside = [Y_FAR, *at.having(SEND_LOW), *at.having(PIECE)]
        at.fence(ACC, THERE, *beside, *chunk_keys)
    at.fence(ACC, *at.having(NEAR_PART))
    dm = at[ACC].astype(F32)
    at[Y_FAR] = flip(at[Y_FAR], top)
    if laid_out:
        send_part(SEND_HIGH, 1, half)
        send_part(SEND_LOW, 0, 0)

    own_mask = at[MASK].astype(F32)
    own_logits = jnp.where(own_mask > 0, nn(m, router_full), -1e30)
    own_e = jnp.where(
        own_mask > 0, jnp.exp(own_logits - jnp.max(own_logits, axis=1, keepdims=True)), 0.0
    )
    gate_own = own_e / jnp.sum(own_e, axis=1, keepdims=True)
    dgates = dm[:, width : width + experts] + dm[:, width + experts : width + 2 * experts]
    dz = (
        gate_own * (dgates - jnp.sum(gate_own * dgates, axis=1, keepdims=True))
    ).astype(BF16)
    dmt = nt(dz, router_full) + dm[:, :width]
    grad_out = cotangent.astype(F32)
    dh = grad_out + rms_back(hid, r_ffn, gains[3], dmt)
    at[DHB] = lax.all_gather(dh.astype(BF16), "expert", axis=0, tiled=True)
    router_part = tn(dz, m)
    gain_ffn = jnp.sum(dmt * hid * r_ffn, axis=0)
    at[Y_NEAR] = fold([[at[key]] for key in at.having(NEAR_PART)])[0]
    chunk_grads(KEEP_HIGH, quarter, whole_cut)
    if laid_out:
        at[TAIL, quarter, 0] = sum_row(KEEP_HIGH, SEND_HIGH, 0)
    chunk_grads(KEEP_LOW, 0, whole_cut)
    at[ROUTER], at[GAIN_FFN] = router_part, gain_ffn
    tails = at.having(TAIL)
    keeps = at.having(KEEP_LOW) + at.having(KEEP_HIGH) + at.having(SEND_LOW)
    at.fence(DHB, Y_FAR, Y_NEAR, ROUTER, GAIN_FFN, *keeps, *at.having(PIECE), *tails)
    dhb = at[DHB]
    if laid_out:
        at[TAIL, 0, 2] = flip(at[TAIL, 2, 0], 2)
        send_part(SEND_LOW, 0, half)
        send_part(SEND_LOW, 1, 0)
    for i in range(1 if laid_out else 0, quarter):
        at[TAIL, quarter + i, 0] = sum_row(KEEP_HIGH, SEND_HIGH, i)
    y_own = add(at[Y_NEAR], at[Y_FAR])
    at[Y] = lax.psum_scatter(
        by_line([y_own[i * rows : (i + 1) * rows] for i in range(zs)]),
        "expert",
        scatter_dimension=0,
        tiled=True,
    )

    dqn, dkn, dv, sums = attend_back(dhb, out_w, qkv, qr, kr, vb, gain_qk, cos, sin, seg)
    means = lax.psum(sums.reshape(-1, rows), "expert").reshape(zs, 2, rows) / width
    out_sum = Halving(at, OUT_GRAD, tn(o, dhb, BF16))
    dqkv, gains_qk = join_back(qkv, dqn, dkn, dv, r_qk, means, gain_qk)
    at[DQKV] = dqkv
    at.fence(DQKV, Y, *at.having(OUT_GRAD), *at.having(PIECE), *at.having(TAIL))
    out_sum.begin(1)

    at[ODD] = attn_grads(a_all, at[DQKV], [], me_at, 1, 2)
    at.fence(ODD, DQKV, *at.having(OUT_GRAD), *at.having(TAIL), *at.having(SEND_LOW))
    out_sum.end()
    out_sum.begin(far_bit)
    at[ODD] = flip(at[ODD], 1)
    if laid_out:
        at[HALF, 0] = flip(at[TAIL, 3, 0][:most], 2)
        send_part(SEND_LOW, 1, e_rows - early)
    at[DA], at[GAIN_ATTN] = first_back(at[DQKV], attn_w, x_all, r_attn, rows)
    even = attn_grads(a_all, at[DQKV], [], me_at, 0, 2)
    at[HELD] = add(even, at[ODD])
    at.fence(HELD, DQKV, DA, GAIN_ATTN, *at.having(OUT_GRAD), *at.having(HALF), *at.having(PIECE))
    at[DA] = lax.psum_scatter(at[DA], "expert", scatter_dimension=0, tiled=True)
    sides = halves(at[HELD], zs * own_rows)
    stage(at, sides, 0)
    out_sum.end()
    out_sum.begin(2)
    at[BESIDE] = extra_columns(
        at[ROUTER], at[GAIN_ATTN], gains_qk, at[GAIN_FFN][None], jnp.reshape(z, (1,))
    )
    for turn_ in range(1, len(bits_of(2, dps))):
        at.fence(*at.having(SIDE), BESIDE, *at.having(OUT_GRAD), *at.having(KEEP_LOW), *at.having(PIECE))
        out_sum.end()
        if laid_out:
            at[OUT_GRAD, 0] = lax.ppermute(
                at[OUT_GRAD, 0], ("dp", "expert"), [(b, a) for a, b in moved]
            )
        if turn_ < len(bits_of(2, dps)) - 1:
            out_sum.begin(2 << turn_)
        if turn_ == 1:
            small_sum = Halving(at, SMALL, at[BESIDE])
            small_sum.begin(1)
            for i in range(quarter):
                at[TAIL, i, 0] = sum_row(KEEP_LOW, SEND_LOW, i)
        sides = unstage(at, sides, turn_ - 1)
        stage(at, sides, turn_)
    at.fence(*at.having(SIDE), *at.having(SMALL), *at.having(TAIL))
    sides = unstage(at, sides, len(bits_of(2, dps)) - 1)
    at[BACK] = jnp.concatenate([sides[0][0][0], sides[1][0][0]], axis=1)
    at.fence(BACK, DA, *at.having(OUT_GRAD), *at.having(SMALL), *at.having(HALF), *at.having(TAIL))
    small_sum.end()
    if not laid_out:
        at[OUT_GRAD, 0] = lax.ppermute(
            at[OUT_GRAD, 0], ("dp", "expert"), [(b, a) for a, b in moved]
        )
    at[BACK] = lax.all_to_all(
        at[BACK].reshape(zs, own_rows, 3 * cols),
        "expert",
        split_axis=0,
        concat_axis=0,
        tiled=True,
    )
    own_at = jnp.reshape(own, (1,))
    bits = bits_of(2, dps)
    small_sum.begin(bits[0])
    if laid_out:
        at[HALF, most] = flip(at[TAIL, 3, 0][most:], 2)
        at[TAIL, 0, 1] = flip(at[TAIL, 1, 0], 1)
        blocks = [(at[TAIL, 0, e], 0) for e in range(local - 1)]
        at[HALF, 0] = flip(at[HALF, 0], 1)
        at[GU], at[DN] = form([*blocks, (at[HALF, 0], 0)], own_at, e_rows, 0, most)
        at.fence(GU, DN, *at.having(SMALL))
        blocks += [(flip(at[HALF, most], 1), most)]
        at[GU], at[DN] = form(blocks, own_at, e_rows, most, e_rows, (at[GU], at[DN]))
    else:
        rest = gather_back({k[1]: at[k] for k in at.having(TAIL)}, local, dps)
        at[GU], at[DN] = form([(rest[e], 0) for e in range(local)], own_at, e_rows, 0, e_rows)
    small_sum.end()
    for bit in bits[1:]:
        small_sum.begin(bit)
        small_sum.end()
    at.fence(BACK, GU, DN, *at.having(OUT_GRAD), *at.having(SMALL))
    grad_w_out = at[OUT_GRAD, 0].astype(F32)
    back = at[BACK].astype(F32)
    grad_w_qkv = jnp.concatenate(
        [back[e, :, i * cols : (i + 1) * cols] for i in range(3) for e in range(zs)], axis=1
    )
    place = place_in_ring(z, zs)
    blocks = at[SMALL, 0].reshape(zs, own_rows, EXTRA)
    extra_sum = pick(blocks, z, 0).astype(F32)
    for i in range(1, zs):
        to = at_place(lax.rem(place + i, zs), zs)
        extra_sum = extra_sum + hop(pick(blocks, to, 0), i).astype(F32)
    grad_router = extra_sum[:, :experts]
    grad_gains = extra_sum[:, experts : experts + 4]
    da = at[DA].astype(F32)

    output = hid + at[Y].astype(F32)
    x_own = tokens.astype(F32)
    grad_tokens = dh + rms_back(x_own, inv_rms(x_own), gains[0], da)
    return (
        output,
        grad_tokens,
        grad_gains,
        grad_w_qkv,
        grad_w_out,
        grad_router,
        at[GU],
        at[DN],
    )


def solution(mesh):
    both = P(("dp", "expert"), None)
    experts = P("dp", "expert", None)
    return jax.shard_map(
        on_device,
        mesh=mesh,
        in_specs=(both, P(), P(), both, both, both, both, both, experts, experts, both),
        out_specs=(both, both, both, both, both, both, experts, experts),
        check_vma=False,
    )
```

```python
import functools

import jax
import jax.numpy as jnp
from jax import lax
from jax.experimental import pallas as pl
from jax.experimental.pallas import tpu as pltpu
from jax.sharding import PartitionSpec as P

HEADS = 16
HEAD_DIM = 128
SEQ_DEV = 2
EPSILON = 1e-06
ROPE_BASE = 50000.0
CAP = 80
EXTRA = 128
VMEM = 56 * 2**20
COST = pl.CostEstimate(flops=10**6, bytes_accessed=10**5, transcendentals=0)

F32 = jnp.float32
BF16 = jnp.bfloat16


def dot(a, b, dims, out=F32):
    return lax.dot_general(a, b, (dims, ((), ())), preferred_element_type=F32).astype(out)


def nn(a, b, out=F32):
    return dot(a, b, ((1,), (0,)), out)


def nt(a, b, out=F32):
    return dot(a, b, ((1,), (1,)), out)


def tn(a, b, out=F32):
    return dot(a, b, ((0,), (0,)), out)


def flip(v, bit):
    return lax.ppermute(v, "dp", [(i, i ^ bit) for i in range(lax.axis_size("dp"))])


def ring(n):
    return [*range(0, n, 2), *reversed(range(1, n, 2))]


def hop(v, step=1):
    order = ring(lax.axis_size("expert"))
    n = len(order)
    pairs = [(order[i], order[(i + step) % n]) for i in range(n)]
    return lax.ppermute(v, "expert", pairs)


def gather_ring(v):
    return [v] + [hop(v, i) for i in range(1, lax.axis_size("expert"))]


def place_in_ring(i, n):
    half = i // 2
    return jnp.where(i % 2 == 0, half, n - 1 - half) if not isinstance(i, int) else (
        half if i % 2 == 0 else n - 1 - half
    )


def at_place(p, n):
    return jnp.where(p < (n + 1) // 2, 2 * p, 2 * (n - 1 - p) + 1)


def by_line(blocks):
    n = len(blocks)
    mine = place_in_ring(lax.axis_index("expert"), n)
    stacked = jnp.stack(blocks)
    return jnp.concatenate(
        [pick(stacked, lax.rem(mine - place_in_ring(i, n) + n, n), 0) for i in range(n)], axis=0
    )


def bits_of(low, high):
    out = []
    while low < high:
        out.append(low)
        low *= 2
    return out


def pick(v, index, axis):
    return lax.dynamic_index_in_dim(v, index, axis, keepdims=False)


def tie(*values):
    return lax.optimization_barrier(values)


(
    ORDER,
    LENGTHS,
    COS,
    SIN,
    SEG,
    MINE,
    W,
    X,
    OUT,
    ATTN,
    ROUTES,
    COT,
    MASK,
    G,
    QKV,
    SQUARES,
    ADDED,
    WA,
    FAR_GA,
    WB,
    M,
    NEAR_GACT,
    C,
    FAR,
    THERE,
    SEND_HIGH,
    ACC,
    Y_PART,
    NEAR_PART,
    SEND_LOW,
    Y_FAR,
    Y_NEAR,
    DHB,
    KEEP_HIGH,
    KEEP_LOW,
    ROUTER,
    GAIN_FFN,
    TAIL,
    Y,
    DQKV,
    ODD,
    DA,
    GAIN_ATTN,
    HELD,
    OUT_GRAD,
    BESIDE,
    SIDE,
    BACK,
    GU,
    DN,
    NEAR,
    DISTANT,
    PIECE,
    BACKS,
    ROWS,
    HALF,
    SMALL,
) = range(57)


class Flow:
    def __init__(self):
        self.of = {}

    def fence(self, *keys):
        out = tie(*[self.of[key] for key in keys])
        for key, v in zip(keys, out, strict=True):
            self.of[key] = v

    def __getitem__(self, key):
        return self.of[key]

    def __setitem__(self, key, value):
        self.of[key] = value

    def having(self, kind):
        return [key for key in self.of if isinstance(key, tuple) and key[0] == kind]


def fan(pieces, low):
    out = [list(pieces)]
    for bit in bits_of(1, low):
        out = out + [[flip(x, bit) for x in xs] for xs in out]
    return out


def add(a, b):
    return (a.astype(F32) + b.astype(F32)).astype(BF16)


def match(pieces, like):
    if len(pieces) == len(like):
        return pieces
    step = like[0].shape[0]
    return [x[i : i + step] for x in pieces for i in range(0, x.shape[0], step)]


def fold(parts):
    parts = list(parts)
    while len(parts) > 1:
        half = len(parts) // 2
        for i in range(half):
            got = match([flip(x, half) for x in reversed(parts[half + i])][::-1], parts[i])
            parts[i] = [add(a, b) for a, b in zip(parts[i], got, strict=True)]
        parts = parts[:half]
    return parts[0]


class Halving:
    def __init__(self, at, kind, value):
        self.at, self.kind, self.dp = at, kind, lax.axis_index("dp")
        n = lax.axis_size("dp")
        self.left = bits_of(1, n)[::-1]
        shape = (2,) * len(self.left) + (value.shape[0] // n, value.shape[1])
        at[kind, 0] = value.reshape(shape)

    def begin(self, bit):
        at, axis = self.at, self.left.index(bit)
        mine = lax.rem(self.dp // bit, 2)
        v = at[self.kind, 0]
        at[self.kind, 1] = flip(pick(v, 1 - mine, axis), bit)
        at[self.kind, 0] = pick(v, mine, axis)
        self.left.remove(bit)

    def end(self):
        at = self.at
        at[self.kind, 0] = add(at[self.kind, 0], at.of.pop((self.kind, 1)))


def blocks_of(parts, tok):
    return [(i, at) for i, p in enumerate(parts) for at in range(0, p.shape[0], tok)]


def onehot_back(pos_t, b):
    slot = lax.broadcasted_iota(jnp.int32, (pos_t.shape[0], CAP), 1)
    return (slot == pos_t[:, b : b + 1]).astype(BF16)


def onehot(pos_ref, b):
    slot = lax.broadcasted_iota(jnp.int32, (CAP, pos_ref.shape[1]), 0)
    return slot == pos_ref[b : b + 1, :]


def mm(a, b, dims):
    return lax.dot_general(a, b, (dims, ((), ())), preferred_element_type=F32)


def to_distance(ref, rows, value, me):
    n = lax.axis_size("dp")
    wide = value.shape[1] // n
    for c in range(n):
        at = pl.multiple_of((me ^ c) * wide, wide)
        ref[rows, pl.ds(at, wide)] = value[:, c * wide : (c + 1) * wide]


def gather_kernel(count, expert, *refs):
    parts, (pos, named, router, rows_out, gate) = refs[:count], refs[count:]
    tok = pos.shape[1]
    for b, (i, first) in enumerate(blocks_of(parts, tok)):
        at = slice(b * CAP, (b + 1) * CAP)
        part = parts[i][first : first + tok, :]
        hot = onehot(pos, b)
        found = mm(hot.astype(BF16), part, ((1,), (0,))).astype(BF16)
        to_distance(rows_out, at, found, expert[1])
        chosen = named[b] > 0
        logits = jnp.where(chosen, mm(router[...], part, ((1,), (1,))), -1e30)
        e = jnp.where(chosen, jnp.exp(logits - jnp.max(logits, axis=0, keepdims=True)), 0.0)
        gates = e / jnp.sum(e, axis=0, keepdims=True)
        mine = lax.broadcasted_iota(jnp.int32, gates.shape, 0) == expert[0]
        row = jnp.sum(jnp.where(mine, gates, 0.0), axis=0, keepdims=True)
        gate[at, :] = jnp.sum(jnp.where(hot, row, 0.0), axis=1, keepdims=True)


def gather_cot_kernel(count, expert, *refs):
    parts, (pos, rows_out) = refs[:count], refs[count:]
    tok = pos.shape[1]
    width = rows_out.shape[1]
    for b, (i, first) in enumerate(blocks_of(parts, tok)):
        part = parts[i][first : first + tok, :width]
        found = mm(onehot(pos, b).astype(BF16), part, ((1,), (0,))).astype(BF16)
        to_distance(rows_out, slice(b * CAP, (b + 1) * CAP), found, expert[1])


def pick_rows(kernel, name, parts, others, outs, expert):
    ins = [*parts, *others]
    whole = lambda x: pl.BlockSpec(x.shape, lambda n, e: (0,) * len(x.shape))
    return pl.pallas_call(
        functools.partial(kernel, len(parts)),
        grid_spec=pltpu.PrefetchScalarGridSpec(
            num_scalar_prefetch=1,
            grid=(1,),
            in_specs=[whole(x) for x in ins],
            out_specs=[whole(x) for x in outs],
        ),
        out_shape=outs,
        compiler_params=pltpu.CompilerParams(vmem_limit_bytes=VMEM),
        cost_estimate=COST,
        name=name,
    )(expert, *ins)


def spans(pieces):
    out, at = [], 0
    for p in pieces:
        out.append(slice(at, at + p.shape[0]))
        at += p.shape[0]
    return out


def expert_kernel(count, pieces, expert, *refs):
    rows_in, gs_in, gate, pos_t = refs[:4]
    parts = [refs[4 + i * pieces : 4 + (i + 1) * pieces] for i in range(3)]
    refs = refs[4 + 3 * pieces :]
    backs, refs = refs[:count], refs[count:]
    dg_out, du_out, gact_out, acc, dgate, wg, wu, wd = refs
    n = pl.program_id(0)
    tok = pos_t.shape[0]
    width = rows_in.shape[1]
    for at, a, b, c in zip(spans(parts[0]), *parts, strict=True):
        wg[at, :] = a[...]
        wu[at, :] = b[...]
        wd[at, :] = c[...]

    rows = rows_in[...]
    g = mm(rows, wg[...], ((1,), (0,)))
    u = mm(rows, wu[...], ((1,), (0,)))
    gw = mm(gs_in[...], wd[...], ((1,), (0,)))
    sg = 1.0 / (1.0 + jnp.exp(-g))
    silu = g * sg
    act = (silu * u).astype(BF16).astype(F32)
    part = jnp.sum(act * gw, axis=1, keepdims=True)
    gate_v = gate[...]
    gact_out[...] = (gate_v * act).astype(BF16)
    dact = gate_v * gw
    dg = (dact * u * (sg * (1.0 + g * (1.0 - sg)))).astype(BF16)
    du = (dact * silu).astype(BF16)
    dg_out[...] = dg
    du_out[...] = du
    back = mm(dg, wg[...], ((1,), (1,))) + mm(du, wu[...], ((1,), (1,)))

    @pl.when(n == 0)
    def _():
        acc[...] = back
        dgate[...] = part

    @pl.when(n > 0)
    def _():
        acc[...] += back
        dgate[...] += part

    @pl.when(n == pl.num_programs(0) - 1)
    def _():
        lane = lax.broadcasted_iota(jnp.int32, (CAP, EXTRA), 1)
        for b, (i, first) in enumerate(blocks_of(backs, tok)):
            at = slice(b * CAP, (b + 1) * CAP)
            to = slice(first, first + tok)
            hot = onehot_back(pos_t, b)
            out = backs[i]
            found = mm(hot, acc[at, :].astype(BF16), ((1,), (0,))).astype(BF16)
            to_distance(out, to, found, expert[1])
            d = dgate[at, :]
            hi = d.astype(BF16).astype(F32)
            beside = jnp.where(
                lane == expert[0], hi, jnp.where(lane == expert[2] + expert[0], d - hi, 0.0)
            ).astype(BF16)
            out[to, width:] = mm(hot, beside, ((1,), (0,))).astype(BF16)


def run_expert(rows, gs, gate, pos_t, pieces, expert, heights, ff):
    slots, width = rows.shape
    tile = min(512, ff)
    steps = ff // tile
    whole = lambda x: pl.BlockSpec(x.shape, lambda n, e: (0,) * len(x.shape))
    column = pl.BlockSpec((slots, tile), lambda n, e: (0, n))
    backs = [jax.ShapeDtypeStruct((h, width + EXTRA), BF16) for h in heights]
    thin = jax.ShapeDtypeStruct((slots, ff), BF16)
    outs = pl.pallas_call(
        functools.partial(expert_kernel, len(heights), len(pieces)),
        grid_spec=pltpu.PrefetchScalarGridSpec(
            num_scalar_prefetch=1,
            grid=(steps,),
            in_specs=[whole(x) for x in (rows, gs, gate, pos_t)]
            + [pl.BlockSpec((p.shape[0], tile), lambda n, e: (0, n)) for p in pieces]
            + [pl.BlockSpec((p.shape[0], tile), lambda n, e: (0, steps + n)) for p in pieces]
            + [pl.BlockSpec((p.shape[0], tile), lambda n, e: (0, 2 * steps + n)) for p in pieces],
            out_specs=[whole(x) for x in backs] + [column, column, column],
            scratch_shapes=[pltpu.VMEM((slots, width), F32), pltpu.VMEM((slots, 1), F32)]
            + [pltpu.VMEM((width, tile), BF16)] * 3,
        ),
        out_shape=backs + [thin, thin, thin],
        compiler_params=pltpu.CompilerParams(vmem_limit_bytes=VMEM),
        cost_estimate=COST,
        name="expert",
    )(expert, rows, gs, gate, pos_t, *pieces, *pieces, *pieces)
    return outs[: len(heights)], outs[len(heights) :]


def result_kernel(count, pieces, wide, me, gact, pos_t, *refs):
    parts, outs, wd = refs[:pieces], refs[pieces : pieces + count], refs[-1]
    tok = pos_t.shape[0]
    n = pl.program_id(0)
    blocks = wd.shape[0] // wide // pl.num_programs(0)

    @pl.when(n == 0)
    def _():
        for at, w in zip(spans(parts), parts, strict=True):
            wd[at, :] = w[...]

    step = blocks * wide
    here = wd[pl.ds(pl.multiple_of(n * step, step), step), :]
    y = mm(gact[...], here, ((1,), (1,))).astype(BF16)
    for b, (i, at) in enumerate(blocks_of(outs, tok)):
        part = y[b * CAP : (b + 1) * CAP, :]
        part = mm(onehot_back(pos_t, b), part, ((1,), (0,))).astype(BF16)
        for k in range(blocks):
            to = pl.multiple_of((me[0] ^ (blocks * n + k)) * wide, wide)
            outs[i][at : at + tok, pl.ds(to, wide)] = part[:, k * wide : (k + 1) * wide]


def result(gact, pos_t, pieces, count, me):
    slots, ff = gact.shape
    width = sum(p.shape[0] for p in pieces)
    wide = width // lax.axis_size("dp")
    tile = max(wide, min(512, width))
    last = (pieces[0].shape[1] - ff) // ff
    out = jax.ShapeDtypeStruct((pos_t.shape[1] // count * pos_t.shape[0], width), BF16)
    return pl.pallas_call(
        functools.partial(result_kernel, count, len(pieces), wide),
        grid_spec=pltpu.PrefetchScalarGridSpec(
            num_scalar_prefetch=1,
            grid=(width // tile,),
            in_specs=[
                pl.BlockSpec((slots, ff), lambda n, me: (0, 0)),
                pl.BlockSpec(pos_t.shape, lambda n, me: (0, 0)),
            ]
            + [pl.BlockSpec((p.shape[0], ff), lambda n, me: (0, last)) for p in pieces],
            out_specs=[pl.BlockSpec(out.shape, lambda n, me: (0, 0))] * count,
            scratch_shapes=[pltpu.VMEM((width, ff), BF16)],
        ),
        out_shape=[out] * count,
        compiler_params=pltpu.CompilerParams(vmem_limit_bytes=VMEM),
        cost_estimate=COST,
        name="result",
    )(me, gact, pos_t, *pieces)


def grads_kernel(count, rows, cuts, *refs):
    ins, outs = refs[: 5 * count], list(refs[5 * count :])
    ff = ins[2].shape[1]
    for b, cut in enumerate(cuts):
        at = slice(b * rows, (b + 1) * rows)
        gate = up = down = 0.0
        for c in range(count):
            tall, gs, dg, du, gact = ins[5 * c : 5 * c + 5]
            gate = gate + mm(tall[:, at], dg[...], ((0,), (0,)))
            up = up + mm(tall[:, at], du[...], ((0,), (0,)))
            down = down + mm(gs[:, at], gact[...], ((0,), (0,)))
        for start, stop in zip(cut[:-1], cut[1:], strict=True):
            out = outs.pop(0)
            out[:, :ff] = gate[start:stop].astype(BF16)
            out[:, ff : 2 * ff] = up[start:stop].astype(BF16)
            out[:, 2 * ff :] = down[start:stop].astype(BF16)


def grads(chunks, first, rows, cuts):
    ff = chunks[0][2].shape[1]
    blocks = len(cuts)
    specs, ins = [], []
    for chunk in chunks:
        slots = chunk[0].shape[0]
        tall = pl.BlockSpec((slots, blocks * rows), lambda i: (0, first // blocks))
        flat = pl.BlockSpec((slots, ff), lambda i: (0, 0))
        specs += [tall, tall, flat, flat, flat]
        ins += list(chunk)
    heights = [b - a for cut in cuts for a, b in zip(cut[:-1], cut[1:], strict=True)]
    return pl.pallas_call(
        functools.partial(grads_kernel, len(chunks), rows, cuts),
        grid=(1,),
        in_specs=specs,
        out_specs=[pl.BlockSpec((h, 3 * ff), lambda i: (0, 0)) for h in heights],
        out_shape=[jax.ShapeDtypeStruct((h, 3 * ff), BF16) for h in heights],
        compiler_params=pltpu.CompilerParams(vmem_limit_bytes=VMEM),
        cost_estimate=COST,
        name="grads",
    )(*ins)


def add_pieces_kernel(keep, *refs):
    pieces, out = refs[:-1], refs[-1]
    for at, p in zip(spans(pieces), pieces, strict=True):
        out[at, :] = (keep[at, :].astype(F32) + p[...].astype(F32)).astype(BF16)


def add_pieces(keep, pieces):
    whole = lambda x: pl.BlockSpec(x.shape, lambda i: (0, 0))
    return pl.pallas_call(
        add_pieces_kernel,
        grid=(1,),
        in_specs=[whole(x) for x in (keep, *pieces)],
        out_specs=whole(keep),
        out_shape=jax.ShapeDtypeStruct(keep.shape, BF16),
        compiler_params=pltpu.CompilerParams(vmem_limit_bytes=VMEM),
        cost_estimate=COST,
        name="add_pieces",
    )(keep, *pieces)


def attn_grads_kernel(me, a, d, *rest):
    k = d.shape[1]
    out = rest[-1]
    out[:, :k] = mm(a[...], d[...], ((0,), (0,))).astype(BF16)
    if len(rest) > 1:
        out[:, k:] = rest[0][...]


def attn_grads(a, d, extra, me, first, stride):
    rows, width = a.shape
    n = lax.axis_size("dp")
    tile = width // n
    count = n // stride
    at = lambda i, me: me[0] ^ (first + stride * i)
    k = d.shape[1] + sum(e.shape[1] for e in extra)
    return pl.pallas_call(
        attn_grads_kernel,
        grid_spec=pltpu.PrefetchScalarGridSpec(
            num_scalar_prefetch=1,
            grid=(count,),
            in_specs=[
                pl.BlockSpec((rows, tile), lambda i, me: (0, at(i, me))),
                pl.BlockSpec(d.shape, lambda i, me: (0, 0)),
            ]
            + [pl.BlockSpec((tile, e.shape[1]), lambda i, me: (at(i, me), 0)) for e in extra],
            out_specs=pl.BlockSpec((tile, k), lambda i, me: (i, 0)),
        ),
        out_shape=jax.ShapeDtypeStruct((count * tile, k), BF16),
        compiler_params=pltpu.CompilerParams(vmem_limit_bytes=VMEM),
        cost_estimate=COST,
        name="attn_grads",
    )(me, a, d, *extra)


def halves(held, rows):
    n = lax.axis_size("dp")
    wide = held.shape[1] // 256 * 128
    out = []
    for left, right, order in (
        (0, wide, bits_of(2, n)),
        (wide, held.shape[1], bits_of(2, n)[::-1]),
    ):
        side = {2 * i: held[i * rows : (i + 1) * rows, left:right] for i in range(n // 2)}
        out.append((side, order))
    return out


def stage(at, sides, step):
    for s, (side, order) in enumerate(sides):
        keys = sorted(r for r in side if r & order[step])
        v = [side[r] for r in keys]
        at[SIDE, s] = flip(jnp.concatenate(v, axis=0) if len(v) > 1 else v[0], order[step])


def unstage(at, sides, step):
    out = []
    for s, (side, order) in enumerate(sides):
        bit = order[step]
        keys = sorted(r for r in side if r & bit)
        rows = side[0].shape[0]
        got = at[SIDE, s]
        kept = {r: v for r, v in side.items() if not r & bit}
        for i, r in enumerate(keys):
            kept[r ^ bit] = add(kept[r ^ bit], got[i * rows : (i + 1) * rows])
        out.append((kept, order))
    return out


def spread(first, n):
    local = len(first)
    have = {(0, e): v for e, v in first.items()}
    for bit in bits_of(1, local):
        for key in sorted(key for key in have if key[1] & bit):
            have[(key[0] ^ bit, key[1] ^ bit)] = flip(have.pop(key), bit)
    for bit in bits_of(local, n):
        for key in sorted(have):
            have[(key[0] ^ bit, 0)] = flip(have[key], bit)
    return [have[key] for key in sorted(have)]


def gather_back(held, local, n):
    held = dict(held)
    for bit in reversed(bits_of(local, n // 2)):
        for r in sorted(r for r in held if r & bit):
            held[r ^ bit] = add(held[r ^ bit], flip(held.pop(r), bit))
    have = {(r, 0): v for r, v in held.items()}
    for bit in reversed(bits_of(1, local)):
        for key in sorted(key for key in have if key[0] & bit):
            have[(key[0] ^ bit, key[1] ^ bit)] = flip(have.pop(key), bit)
    return {e: v for (_, e), v in have.items()}


def per_row(row):
    return jnp.broadcast_to(row, (row.shape[1], row.shape[1])).T


def turn(v, cos, sin):
    return v * cos + pltpu.roll(v, v.shape[1] // 2, 1) * sin


def softmax_rows(qr, kr, same, scale):
    s = jnp.where(same, mm(qr, kr, ((1,), (1,))) * scale, -1e30)
    e = jnp.exp(s - jnp.max(s, axis=1, keepdims=True))
    return e / jnp.sum(e, axis=1, keepdims=True)


def attend_kernel(scale, qkv, r, gains, cos, sin, seg, qr_out, kr_out, vb_out, o_out):
    cols = o_out.shape[1]
    rq, rk = per_row(r[0, 0:1, :]), per_row(r[0, 1:2, :])
    seg_row = seg[0]
    same = per_row(seg_row) == seg_row
    for h in range(cols // HEAD_DIM):
        at = slice(h * HEAD_DIM, (h + 1) * HEAD_DIM)
        k_at = slice(cols + h * HEAD_DIM, cols + (h + 1) * HEAD_DIM)
        v_at = slice(2 * cols + h * HEAD_DIM, 2 * cols + (h + 1) * HEAD_DIM)
        qr = turn(qkv[:, at] * rq * gains[0:1, at], cos[...], sin[...]).astype(BF16)
        kr = turn(qkv[:, k_at] * rk * gains[1:2, at], cos[...], sin[...]).astype(BF16)
        vb = qkv[:, v_at].astype(BF16)
        p = softmax_rows(qr, kr, same, scale)
        qr_out[:, at] = qr
        kr_out[:, at] = kr
        vb_out[:, at] = vb
        o_out[:, at] = mm(p.astype(BF16), vb, ((1,), (0,))).astype(BF16)


def attend(qkv, r, gains, cos, sin, seg):
    total, cols = qkv.shape[0], qkv.shape[1] // 3
    zs, tok = seg.shape[0], seg.shape[2]
    tall = lambda w: pl.BlockSpec((tok, w), lambda b: (b, 0))
    fixed = lambda x: pl.BlockSpec(x.shape, lambda b: (0, 0))
    thin = jax.ShapeDtypeStruct((total, cols), BF16)
    return pl.pallas_call(
        functools.partial(attend_kernel, HEAD_DIM ** (-0.5)),
        grid=(zs,),
        in_specs=[
            tall(qkv.shape[1]),
            pl.BlockSpec((1, 2, tok), lambda b: (b, 0, 0)),
            fixed(gains),
            tall(HEAD_DIM),
            tall(HEAD_DIM),
            pl.BlockSpec((1, 1, tok), lambda b: (b, 0, 0)),
        ],
        out_specs=[tall(cols)] * 4,
        out_shape=[thin] * 4,
        compiler_params=pltpu.CompilerParams(vmem_limit_bytes=VMEM),
        cost_estimate=COST,
        name="attend",
    )(qkv, r, gains, cos, sin, seg)


def attend_back_kernel(
    scale, dhb, wo, q, k, qr, kr, vb, gains, cos, sin, seg, dq_out, dk_out, dv_out, sums
):
    cols = wo.shape[0]
    seg_row = seg[0]
    same = per_row(seg_row) == seg_row
    do_all = mm(dhb[...], wo[...], ((1,), (1,))).astype(BF16)
    sum_q = sum_k = 0.0
    for h in range(cols // HEAD_DIM):
        at = slice(h * HEAD_DIM, (h + 1) * HEAD_DIM)
        do = do_all[:, at]
        p = softmax_rows(qr[:, at], kr[:, at], same, scale)
        dp = mm(do, vb[:, at], ((1,), (1,)))
        ds = (p * (dp - jnp.sum(p * dp, axis=1, keepdims=True))).astype(BF16)
        dv_out[:, at] = mm(p.astype(BF16), do, ((0,), (0,))).astype(BF16)
        dq = turn(mm(ds, kr[:, at], ((1,), (0,))) * scale, cos[...], -sin[...])
        dk = turn(mm(ds, qr[:, at], ((0,), (0,))) * scale, cos[...], -sin[...])
        dq_out[:, at] = dq
        dk_out[:, at] = dk
        sum_q = sum_q + jnp.sum(q[:, at] * gains[0:1, at] * dq, axis=1, keepdims=True)
        sum_k = sum_k + jnp.sum(k[:, at] * gains[1:2, at] * dk, axis=1, keepdims=True)
    tok = dhb.shape[0]
    sums[0, 0:1, :] = jnp.broadcast_to(sum_q, (tok, tok)).T[0:1, :]
    sums[0, 1:2, :] = jnp.broadcast_to(sum_k, (tok, tok)).T[0:1, :]


def attend_back(dhb, wo, qkv, qr, kr, vb, gains, cos, sin, seg):
    total, cols = qkv.shape[0], wo.shape[0]
    zs, tok = seg.shape[0], seg.shape[2]
    tall = lambda w, at=0: pl.BlockSpec((tok, w), lambda b: (b, at))
    fixed = lambda x: pl.BlockSpec(x.shape, lambda b: (0, 0))
    wide = jax.ShapeDtypeStruct((total, cols), F32)
    return pl.pallas_call(
        functools.partial(attend_back_kernel, HEAD_DIM ** (-0.5)),
        grid=(zs,),
        in_specs=[
            tall(dhb.shape[1]),
            fixed(wo),
            tall(cols, 0),
            tall(cols, 1),
            tall(cols),
            tall(cols),
            tall(cols),
            fixed(gains),
            tall(HEAD_DIM),
            tall(HEAD_DIM),
            pl.BlockSpec((1, 1, tok), lambda b: (b, 0, 0)),
        ],
        out_specs=[tall(cols)] * 3 + [pl.BlockSpec((1, 2, tok), lambda b: (b, 0, 0))],
        out_shape=[
            wide,
            wide,
            jax.ShapeDtypeStruct((total, cols), BF16),
            jax.ShapeDtypeStruct((zs, 2, tok), F32),
        ],
        compiler_params=pltpu.CompilerParams(vmem_limit_bytes=VMEM),
        cost_estimate=COST,
        name="attend_back",
    )(dhb, wo, qkv, qkv, qr, kr, vb, gains, cos, sin, seg)


def join_back_kernel(q, k, dqn, dkn, dv, r, means, gains, out, gain_out):
    cols = dv.shape[1]
    for at, v, d in ((0, q, dqn), (1, k, dkn)):
        rr = per_row(r[0, at : at + 1, :])
        mean = per_row(means[0, at : at + 1, :])
        part = []
        for h in range(cols // HEAD_DIM):
            to = slice(h * HEAD_DIM, (h + 1) * HEAD_DIM)
            vr = v[:, to] * rr
            out[:, at * cols + h * HEAD_DIM : at * cols + (h + 1) * HEAD_DIM] = (
                rr * (gains[at : at + 1, to] * d[:, to]) - vr * (rr * rr) * mean
            ).astype(BF16)
            part.append(jnp.sum(d[:, to] * vr, axis=0, keepdims=True))
        row = jnp.concatenate(part, axis=1)

        @pl.when(pl.program_id(0) == 0)
        def _():
            gain_out[at : at + 1, :] = row

        @pl.when(pl.program_id(0) > 0)
        def _():
            gain_out[at : at + 1, :] += row

    out[:, 2 * cols :] = dv[...]


def join_back(qkv, dqn, dkn, dv, r, means, gains):
    total, cols = dv.shape
    zs, tok = r.shape[0], r.shape[2]
    tall = lambda w, at=0: pl.BlockSpec((tok, w), lambda b: (b, at))
    row = pl.BlockSpec((1, 2, tok), lambda b: (b, 0, 0))
    return pl.pallas_call(
        join_back_kernel,
        grid=(zs,),
        in_specs=[tall(cols, 0), tall(cols, 1), tall(cols), tall(cols), tall(cols), row, row]
        + [pl.BlockSpec(gains.shape, lambda b: (0, 0))],
        out_specs=[tall(3 * cols), pl.BlockSpec((2, cols), lambda b: (0, 0))],
        out_shape=[
            jax.ShapeDtypeStruct((total, 3 * cols), BF16),
            jax.ShapeDtypeStruct((2, cols), F32),
        ],
        compiler_params=pltpu.CompilerParams(vmem_limit_bytes=VMEM),
        cost_estimate=COST,
        name="join_back",
    )(qkv, qkv, dqn, dkn, dv, r, means, gains)


def first_back_kernel(d, w, x, r, da, gain):
    back = mm(d[...], w[...], ((1,), (1,)))
    da[...] = back.astype(BF16)
    row = jnp.sum(back * (x[...].astype(F32) * r[...]), axis=0, keepdims=True)

    @pl.when(pl.program_id(0) == 0)
    def _():
        gain[...] = row

    @pl.when(pl.program_id(0) > 0)
    def _():
        gain[...] += row


def first_back(d, w, x, r, tok):
    total, width = x.shape
    k = d.shape[1]
    return pl.pallas_call(
        first_back_kernel,
        grid=(total // tok,),
        in_specs=[
            pl.BlockSpec((tok, k), lambda b: (b, 0)),
            pl.BlockSpec((width, k), lambda b: (0, 0)),
            pl.BlockSpec((tok, width), lambda b: (b, 0)),
            pl.BlockSpec((tok, 1), lambda b: (b, 0)),
        ],
        out_specs=[
            pl.BlockSpec((tok, width), lambda b: (b, 0)),
            pl.BlockSpec((1, width), lambda b: (0, 0)),
        ],
        out_shape=[
            jax.ShapeDtypeStruct((total, width), BF16),
            jax.ShapeDtypeStruct((1, width), F32),
        ],
        compiler_params=pltpu.CompilerParams(vmem_limit_bytes=VMEM),
        cost_estimate=COST,
        name="first_back",
    )(d, w, x, r)


def form_kernel(count, own, *refs):
    ins, (gate_up, down) = refs[:count], refs[-2:]
    wide = gate_up.shape[2]
    for o in range(count):

        @pl.when(own[0] == o)
        def _():
            for e in range(count):
                gate_up[:, e, :] = ins[o ^ e][:, :wide].astype(F32)
                down[:, e, :] = ins[o ^ e][:, wide:].astype(F32)


def form(blocks, own, rows, start, stop, before=()):
    k = blocks[0][0].shape[1]
    count, ff, tile = len(blocks), k // 3, 32

    def spec(at):
        return pl.BlockSpec((tile, k), lambda i, o: (i + (start - at) // tile, 0))

    shapes = [
        jax.ShapeDtypeStruct((rows, count, 2 * ff), F32),
        jax.ShapeDtypeStruct((rows, count, ff), F32),
    ]
    outs = [
        pl.BlockSpec((tile, *s.shape[1:]), lambda i, o: (i + start // tile, 0, 0)) for s in shapes
    ]
    return pl.pallas_call(
        functools.partial(form_kernel, count),
        grid_spec=pltpu.PrefetchScalarGridSpec(
            num_scalar_prefetch=1,
            grid=((stop - start) // tile,),
            in_specs=[spec(at) for _, at in blocks]
            + [pl.BlockSpec(memory_space=pl.ANY)] * len(before),
            out_specs=outs,
        ),
        out_shape=shapes,
        input_output_aliases={1 + count + n: n for n in range(len(before))},
        compiler_params=pltpu.CompilerParams(vmem_limit_bytes=VMEM),
        cost_estimate=COST,
        name="form",
    )(own, *[v for v, _ in blocks], *before)


def extra_kernel(zat, router, attn, qk, ffn, out, rows):
    experts, cols = router.shape[0], qk.shape[1]
    rows[...] = jnp.zeros_like(rows)
    rows[:experts, :] = router[...]
    rows[experts : experts + 1, :] = attn[...]
    at = pl.ds(pl.multiple_of(zat[0] * cols, cols), cols)
    rows[experts + 1 : experts + 3, at] = qk[...]
    rows[experts + 3 : experts + 4, :] = ffn[...]
    out[...] = rows[...].T.astype(BF16)


def extra_columns(router, attn, qk, ffn, zat):
    width = attn.shape[1]
    whole = lambda x: pl.BlockSpec(x.shape, lambda i, z: (0, 0))
    out = jax.ShapeDtypeStruct((width, EXTRA), BF16)
    return pl.pallas_call(
        extra_kernel,
        grid_spec=pltpu.PrefetchScalarGridSpec(
            num_scalar_prefetch=1,
            grid=(1,),
            in_specs=[whole(x) for x in (router, attn, qk, ffn)],
            out_specs=whole(out),
            scratch_shapes=[pltpu.VMEM((EXTRA, width), F32)],
        ),
        out_shape=out,
        compiler_params=pltpu.CompilerParams(vmem_limit_bytes=VMEM),
        cost_estimate=COST,
        name="extra_columns",
    )(zat, router, attn, qk, ffn)


def inv_rms(v):
    return lax.rsqrt(jnp.mean(v * v, axis=-1, keepdims=True) + EPSILON)


def rms_back(v, r, gain, c):
    gc = gain * c
    return r * gc - v * (r * r * r) * jnp.mean(v * gc, axis=-1, keepdims=True)


def places_and_tables(at, dp, zs, rows):
    dealt = lax.dynamic_slice_in_dim(at[ORDER], dp * zs * SEQ_DEV, zs * SEQ_DEV)
    lens = jnp.take(at[LENGTHS], dealt).reshape(zs, SEQ_DEV)
    ends = jnp.cumsum(lens, axis=1)
    places = jnp.arange(rows, dtype=jnp.int32)
    segment = jnp.sum((places[None, :, None] >= ends[:, None, :]).astype(jnp.int32), axis=2)
    starts = ends - lens
    offset = jnp.sum(
        jnp.where(
            segment[:, :, None] == jnp.arange(SEQ_DEV, dtype=jnp.int32), starts[:, None, :], 0
        ),
        axis=2,
    )
    half = HEAD_DIM // 2
    inverse = ROPE_BASE ** (-2.0 * jnp.arange(half, dtype=F32) / HEAD_DIM)
    turned = (places[None] - offset).astype(F32)[..., None] * inverse
    at[COS] = jnp.tile(jnp.cos(turned), (1, 1, 2)).reshape(zs * rows, HEAD_DIM)
    sin = jnp.sin(turned)
    at[SIN] = jnp.concatenate([-sin, sin], axis=2).reshape(zs * rows, HEAD_DIM)
    at[SEG] = segment.astype(F32)[:, None, :]


def on_device(
    tokens,
    lengths,
    permutation,
    routes,
    norm_gains,
    w_qkv,
    w_out,
    router,
    w_gate_up,
    w_down,
    cotangent,
):
    rows, width = tokens.shape
    zs = lax.axis_size("expert")
    dps = lax.axis_size("dp")
    z = lax.axis_index("expert")
    dp = lax.axis_index("dp")
    local = w_gate_up.shape[1]
    ff = w_down.shape[2]
    experts = router.shape[1]
    own_rows = w_qkv.shape[0]
    e_rows = w_gate_up.shape[0]
    cols = width // zs
    expert = z * local + lax.rem(dp, local)
    own = lax.rem(dp, local)
    top = local // 2
    far_bit = dps // 2
    mid = zs // 2
    laid_out = local == 4 and dps == 8
    me_at = jnp.reshape(dp, (1,)).astype(jnp.int32)
    expert_at = jnp.stack([expert, dp, jnp.int32(experts)]).astype(jnp.int32)
    at = Flow()

    extra = jnp.concatenate(
        [router, norm_gains, jnp.zeros((own_rows, EXTRA - experts - 4), BF16)], axis=1
    )
    sent = jnp.stack(
        [
            jnp.concatenate(
                [w_qkv[:, i * width + e * cols : i * width + (e + 1) * cols] for i in range(3)]
                + [extra],
                axis=1,
            )
            for e in range(zs)
        ]
    )
    at[MINE] = lax.all_to_all(sent, "expert", split_axis=0, concat_axis=0, tiled=True)
    moved = [(b, (b % dps) * zs + b // dps) for b in range(dps * zs)]

    for e in range(local):
        at[W, 0, e] = jnp.concatenate(
            [pick(w_gate_up, own ^ e, 1), pick(w_down, own ^ e, 1)], axis=1
        )
    at[X, 0] = tokens
    at[OUT] = w_out
    at.fence(MINE, (X, 0), OUT, *at.having(W))

    at[ATTN] = lax.all_gather(
        at[MINE].reshape(zs * own_rows, 3 * cols + EXTRA), "dp", axis=0, tiled=True
    )
    if laid_out:
        at[W, 1, 0] = flip(at[W, 0, 1], 1)
        at[W, 1, 2] = flip(at[W, 0, 3], 1)
    at[LENGTHS], at[ORDER], at[ROUTES], at[COT] = lengths, permutation, routes, cotangent
    for i in range(1, zs):
        at[X, i] = hop(at[X, i - 1])
        if i == 1:
            at.fence((X, 1), LENGTHS, ORDER, ROUTES, COT, OUT)
            places_and_tables(at, dp, zs, rows)
        elif i == 2:
            at.fence((X, 2), COS, SIN, SEG, ROUTES, COT)
            at[MASK] = jnp.sum(
                (at[ROUTES][:, :, None] == jnp.arange(experts, dtype=jnp.int32)).astype(BF16),
                axis=1,
            )
            mask_pad = jnp.concatenate(
                [at[MASK], jnp.zeros((rows, EXTRA - experts), BF16)], axis=1
            )
            at[G, 0] = jnp.concatenate([at[COT], mask_pad], axis=1)
            at[OUT] = lax.ppermute(at[OUT], ("dp", "expert"), moved)
        else:
            at.fence((X, i))
    xs = [(X, i) for i in range(zs)]
    at.fence(ATTN, OUT, (G, 0), MASK, *xs, *at.having(W))

    cut = e_rows // 4
    if laid_out:
        at[W, 2, 0] = flip(at[W, 0, 2], 2)
        at[W, 4, 0] = flip(at[W, 0, 0], 4)
    at[G, 1] = hop(at[G, 0])
    out_w = lax.all_gather(at[OUT], "dp", axis=0, tiled=True)
    attn_w = at[ATTN]
    qkv_w = attn_w[:, : 3 * cols]
    router_full = attn_w[:, 3 * cols : 3 * cols + experts]
    gains = attn_w[:, 3 * cols + experts : 3 * cols + experts + 4].astype(F32).T
    router_t = router_full.T
    x_all = by_line([at[key] for key in xs])
    xf = x_all.astype(F32)
    r_attn = inv_rms(xf)
    a_all = (xf * r_attn * gains[0]).astype(BF16)
    at[QKV] = nn(a_all, qkv_w)
    at.fence(QKV, (G, 1))
    qkv = at[QKV]
    q, k = qkv[:, :cols], qkv[:, cols : 2 * cols]
    at[SQUARES] = lax.psum(
        jnp.stack([jnp.sum(q * q, axis=1), jnp.sum(k * k, axis=1)]), "expert"
    )
    at.fence(SQUARES, (G, 1))
    at[G, 2] = hop(at[G, 1])
    by_block = lambda v: v.reshape(2, zs, rows).transpose(1, 0, 2)
    r_qk = by_block(lax.rsqrt(at[SQUARES] / width + EPSILON))
    gain_qk = lax.dynamic_slice_in_dim(gains[1:3], z * cols, cols, axis=1)
    cos, sin, seg = at[COS], at[SIN], at[SEG]
    qr, kr, vb, o = attend(qkv, r_qk, gain_qk, cos, sin, seg)
    at[ADDED] = nn(o, out_w, BF16)
    at.fence(ADDED, (G, 2), *(w for w in at.having(W) if laid_out))
    at[ADDED] = lax.psum_scatter(at[ADDED], "expert", scatter_dimension=0, tiled=True)
    for i in range(3, zs):
        at[G, i] = hop(at[G, i - 1])
    if laid_out:
        at[W, 3, 0] = flip(at[W, 1, 2], 2)
        at[W, 5, 0] = flip(at[W, 1, 0], 4)
        at[WA, 6] = flip(at[W, 2, 0][: 11 * cut // 4], 4)
    first_g = [(G, i) for i in range(mid)]
    last_g = [(G, i) for i in range(mid, zs)]
    at[FAR_GA] = flip(jnp.concatenate([at[key] for key in first_g], axis=0), top)
    weight_keys = at.having(W) + at.having(WA)
    at.fence(ADDED, FAR_GA, (G, zs - 1), *(w for w in weight_keys if laid_out))
    marks = (0, 3 * cut // 4, 9 * cut // 4, e_rows)
    hid = tokens.astype(F32) + at[ADDED].astype(F32)
    r_ffn = inv_rms(hid)
    m = (hid * r_ffn * gains[3]).astype(BF16)

    at[M, 0] = m
    mine_e = (jnp.arange(experts) == expert).astype(F32)

    def chunk_places(kind, parts):
        masks = jnp.concatenate([x[:, width : width + experts] for x in parts], axis=0)
        masks = masks.astype(F32).reshape(-1, rows, experts)
        on = jnp.sum(masks * mine_e, axis=2)
        pos = jnp.where(on > 0, jnp.cumsum(on, axis=1) - 1.0, -1.0).astype(jnp.int32)
        at[kind, 0], at[kind, 1], at[kind, 2] = pos, pos.T, masks.transpose(0, 2, 1)
        out = jax.ShapeDtypeStruct((pos.shape[0] * CAP, width), BF16)
        (at[kind, 3],) = pick_rows(gather_cot_kernel, "gather_cot", parts, [pos], [out], expert_at)

    waiting = [(G, key) for key in last_g] + [(M, (M, i)) for i in range(zs)]
    near_cores = [fan([m], top)[1:]]
    for i in range(1, zs):
        at[M, i] = hop(at[M, i - 1])
        kind, key = waiting.pop(0)
        at[FAR, *key] = flip(at[key], top)
        beside = [(FAR, *key)]
        if laid_out:
            at[WB, i] = flip(at[W, 3, 0][marks[i - 1] : marks[i]], 4)
            beside.append((WB, i))
            if i == 1:
                at[WA, 7] = flip(at[W, 2, 0][11 * cut // 4 :], 4)
                beside.append((WA, 7))
        if i == 1:
            g_near = [jnp.concatenate([at[key] for key in first_g + last_g], axis=0)]
            chunk_places(NEAR, [x for xs in fan(g_near, top) for x in xs])
        if i == 2:
            beside += at.having(NEAR)
        if i == zs - 1:
            g_far = [at[FAR_GA], *[at[FAR, *k] for k in last_g]]
            chunk_places(DISTANT, [x for xs in fan(g_far, top) for x in xs])
            beside += at.having(DISTANT)
        at.fence((M, i), *beside)
        near_cores.append(fan([at[M, i]], top)[1:])
    key = waiting.pop(0)[1]
    at[FAR, *key] = flip(at[key], top)

    def chunk_gather(kind, blocks, cores):
        flat = [*blocks, *(x[0] for d in range(top - 1) for x in (c[d] for c in cores))]
        slots = at[kind, 0].shape[0] * CAP
        outs = [
            jax.ShapeDtypeStruct((slots, width), BF16),
            jax.ShapeDtypeStruct((slots, 1), F32),
        ]
        others = [at[kind, 0], at[kind, 2], router_t]
        picked, gate = pick_rows(gather_kernel, "gather", flat, others, outs, expert_at)
        return picked, at[kind, 3], gate

    def chunk_expert(kind, groups, got):
        heights = [h for group in groups for h in group]
        backs, outs = run_expert(*got, at[kind, 1], weights, expert_at, heights, ff)
        back = []
        for group in groups:
            back.append(backs[: len(group)])
            backs = backs[len(group) :]
        return back, (got[0], got[1], *outs)

    ms = [at[M, i] for i in range(zs)]
    near_rows = chunk_gather(NEAR, ms, near_cores)
    for i, v in enumerate(near_rows):
        at[ROWS, i] = v
    at.fence(*at.having(ROWS), (FAR, *key))
    while waiting:
        key = waiting.pop(0)[1]
        at[FAR, *key] = flip(at[key], top)
    if laid_out:
        keys = [(W, r, 0) for r in range(6)] + [(WA, 6), (WA, 7), (WB, 1), (WB, 2), (WB, 3)]
        weights = [at[key] for key in keys]
    else:
        weights = spread({e: at[W, 0, e] for e in range(local)}, dps)
    own_heights = [rows] * zs
    near_back, near_outs = chunk_expert(
        NEAR, [own_heights] + [[zs * rows]] * (top - 1), [at[ROWS, i] for i in range(3)]
    )
    far_ms = [(FAR, M, i) for i in range(zs)]
    at[NEAR_GACT] = near_outs[4]
    at.fence(NEAR_GACT, *far_ms)
    ms = [at[key] for key in far_ms]
    far_rows = chunk_gather(DISTANT, ms, [fan([v], top)[1:] for v in ms])
    far_back, far_outs = chunk_expert(
        DISTANT, [own_heights] + [[mid * rows, (zs - mid) * rows]] * (top - 1), far_rows
    )
    near_outs = (*near_outs[:4], at[NEAR_GACT])

    quarter = dps // 4
    near_sum = fold(near_back)
    far_sum = fold(far_back)
    chunk_keys = [(C, n) for n in range(10)]
    for key, v in zip(chunk_keys, (*near_outs, *far_outs), strict=True):
        at[key] = v
    for i, v in enumerate(far_sum):
        at[BACKS, i] = v
    at.fence(*at.having(BACKS), *chunk_keys)

    halves_cut = [(0, e_rows // 2, e_rows) if laid_out else (0, e_rows)] * quarter

    def chunk_grads(kind, first, cuts):
        c = [at[key] for key in chunk_keys]
        made = list(grads([c[:5], c[5:]], first, e_rows, cuts))
        for row, cut in enumerate(cuts):
            for start in cut[:-1]:
                at[kind, row, start] = made.pop(0)

    def send_part(key, row, start):
        at[PIECE, key, row, start] = flip(at[key, row, start], far_bit)

    def sum_row(keep, key, row):
        starts = sorted(k[2] for k in at.having(key) if k[1] == row)
        if not laid_out:
            send_part(key, row, 0)
        return add_pieces(at[keep, row, 0], [at[PIECE, key, row, start] for start in starts])

    whole_cut = [(0, e_rows)] * quarter
    last = zs - 1

    at[THERE] = flip(at[BACKS, last], top)
    chunk_grads(SEND_HIGH, 3 * quarter, halves_cut)
    at.fence(THERE, *at.having(SEND_HIGH), *chunk_keys)
    half = e_rows // 2
    early, most = 3 * e_rows // 8, 3 * e_rows // 4
    for i in reversed(range(zs)):
        here = near_sum[i].astype(F32) + at[THERE].astype(F32)
        if i < last:
            here = here + at[ACC].astype(F32)
        at[ACC] = here.astype(BF16)
        if not i:
            break
        at[ACC] = hop(at[ACC], -1)
        at[THERE] = flip(at[BACKS, i - 1], top)
        beside = []
        if i == last:
            if laid_out:
                send_part(SEND_HIGH, 0, 0)
            for n, y in enumerate(result(at[C, 9], at[DISTANT, 1], weights, top, me_at)):
                at[Y_PART, n] = y
            beside = [*at.having(Y_PART), *at.having(PIECE)]
        if i == last - 1:
            for n, y in enumerate(result(at[C, 4], at[NEAR, 1], weights, top, me_at)):
                at[NEAR_PART, n] = y
            if laid_out:
                send_part(SEND_HIGH, 0, half)
            beside = [*at.having(NEAR_PART), *at.having(PIECE)]
        if i == last - 2:
            if laid_out:
                send_part(SEND_HIGH, 1, 0)
            low_cut = halves_cut
            if laid_out:
                low_cut = [halves_cut[0], (0, e_rows - early, e_rows)]
            chunk_grads(SEND_LOW, 2 * quarter, low_cut)
            at[Y_FAR] = fold([[at[key]] for key in at.having(Y_PART)])[0]
            beside = [Y_FAR, *at.having(SEND_LOW), *at.having(PIECE)]
        at.fence(ACC, THERE, *beside, *chunk_keys)
    at.fence(ACC, *at.having(NEAR_PART))
    dm = at[ACC].astype(F32)
    at[Y_FAR] = flip(at[Y_FAR], top)
    if laid_out:
        send_part(SEND_HIGH, 1, half)
        send_part(SEND_LOW, 0, 0)

    own_mask = at[MASK].astype(F32)
    own_logits = jnp.where(own_mask > 0, nn(m, router_full), -1e30)
    own_e = jnp.where(
        own_mask > 0, jnp.exp(own_logits - jnp.max(own_logits, axis=1, keepdims=True)), 0.0
    )
    gate_own = own_e / jnp.sum(own_e, axis=1, keepdims=True)
    dgates = dm[:, width : width + experts] + dm[:, width + experts : width + 2 * experts]
    dz = (
        gate_own * (dgates - jnp.sum(gate_own * dgates, axis=1, keepdims=True))
    ).astype(BF16)
    dmt = nt(dz, router_full) + dm[:, :width]
    grad_out = cotangent.astype(F32)
    dh = grad_out + rms_back(hid, r_ffn, gains[3], dmt)
    at[DHB] = lax.all_gather(dh.astype(BF16), "expert", axis=0, tiled=True)
    router_part = tn(dz, m)
    gain_ffn = jnp.sum(dmt * hid * r_ffn, axis=0)
    at[Y_NEAR] = fold([[at[key]] for key in at.having(NEAR_PART)])[0]
    chunk_grads(KEEP_HIGH, quarter, whole_cut)
    if laid_out:
        for i in range(quarter):
            at[TAIL, quarter + i, 0] = sum_row(KEEP_HIGH, SEND_HIGH, i)
    chunk_grads(KEEP_LOW, 0, whole_cut)
    at[ROUTER], at[GAIN_FFN] = router_part, gain_ffn
    tails = at.having(TAIL)
    keeps = at.having(KEEP_LOW) + at.having(KEEP_HIGH) + at.having(SEND_LOW)
    at.fence(DHB, Y_FAR, Y_NEAR, ROUTER, GAIN_FFN, *keeps, *at.having(PIECE), *tails)
    dhb = at[DHB]
    if laid_out:
        at[TAIL, 0, 2] = flip(at[TAIL, 2, 0], 2)
        send_part(SEND_LOW, 0, half)
        send_part(SEND_LOW, 1, 0)
    if not laid_out:
        for i in range(quarter):
            at[TAIL, quarter + i, 0] = sum_row(KEEP_HIGH, SEND_HIGH, i)
    y_own = add(at[Y_NEAR], at[Y_FAR])
    at[Y] = lax.psum_scatter(
        by_line([y_own[i * rows : (i + 1) * rows] for i in range(zs)]),
        "expert",
        scatter_dimension=0,
        tiled=True,
    )

    dqn, dkn, dv, sums = attend_back(dhb, out_w, qkv, qr, kr, vb, gain_qk, cos, sin, seg)
    means = lax.psum(sums.reshape(-1, rows), "expert").reshape(zs, 2, rows) / width
    out_sum = Halving(at, OUT_GRAD, tn(o, dhb, BF16))
    dqkv, gains_qk = join_back(qkv, dqn, dkn, dv, r_qk, means, gain_qk)
    at[DQKV] = dqkv
    at.fence(DQKV, Y, *at.having(OUT_GRAD), *at.having(PIECE), *at.having(TAIL))
    out_sum.begin(1)

    at[ODD] = attn_grads(a_all, at[DQKV], [], me_at, 1, 2)
    at.fence(ODD, DQKV, *at.having(OUT_GRAD), *at.having(TAIL), *at.having(SEND_LOW))
    out_sum.end()
    out_sum.begin(far_bit)
    at[ODD] = flip(at[ODD], 1)
    if laid_out:
        at[HALF, 0] = flip(at[TAIL, 3, 0][:most], 2)
        send_part(SEND_LOW, 1, e_rows - early)
    at[DA], at[GAIN_ATTN] = first_back(at[DQKV], attn_w, x_all, r_attn, rows)
    even = attn_grads(a_all, at[DQKV], [], me_at, 0, 2)
    at[HELD] = add(even, at[ODD])
    at.fence(HELD, DQKV, DA, GAIN_ATTN, *at.having(OUT_GRAD), *at.having(HALF), *at.having(PIECE))
    at[DA] = lax.psum_scatter(at[DA], "expert", scatter_dimension=0, tiled=True)
    sides = halves(at[HELD], zs * own_rows)
    stage(at, sides, 0)
    out_sum.end()
    out_sum.begin(2)
    at[BESIDE] = extra_columns(
        at[ROUTER], at[GAIN_ATTN], gains_qk, at[GAIN_FFN][None], jnp.reshape(z, (1,))
    )
    for turn_ in range(1, len(bits_of(2, dps))):
        at.fence(*at.having(SIDE), BESIDE, *at.having(OUT_GRAD), *at.having(KEEP_LOW), *at.having(PIECE))
        out_sum.end()
        if laid_out:
            at[OUT_GRAD, 0] = lax.ppermute(
                at[OUT_GRAD, 0], ("dp", "expert"), [(b, a) for a, b in moved]
            )
        if turn_ < len(bits_of(2, dps)) - 1:
            out_sum.begin(2 << turn_)
        if turn_ == 1:
            small_sum = Halving(at, SMALL, at[BESIDE])
            small_sum.begin(1)
            for i in range(quarter):
                at[TAIL, i, 0] = sum_row(KEEP_LOW, SEND_LOW, i)
        sides = unstage(at, sides, turn_ - 1)
        stage(at, sides, turn_)
    at.fence(*at.having(SIDE), *at.having(SMALL), *at.having(TAIL))
    sides = unstage(at, sides, len(bits_of(2, dps)) - 1)
    at[BACK] = jnp.concatenate([sides[0][0][0], sides[1][0][0]], axis=1)
    at.fence(BACK, *at.having(OUT_GRAD), *at.having(SMALL), *at.having(HALF), *at.having(TAIL))
    small_sum.end()
    if not laid_out:
        at[OUT_GRAD, 0] = lax.ppermute(
            at[OUT_GRAD, 0], ("dp", "expert"), [(b, a) for a, b in moved]
        )
    at[BACK] = lax.all_to_all(
        at[BACK].reshape(zs, own_rows, 3 * cols),
        "expert",
        split_axis=0,
        concat_axis=0,
        tiled=True,
    )
    own_at = jnp.reshape(own, (1,))
    bits = bits_of(2, dps)
    small_sum.begin(bits[0])
    if laid_out:
        at[HALF, most] = flip(at[TAIL, 3, 0][most:], 2)
        at[TAIL, 0, 1] = flip(at[TAIL, 1, 0], 1)
        blocks = [(at[TAIL, 0, e], 0) for e in range(local - 1)]
        at[HALF, 0] = flip(at[HALF, 0], 1)
        at[GU], at[DN] = form([*blocks, (at[HALF, 0], 0)], own_at, e_rows, 0, most)
        at.fence(GU, DN, DA, *at.having(SMALL))
        blocks += [(flip(at[HALF, most], 1), most)]
        at[GU], at[DN] = form(blocks, own_at, e_rows, most, e_rows, (at[GU], at[DN]))
    else:
        rest = gather_back({k[1]: at[k] for k in at.having(TAIL)}, local, dps)
        at[GU], at[DN] = form([(rest[e], 0) for e in range(local)], own_at, e_rows, 0, e_rows)
    small_sum.end()
    for bit in bits[1:]:
        small_sum.begin(bit)
        small_sum.end()
    at.fence(BACK, GU, DN, *at.having(OUT_GRAD), *at.having(SMALL))
    grad_w_out = at[OUT_GRAD, 0].astype(F32)
    back = at[BACK].astype(F32)
    grad_w_qkv = jnp.concatenate(
        [back[e, :, i * cols : (i + 1) * cols] for i in range(3) for e in range(zs)], axis=1
    )
    place = place_in_ring(z, zs)
    blocks = at[SMALL, 0].reshape(zs, own_rows, EXTRA)
    extra_sum = pick(blocks, z, 0).astype(F32)
    for i in range(1, zs):
        to = at_place(lax.rem(place + i, zs), zs)
        extra_sum = extra_sum + hop(pick(blocks, to, 0), i).astype(F32)
    grad_router = extra_sum[:, :experts]
    grad_gains = extra_sum[:, experts : experts + 4]
    da = at[DA].astype(F32)

    output = hid + at[Y].astype(F32)
    x_own = tokens.astype(F32)
    grad_tokens = dh + rms_back(x_own, inv_rms(x_own), gains[0], da)
    return (
        output,
        grad_tokens,
        grad_gains,
        grad_w_qkv,
        grad_w_out,
        grad_router,
        at[GU],
        at[DN],
    )


def solution(mesh):
    both = P(("dp", "expert"), None)
    experts = P("dp", "expert", None)
    return jax.shard_map(
        on_device,
        mesh=mesh,
        in_specs=(both, P(), P(), both, both, both, both, both, experts, experts, both),
        out_specs=(both, both, both, both, both, both, experts, experts),
        check_vma=False,
    )
```

```python
import functools

import jax
import jax.numpy as jnp
from jax import lax
from jax.experimental import pallas as pl
from jax.experimental.pallas import tpu as pltpu
from jax.sharding import PartitionSpec as P

HEADS = 16
HEAD_DIM = 128
SEQ_DEV = 2
EPSILON = 1e-06
ROPE_BASE = 50000.0
CAP = 80
EXTRA = 128
VMEM = 56 * 2**20
COST = pl.CostEstimate(flops=10**6, bytes_accessed=10**5, transcendentals=0)

F32 = jnp.float32
BF16 = jnp.bfloat16


def dot(a, b, dims, out=F32):
    return lax.dot_general(a, b, (dims, ((), ())), preferred_element_type=F32).astype(out)


def nn(a, b, out=F32):
    return dot(a, b, ((1,), (0,)), out)


def nt(a, b, out=F32):
    return dot(a, b, ((1,), (1,)), out)


def tn(a, b, out=F32):
    return dot(a, b, ((0,), (0,)), out)


def flip(v, bit):
    return lax.ppermute(v, "dp", [(i, i ^ bit) for i in range(lax.axis_size("dp"))])


def ring(n):
    return [*range(0, n, 2), *reversed(range(1, n, 2))]


def hop(v, step=1):
    order = ring(lax.axis_size("expert"))
    n = len(order)
    pairs = [(order[i], order[(i + step) % n]) for i in range(n)]
    return lax.ppermute(v, "expert", pairs)


def gather_ring(v):
    return [v] + [hop(v, i) for i in range(1, lax.axis_size("expert"))]


def place_in_ring(i, n):
    half = i // 2
    return jnp.where(i % 2 == 0, half, n - 1 - half) if not isinstance(i, int) else (
        half if i % 2 == 0 else n - 1 - half
    )


def at_place(p, n):
    return jnp.where(p < (n + 1) // 2, 2 * p, 2 * (n - 1 - p) + 1)


def by_line(blocks):
    n = len(blocks)
    mine = place_in_ring(lax.axis_index("expert"), n)
    stacked = jnp.stack(blocks)
    return jnp.concatenate(
        [pick(stacked, lax.rem(mine - place_in_ring(i, n) + n, n), 0) for i in range(n)], axis=0
    )


def bits_of(low, high):
    out = []
    while low < high:
        out.append(low)
        low *= 2
    return out


def pick(v, index, axis):
    return lax.dynamic_index_in_dim(v, index, axis, keepdims=False)


def tie(*values):
    return lax.optimization_barrier(values)


(
    ORDER,
    LENGTHS,
    COS,
    SIN,
    SEG,
    MINE,
    W,
    X,
    OUT,
    ATTN,
    ROUTES,
    COT,
    MASK,
    G,
    QKV,
    SQUARES,
    ADDED,
    WA,
    FAR_GA,
    WB,
    M,
    NEAR_GACT,
    C,
    FAR,
    THERE,
    SEND_HIGH,
    ACC,
    Y_PART,
    NEAR_PART,
    SEND_LOW,
    Y_FAR,
    Y_NEAR,
    DHB,
    KEEP_HIGH,
    KEEP_LOW,
    ROUTER,
    GAIN_FFN,
    TAIL,
    Y,
    DQKV,
    ODD,
    DA,
    GAIN_ATTN,
    HELD,
    OUT_GRAD,
    BESIDE,
    SIDE,
    BACK,
    GU,
    DN,
    NEAR,
    DISTANT,
    PIECE,
    BACKS,
    ROWS,
    HALF,
    SMALL,
) = range(57)


class Flow:
    def __init__(self):
        self.of = {}

    def fence(self, *keys):
        out = tie(*[self.of[key] for key in keys])
        for key, v in zip(keys, out, strict=True):
            self.of[key] = v

    def __getitem__(self, key):
        return self.of[key]

    def __setitem__(self, key, value):
        self.of[key] = value

    def having(self, kind):
        return [key for key in self.of if isinstance(key, tuple) and key[0] == kind]


def fan(pieces, low):
    out = [list(pieces)]
    for bit in bits_of(1, low):
        out = out + [[flip(x, bit) for x in xs] for xs in out]
    return out


def add(a, b):
    return (a.astype(F32) + b.astype(F32)).astype(BF16)


def match(pieces, like):
    if len(pieces) == len(like):
        return pieces
    step = like[0].shape[0]
    return [x[i : i + step] for x in pieces for i in range(0, x.shape[0], step)]


def fold(parts):
    parts = list(parts)
    while len(parts) > 1:
        half = len(parts) // 2
        for i in range(half):
            got = match([flip(x, half) for x in reversed(parts[half + i])][::-1], parts[i])
            parts[i] = [add(a, b) for a, b in zip(parts[i], got, strict=True)]
        parts = parts[:half]
    return parts[0]


class Halving:
    def __init__(self, at, kind, value):
        self.at, self.kind, self.dp = at, kind, lax.axis_index("dp")
        n = lax.axis_size("dp")
        self.left = bits_of(1, n)[::-1]
        shape = (2,) * len(self.left) + (value.shape[0] // n, value.shape[1])
        at[kind, 0] = value.reshape(shape)

    def begin(self, bit):
        at, axis = self.at, self.left.index(bit)
        mine = lax.rem(self.dp // bit, 2)
        v = at[self.kind, 0]
        at[self.kind, 1] = flip(pick(v, 1 - mine, axis), bit)
        at[self.kind, 0] = pick(v, mine, axis)
        self.left.remove(bit)

    def end(self):
        at = self.at
        at[self.kind, 0] = add(at[self.kind, 0], at.of.pop((self.kind, 1)))


def blocks_of(parts, tok):
    return [(i, at) for i, p in enumerate(parts) for at in range(0, p.shape[0], tok)]


def onehot_back(pos_t, b):
    slot = lax.broadcasted_iota(jnp.int32, (pos_t.shape[0], CAP), 1)
    return (slot == pos_t[:, b : b + 1]).astype(BF16)


def onehot(pos_ref, b):
    slot = lax.broadcasted_iota(jnp.int32, (CAP, pos_ref.shape[1]), 0)
    return slot == pos_ref[b : b + 1, :]


def mm(a, b, dims):
    return lax.dot_general(a, b, (dims, ((), ())), preferred_element_type=F32)


def to_distance(ref, rows, value, me):
    n = lax.axis_size("dp")
    wide = value.shape[1] // n
    for c in range(n):
        at = pl.multiple_of((me ^ c) * wide, wide)
        ref[rows, pl.ds(at, wide)] = value[:, c * wide : (c + 1) * wide]


def gather_kernel(count, expert, *refs):
    parts, (pos, named, router, rows_out, gate) = refs[:count], refs[count:]
    tok = pos.shape[1]
    for b, (i, first) in enumerate(blocks_of(parts, tok)):
        at = slice(b * CAP, (b + 1) * CAP)
        part = parts[i][first : first + tok, :]
        hot = onehot(pos, b)
        found = mm(hot.astype(BF16), part, ((1,), (0,))).astype(BF16)
        to_distance(rows_out, at, found, expert[1])
        chosen = named[b] > 0
        logits = jnp.where(chosen, mm(router[...], part, ((1,), (1,))), -1e30)
        e = jnp.where(chosen, jnp.exp(logits - jnp.max(logits, axis=0, keepdims=True)), 0.0)
        gates = e / jnp.sum(e, axis=0, keepdims=True)
        mine = lax.broadcasted_iota(jnp.int32, gates.shape, 0) == expert[0]
        row = jnp.sum(jnp.where(mine, gates, 0.0), axis=0, keepdims=True)
        gate[at, :] = jnp.sum(jnp.where(hot, row, 0.0), axis=1, keepdims=True)


def gather_cot_kernel(count, expert, *refs):
    parts, (pos, rows_out) = refs[:count], refs[count:]
    tok = pos.shape[1]
    width = rows_out.shape[1]
    for b, (i, first) in enumerate(blocks_of(parts, tok)):
        part = parts[i][first : first + tok, :width]
        found = mm(onehot(pos, b).astype(BF16), part, ((1,), (0,))).astype(BF16)
        to_distance(rows_out, slice(b * CAP, (b + 1) * CAP), found, expert[1])


def pick_rows(kernel, name, parts, others, outs, expert):
    ins = [*parts, *others]
    whole = lambda x: pl.BlockSpec(x.shape, lambda n, e: (0,) * len(x.shape))
    return pl.pallas_call(
        functools.partial(kernel, len(parts)),
        grid_spec=pltpu.PrefetchScalarGridSpec(
            num_scalar_prefetch=1,
            grid=(1,),
            in_specs=[whole(x) for x in ins],
            out_specs=[whole(x) for x in outs],
        ),
        out_shape=outs,
        compiler_params=pltpu.CompilerParams(vmem_limit_bytes=VMEM),
        cost_estimate=COST,
        name=name,
    )(expert, *ins)


def spans(pieces):
    out, at = [], 0
    for p in pieces:
        out.append(slice(at, at + p.shape[0]))
        at += p.shape[0]
    return out


def expert_kernel(count, pieces, expert, *refs):
    rows_in, gs_in, gate, pos_t = refs[:4]
    parts = [refs[4 + i * pieces : 4 + (i + 1) * pieces] for i in range(3)]
    refs = refs[4 + 3 * pieces :]
    backs, refs = refs[:count], refs[count:]
    dg_out, du_out, gact_out, acc, dgate, wg, wu, wd = refs
    n = pl.program_id(0)
    tok = pos_t.shape[0]
    width = rows_in.shape[1]
    for at, a, b, c in zip(spans(parts[0]), *parts, strict=True):
        wg[at, :] = a[...]
        wu[at, :] = b[...]
        wd[at, :] = c[...]

    rows = rows_in[...]
    g = mm(rows, wg[...], ((1,), (0,)))
    u = mm(rows, wu[...], ((1,), (0,)))
    gw = mm(gs_in[...], wd[...], ((1,), (0,)))
    sg = 1.0 / (1.0 + jnp.exp(-g))
    silu = g * sg
    act = (silu * u).astype(BF16).astype(F32)
    part = jnp.sum(act * gw, axis=1, keepdims=True)
    gate_v = gate[...]
    gact_out[...] = (gate_v * act).astype(BF16)
    dact = gate_v * gw
    dg = (dact * u * (sg * (1.0 + g * (1.0 - sg)))).astype(BF16)
    du = (dact * silu).astype(BF16)
    dg_out[...] = dg
    du_out[...] = du
    back = mm(dg, wg[...], ((1,), (1,))) + mm(du, wu[...], ((1,), (1,)))

    @pl.when(n == 0)
    def _():
        acc[...] = back
        dgate[...] = part

    @pl.when(n > 0)
    def _():
        acc[...] += back
        dgate[...] += part

    @pl.when(n == pl.num_programs(0) - 1)
    def _():
        lane = lax.broadcasted_iota(jnp.int32, (CAP, EXTRA), 1)
        for b, (i, first) in enumerate(blocks_of(backs, tok)):
            at = slice(b * CAP, (b + 1) * CAP)
            to = slice(first, first + tok)
            hot = onehot_back(pos_t, b)
            out = backs[i]
            found = mm(hot, acc[at, :].astype(BF16), ((1,), (0,))).astype(BF16)
            to_distance(out, to, found, expert[1])
            d = dgate[at, :]
            hi = d.astype(BF16).astype(F32)
            beside = jnp.where(
                lane == expert[0], hi, jnp.where(lane == expert[2] + expert[0], d - hi, 0.0)
            ).astype(BF16)
            out[to, width:] = mm(hot, beside, ((1,), (0,))).astype(BF16)


def run_expert(rows, gs, gate, pos_t, pieces, expert, heights, ff):
    slots, width = rows.shape
    tile = min(512, ff)
    steps = ff // tile
    whole = lambda x: pl.BlockSpec(x.shape, lambda n, e: (0,) * len(x.shape))
    column = pl.BlockSpec((slots, tile), lambda n, e: (0, n))
    backs = [jax.ShapeDtypeStruct((h, width + EXTRA), BF16) for h in heights]
    thin = jax.ShapeDtypeStruct((slots, ff), BF16)
    outs = pl.pallas_call(
        functools.partial(expert_kernel, len(heights), len(pieces)),
        grid_spec=pltpu.PrefetchScalarGridSpec(
            num_scalar_prefetch=1,
            grid=(steps,),
            in_specs=[whole(x) for x in (rows, gs, gate, pos_t)]
            + [pl.BlockSpec((p.shape[0], tile), lambda n, e: (0, n)) for p in pieces]
            + [pl.BlockSpec((p.shape[0], tile), lambda n, e: (0, steps + n)) for p in pieces]
            + [pl.BlockSpec((p.shape[0], tile), lambda n, e: (0, 2 * steps + n)) for p in pieces],
            out_specs=[whole(x) for x in backs] + [column, column, column],
            scratch_shapes=[pltpu.VMEM((slots, width), F32), pltpu.VMEM((slots, 1), F32)]
            + [pltpu.VMEM((width, tile), BF16)] * 3,
        ),
        out_shape=backs + [thin, thin, thin],
        compiler_params=pltpu.CompilerParams(vmem_limit_bytes=VMEM),
        cost_estimate=COST,
        name="expert",
    )(expert, rows, gs, gate, pos_t, *pieces, *pieces, *pieces)
    return outs[: len(heights)], outs[len(heights) :]


def result_kernel(count, pieces, wide, me, gact, pos_t, *refs):
    parts, outs, wd = refs[:pieces], refs[pieces : pieces + count], refs[-1]
    tok = pos_t.shape[0]
    n = pl.program_id(0)
    blocks = wd.shape[0] // wide // pl.num_programs(0)

    @pl.when(n == 0)
    def _():
        for at, w in zip(spans(parts), parts, strict=True):
            wd[at, :] = w[...]

    step = blocks * wide
    here = wd[pl.ds(pl.multiple_of(n * step, step), step), :]
    y = mm(gact[...], here, ((1,), (1,))).astype(BF16)
    for b, (i, at) in enumerate(blocks_of(outs, tok)):
        part = y[b * CAP : (b + 1) * CAP, :]
        part = mm(onehot_back(pos_t, b), part, ((1,), (0,))).astype(BF16)
        for k in range(blocks):
            to = pl.multiple_of((me[0] ^ (blocks * n + k)) * wide, wide)
            outs[i][at : at + tok, pl.ds(to, wide)] = part[:, k * wide : (k + 1) * wide]


def result(gact, pos_t, pieces, count, me):
    slots, ff = gact.shape
    width = sum(p.shape[0] for p in pieces)
    wide = width // lax.axis_size("dp")
    tile = max(wide, min(512, width))
    last = (pieces[0].shape[1] - ff) // ff
    out = jax.ShapeDtypeStruct((pos_t.shape[1] // count * pos_t.shape[0], width), BF16)
    return pl.pallas_call(
        functools.partial(result_kernel, count, len(pieces), wide),
        grid_spec=pltpu.PrefetchScalarGridSpec(
            num_scalar_prefetch=1,
            grid=(width // tile,),
            in_specs=[
                pl.BlockSpec((slots, ff), lambda n, me: (0, 0)),
                pl.BlockSpec(pos_t.shape, lambda n, me: (0, 0)),
            ]
            + [pl.BlockSpec((p.shape[0], ff), lambda n, me: (0, last)) for p in pieces],
            out_specs=[pl.BlockSpec(out.shape, lambda n, me: (0, 0))] * count,
            scratch_shapes=[pltpu.VMEM((width, ff), BF16)],
        ),
        out_shape=[out] * count,
        compiler_params=pltpu.CompilerParams(vmem_limit_bytes=VMEM),
        cost_estimate=COST,
        name="result",
    )(me, gact, pos_t, *pieces)


def grads_kernel(count, rows, cuts, *refs):
    ins, outs = refs[: 5 * count], list(refs[5 * count :])
    ff = ins[2].shape[1]
    for b, cut in enumerate(cuts):
        at = slice(b * rows, (b + 1) * rows)
        gate = up = down = 0.0
        for c in range(count):
            tall, gs, dg, du, gact = ins[5 * c : 5 * c + 5]
            gate = gate + mm(tall[:, at], dg[...], ((0,), (0,)))
            up = up + mm(tall[:, at], du[...], ((0,), (0,)))
            down = down + mm(gs[:, at], gact[...], ((0,), (0,)))
        for start, stop in zip(cut[:-1], cut[1:], strict=True):
            out = outs.pop(0)
            out[:, :ff] = gate[start:stop].astype(BF16)
            out[:, ff : 2 * ff] = up[start:stop].astype(BF16)
            out[:, 2 * ff :] = down[start:stop].astype(BF16)


def grads(chunks, first, rows, cuts):
    ff = chunks[0][2].shape[1]
    blocks = len(cuts)
    specs, ins = [], []
    for chunk in chunks:
        slots = chunk[0].shape[0]
        tall = pl.BlockSpec((slots, blocks * rows), lambda i: (0, first // blocks))
        flat = pl.BlockSpec((slots, ff), lambda i: (0, 0))
        specs += [tall, tall, flat, flat, flat]
        ins += list(chunk)
    heights = [b - a for cut in cuts for a, b in zip(cut[:-1], cut[1:], strict=True)]
    return pl.pallas_call(
        functools.partial(grads_kernel, len(chunks), rows, cuts),
        grid=(1,),
        in_specs=specs,
        out_specs=[pl.BlockSpec((h, 3 * ff), lambda i: (0, 0)) for h in heights],
        out_shape=[jax.ShapeDtypeStruct((h, 3 * ff), BF16) for h in heights],
        compiler_params=pltpu.CompilerParams(vmem_limit_bytes=VMEM),
        cost_estimate=COST,
        name="grads",
    )(*ins)


def add_pieces_kernel(keep, *refs):
    pieces, out = refs[:-1], refs[-1]
    for at, p in zip(spans(pieces), pieces, strict=True):
        out[at, :] = (keep[at, :].astype(F32) + p[...].astype(F32)).astype(BF16)


def add_pieces(keep, pieces):
    whole = lambda x: pl.BlockSpec(x.shape, lambda i: (0, 0))
    return pl.pallas_call(
        add_pieces_kernel,
        grid=(1,),
        in_specs=[whole(x) for x in (keep, *pieces)],
        out_specs=whole(keep),
        out_shape=jax.ShapeDtypeStruct(keep.shape, BF16),
        compiler_params=pltpu.CompilerParams(vmem_limit_bytes=VMEM),
        cost_estimate=COST,
        name="add_pieces",
    )(keep, *pieces)


def attn_grads_kernel(me, a, d, *rest):
    k = d.shape[1]
    out = rest[-1]
    out[:, :k] = mm(a[...], d[...], ((0,), (0,))).astype(BF16)
    if len(rest) > 1:
        out[:, k:] = rest[0][...]


def attn_grads(a, d, extra, me, first, stride):
    rows, width = a.shape
    n = lax.axis_size("dp")
    tile = width // n
    count = n // stride
    at = lambda i, me: me[0] ^ (first + stride * i)
    k = d.shape[1] + sum(e.shape[1] for e in extra)
    return pl.pallas_call(
        attn_grads_kernel,
        grid_spec=pltpu.PrefetchScalarGridSpec(
            num_scalar_prefetch=1,
            grid=(count,),
            in_specs=[
                pl.BlockSpec((rows, tile), lambda i, me: (0, at(i, me))),
                pl.BlockSpec(d.shape, lambda i, me: (0, 0)),
            ]
            + [pl.BlockSpec((tile, e.shape[1]), lambda i, me: (at(i, me), 0)) for e in extra],
            out_specs=pl.BlockSpec((tile, k), lambda i, me: (i, 0)),
        ),
        out_shape=jax.ShapeDtypeStruct((count * tile, k), BF16),
        compiler_params=pltpu.CompilerParams(vmem_limit_bytes=VMEM),
        cost_estimate=COST,
        name="attn_grads",
    )(me, a, d, *extra)


def halves(held, rows):
    n = lax.axis_size("dp")
    wide = held.shape[1] // 256 * 128
    out = []
    for left, right, order in (
        (0, wide, bits_of(2, n)),
        (wide, held.shape[1], bits_of(2, n)[::-1]),
    ):
        side = {2 * i: held[i * rows : (i + 1) * rows, left:right] for i in range(n // 2)}
        out.append((side, order))
    return out


def stage(at, sides, step):
    for s, (side, order) in enumerate(sides):
        keys = sorted(r for r in side if r & order[step])
        v = [side[r] for r in keys]
        at[SIDE, s] = flip(jnp.concatenate(v, axis=0) if len(v) > 1 else v[0], order[step])


def unstage(at, sides, step):
    out = []
    for s, (side, order) in enumerate(sides):
        bit = order[step]
        keys = sorted(r for r in side if r & bit)
        rows = side[0].shape[0]
        got = at[SIDE, s]
        kept = {r: v for r, v in side.items() if not r & bit}
        for i, r in enumerate(keys):
            kept[r ^ bit] = add(kept[r ^ bit], got[i * rows : (i + 1) * rows])
        out.append((kept, order))
    return out


def spread(first, n):
    local = len(first)
    have = {(0, e): v for e, v in first.items()}
    for bit in bits_of(1, local):
        for key in sorted(key for key in have if key[1] & bit):
            have[(key[0] ^ bit, key[1] ^ bit)] = flip(have.pop(key), bit)
    for bit in bits_of(local, n):
        for key in sorted(have):
            have[(key[0] ^ bit, 0)] = flip(have[key], bit)
    return [have[key] for key in sorted(have)]


def gather_back(held, local, n):
    held = dict(held)
    for bit in reversed(bits_of(local, n // 2)):
        for r in sorted(r for r in held if r & bit):
            held[r ^ bit] = add(held[r ^ bit], flip(held.pop(r), bit))
    have = {(r, 0): v for r, v in held.items()}
    for bit in reversed(bits_of(1, local)):
        for key in sorted(key for key in have if key[0] & bit):
            have[(key[0] ^ bit, key[1] ^ bit)] = flip(have.pop(key), bit)
    return {e: v for (_, e), v in have.items()}


def per_row(row):
    return jnp.broadcast_to(row, (row.shape[1], row.shape[1])).T


def turn(v, cos, sin):
    return v * cos + pltpu.roll(v, v.shape[1] // 2, 1) * sin


def softmax_rows(qr, kr, same, scale):
    s = jnp.where(same, mm(qr, kr, ((1,), (1,))) * scale, -1e30)
    e = jnp.exp(s - jnp.max(s, axis=1, keepdims=True))
    return e / jnp.sum(e, axis=1, keepdims=True)


def attend_kernel(scale, qkv, r, gains, cos, sin, seg, qr_out, kr_out, vb_out, o_out):
    cols = o_out.shape[1]
    rq, rk = per_row(r[0, 0:1, :]), per_row(r[0, 1:2, :])
    seg_row = seg[0]
    same = per_row(seg_row) == seg_row
    for h in range(cols // HEAD_DIM):
        at = slice(h * HEAD_DIM, (h + 1) * HEAD_DIM)
        k_at = slice(cols + h * HEAD_DIM, cols + (h + 1) * HEAD_DIM)
        v_at = slice(2 * cols + h * HEAD_DIM, 2 * cols + (h + 1) * HEAD_DIM)
        qr = turn(qkv[:, at] * rq * gains[0:1, at], cos[...], sin[...]).astype(BF16)
        kr = turn(qkv[:, k_at] * rk * gains[1:2, at], cos[...], sin[...]).astype(BF16)
        vb = qkv[:, v_at].astype(BF16)
        p = softmax_rows(qr, kr, same, scale)
        qr_out[:, at] = qr
        kr_out[:, at] = kr
        vb_out[:, at] = vb
        o_out[:, at] = mm(p.astype(BF16), vb, ((1,), (0,))).astype(BF16)


def attend(qkv, r, gains, cos, sin, seg):
    total, cols = qkv.shape[0], qkv.shape[1] // 3
    zs, tok = seg.shape[0], seg.shape[2]
    tall = lambda w: pl.BlockSpec((tok, w), lambda b: (b, 0))
    fixed = lambda x: pl.BlockSpec(x.shape, lambda b: (0, 0))
    thin = jax.ShapeDtypeStruct((total, cols), BF16)
    return pl.pallas_call(
        functools.partial(attend_kernel, HEAD_DIM ** (-0.5)),
        grid=(zs,),
        in_specs=[
            tall(qkv.shape[1]),
            pl.BlockSpec((1, 2, tok), lambda b: (b, 0, 0)),
            fixed(gains),
            tall(HEAD_DIM),
            tall(HEAD_DIM),
            pl.BlockSpec((1, 1, tok), lambda b: (b, 0, 0)),
        ],
        out_specs=[tall(cols)] * 4,
        out_shape=[thin] * 4,
        compiler_params=pltpu.CompilerParams(vmem_limit_bytes=VMEM),
        cost_estimate=COST,
        name="attend",
    )(qkv, r, gains, cos, sin, seg)


def attend_back_kernel(
    scale, dhb, wo, q, k, qr, kr, vb, gains, cos, sin, seg, dq_out, dk_out, dv_out, sums
):
    cols = wo.shape[0]
    seg_row = seg[0]
    same = per_row(seg_row) == seg_row
    do_all = mm(dhb[...], wo[...], ((1,), (1,))).astype(BF16)
    sum_q = sum_k = 0.0
    for h in range(cols // HEAD_DIM):
        at = slice(h * HEAD_DIM, (h + 1) * HEAD_DIM)
        do = do_all[:, at]
        p = softmax_rows(qr[:, at], kr[:, at], same, scale)
        dp = mm(do, vb[:, at], ((1,), (1,)))
        ds = (p * (dp - jnp.sum(p * dp, axis=1, keepdims=True))).astype(BF16)
        dv_out[:, at] = mm(p.astype(BF16), do, ((0,), (0,))).astype(BF16)
        dq = turn(mm(ds, kr[:, at], ((1,), (0,))) * scale, cos[...], -sin[...])
        dk = turn(mm(ds, qr[:, at], ((0,), (0,))) * scale, cos[...], -sin[...])
        dq_out[:, at] = dq
        dk_out[:, at] = dk
        sum_q = sum_q + jnp.sum(q[:, at] * gains[0:1, at] * dq, axis=1, keepdims=True)
        sum_k = sum_k + jnp.sum(k[:, at] * gains[1:2, at] * dk, axis=1, keepdims=True)
    tok = dhb.shape[0]
    sums[0, 0:1, :] = jnp.broadcast_to(sum_q, (tok, tok)).T[0:1, :]
    sums[0, 1:2, :] = jnp.broadcast_to(sum_k, (tok, tok)).T[0:1, :]


def attend_back(dhb, wo, qkv, qr, kr, vb, gains, cos, sin, seg):
    total, cols = qkv.shape[0], wo.shape[0]
    zs, tok = seg.shape[0], seg.shape[2]
    tall = lambda w, at=0: pl.BlockSpec((tok, w), lambda b: (b, at))
    fixed = lambda x: pl.BlockSpec(x.shape, lambda b: (0, 0))
    wide = jax.ShapeDtypeStruct((total, cols), F32)
    return pl.pallas_call(
        functools.partial(attend_back_kernel, HEAD_DIM ** (-0.5)),
        grid=(zs,),
        in_specs=[
            tall(dhb.shape[1]),
            fixed(wo),
            tall(cols, 0),
            tall(cols, 1),
            tall(cols),
            tall(cols),
            tall(cols),
            fixed(gains),
            tall(HEAD_DIM),
            tall(HEAD_DIM),
            pl.BlockSpec((1, 1, tok), lambda b: (b, 0, 0)),
        ],
        out_specs=[tall(cols)] * 3 + [pl.BlockSpec((1, 2, tok), lambda b: (b, 0, 0))],
        out_shape=[
            wide,
            wide,
            jax.ShapeDtypeStruct((total, cols), BF16),
            jax.ShapeDtypeStruct((zs, 2, tok), F32),
        ],
        compiler_params=pltpu.CompilerParams(vmem_limit_bytes=VMEM),
        cost_estimate=COST,
        name="attend_back",
    )(dhb, wo, qkv, qkv, qr, kr, vb, gains, cos, sin, seg)


def join_back_kernel(q, k, dqn, dkn, dv, r, means, gains, out, gain_out):
    cols = dv.shape[1]
    for at, v, d in ((0, q, dqn), (1, k, dkn)):
        rr = per_row(r[0, at : at + 1, :])
        mean = per_row(means[0, at : at + 1, :])
        part = []
        for h in range(cols // HEAD_DIM):
            to = slice(h * HEAD_DIM, (h + 1) * HEAD_DIM)
            vr = v[:, to] * rr
            out[:, at * cols + h * HEAD_DIM : at * cols + (h + 1) * HEAD_DIM] = (
                rr * (gains[at : at + 1, to] * d[:, to]) - vr * (rr * rr) * mean
            ).astype(BF16)
            part.append(jnp.sum(d[:, to] * vr, axis=0, keepdims=True))
        row = jnp.concatenate(part, axis=1)

        @pl.when(pl.program_id(0) == 0)
        def _():
            gain_out[at : at + 1, :] = row

        @pl.when(pl.program_id(0) > 0)
        def _():
            gain_out[at : at + 1, :] += row

    out[:, 2 * cols :] = dv[...]


def join_back(qkv, dqn, dkn, dv, r, means, gains):
    total, cols = dv.shape
    zs, tok = r.shape[0], r.shape[2]
    tall = lambda w, at=0: pl.BlockSpec((tok, w), lambda b: (b, at))
    row = pl.BlockSpec((1, 2, tok), lambda b: (b, 0, 0))
    return pl.pallas_call(
        join_back_kernel,
        grid=(zs,),
        in_specs=[tall(cols, 0), tall(cols, 1), tall(cols), tall(cols), tall(cols), row, row]
        + [pl.BlockSpec(gains.shape, lambda b: (0, 0))],
        out_specs=[tall(3 * cols), pl.BlockSpec((2, cols), lambda b: (0, 0))],
        out_shape=[
            jax.ShapeDtypeStruct((total, 3 * cols), BF16),
            jax.ShapeDtypeStruct((2, cols), F32),
        ],
        compiler_params=pltpu.CompilerParams(vmem_limit_bytes=VMEM),
        cost_estimate=COST,
        name="join_back",
    )(qkv, qkv, dqn, dkn, dv, r, means, gains)


def first_back_kernel(d, w, x, r, da, gain):
    back = mm(d[...], w[...], ((1,), (1,)))
    da[...] = back.astype(BF16)
    row = jnp.sum(back * (x[...].astype(F32) * r[...]), axis=0, keepdims=True)

    @pl.when(pl.program_id(0) == 0)
    def _():
        gain[...] = row

    @pl.when(pl.program_id(0) > 0)
    def _():
        gain[...] += row


def first_back(d, w, x, r, tok):
    total, width = x.shape
    k = d.shape[1]
    return pl.pallas_call(
        first_back_kernel,
        grid=(total // tok,),
        in_specs=[
            pl.BlockSpec((tok, k), lambda b: (b, 0)),
            pl.BlockSpec((width, k), lambda b: (0, 0)),
            pl.BlockSpec((tok, width), lambda b: (b, 0)),
            pl.BlockSpec((tok, 1), lambda b: (b, 0)),
        ],
        out_specs=[
            pl.BlockSpec((tok, width), lambda b: (b, 0)),
            pl.BlockSpec((1, width), lambda b: (0, 0)),
        ],
        out_shape=[
            jax.ShapeDtypeStruct((total, width), BF16),
            jax.ShapeDtypeStruct((1, width), F32),
        ],
        compiler_params=pltpu.CompilerParams(vmem_limit_bytes=VMEM),
        cost_estimate=COST,
        name="first_back",
    )(d, w, x, r)


def form_kernel(count, own, *refs):
    ins, (gate_up, down) = refs[:count], refs[-2:]
    wide = gate_up.shape[2]
    for o in range(count):

        @pl.when(own[0] == o)
        def _():
            for e in range(count):
                gate_up[:, e, :] = ins[o ^ e][:, :wide].astype(F32)
                down[:, e, :] = ins[o ^ e][:, wide:].astype(F32)


def form(blocks, own, rows, start, stop, before=()):
    k = blocks[0][0].shape[1]
    count, ff, tile = len(blocks), k // 3, 32

    def spec(at):
        return pl.BlockSpec((tile, k), lambda i, o: (i + (start - at) // tile, 0))

    shapes = [
        jax.ShapeDtypeStruct((rows, count, 2 * ff), F32),
        jax.ShapeDtypeStruct((rows, count, ff), F32),
    ]
    outs = [
        pl.BlockSpec((tile, *s.shape[1:]), lambda i, o: (i + start // tile, 0, 0)) for s in shapes
    ]
    return pl.pallas_call(
        functools.partial(form_kernel, count),
        grid_spec=pltpu.PrefetchScalarGridSpec(
            num_scalar_prefetch=1,
            grid=((stop - start) // tile,),
            in_specs=[spec(at) for _, at in blocks]
            + [pl.BlockSpec(memory_space=pl.ANY)] * len(before),
            out_specs=outs,
        ),
        out_shape=shapes,
        input_output_aliases={1 + count + n: n for n in range(len(before))},
        compiler_params=pltpu.CompilerParams(vmem_limit_bytes=VMEM),
        cost_estimate=COST,
        name="form",
    )(own, *[v for v, _ in blocks], *before)


def extra_kernel(zat, router, attn, qk, ffn, out, rows):
    experts, cols = router.shape[0], qk.shape[1]
    rows[...] = jnp.zeros_like(rows)
    rows[:experts, :] = router[...]
    rows[experts : experts + 1, :] = attn[...]
    at = pl.ds(pl.multiple_of(zat[0] * cols, cols), cols)
    rows[experts + 1 : experts + 3, at] = qk[...]
    rows[experts + 3 : experts + 4, :] = ffn[...]
    out[...] = rows[...].T.astype(BF16)


def extra_columns(router, attn, qk, ffn, zat):
    width = attn.shape[1]
    whole = lambda x: pl.BlockSpec(x.shape, lambda i, z: (0, 0))
    out = jax.ShapeDtypeStruct((width, EXTRA), BF16)
    return pl.pallas_call(
        extra_kernel,
        grid_spec=pltpu.PrefetchScalarGridSpec(
            num_scalar_prefetch=1,
            grid=(1,),
            in_specs=[whole(x) for x in (router, attn, qk, ffn)],
            out_specs=whole(out),
            scratch_shapes=[pltpu.VMEM((EXTRA, width), F32)],
        ),
        out_shape=out,
        compiler_params=pltpu.CompilerParams(vmem_limit_bytes=VMEM),
        cost_estimate=COST,
        name="extra_columns",
    )(zat, router, attn, qk, ffn)


def inv_rms(v):
    return lax.rsqrt(jnp.mean(v * v, axis=-1, keepdims=True) + EPSILON)


def rms_back(v, r, gain, c):
    gc = gain * c
    return r * gc - v * (r * r * r) * jnp.mean(v * gc, axis=-1, keepdims=True)


def places_and_tables(at, dp, zs, rows):
    dealt = lax.dynamic_slice_in_dim(at[ORDER], dp * zs * SEQ_DEV, zs * SEQ_DEV)
    lens = jnp.take(at[LENGTHS], dealt).reshape(zs, SEQ_DEV)
    ends = jnp.cumsum(lens, axis=1)
    places = jnp.arange(rows, dtype=jnp.int32)
    segment = jnp.sum((places[None, :, None] >= ends[:, None, :]).astype(jnp.int32), axis=2)
    starts = ends - lens
    offset = jnp.sum(
        jnp.where(
            segment[:, :, None] == jnp.arange(SEQ_DEV, dtype=jnp.int32), starts[:, None, :], 0
        ),
        axis=2,
    )
    half = HEAD_DIM // 2
    inverse = ROPE_BASE ** (-2.0 * jnp.arange(half, dtype=F32) / HEAD_DIM)
    turned = (places[None] - offset).astype(F32)[..., None] * inverse
    at[COS] = jnp.tile(jnp.cos(turned), (1, 1, 2)).reshape(zs * rows, HEAD_DIM)
    sin = jnp.sin(turned)
    at[SIN] = jnp.concatenate([-sin, sin], axis=2).reshape(zs * rows, HEAD_DIM)
    at[SEG] = segment.astype(F32)[:, None, :]


def on_device(
    tokens,
    lengths,
    permutation,
    routes,
    norm_gains,
    w_qkv,
    w_out,
    router,
    w_gate_up,
    w_down,
    cotangent,
):
    rows, width = tokens.shape
    zs = lax.axis_size("expert")
    dps = lax.axis_size("dp")
    z = lax.axis_index("expert")
    dp = lax.axis_index("dp")
    local = w_gate_up.shape[1]
    ff = w_down.shape[2]
    experts = router.shape[1]
    own_rows = w_qkv.shape[0]
    e_rows = w_gate_up.shape[0]
    cols = width // zs
    expert = z * local + lax.rem(dp, local)
    own = lax.rem(dp, local)
    top = local // 2
    far_bit = dps // 2
    mid = zs // 2
    laid_out = local == 4 and dps == 8
    me_at = jnp.reshape(dp, (1,)).astype(jnp.int32)
    expert_at = jnp.stack([expert, dp, jnp.int32(experts)]).astype(jnp.int32)
    at = Flow()

    extra = jnp.concatenate(
        [router, norm_gains, jnp.zeros((own_rows, EXTRA - experts - 4), BF16)], axis=1
    )
    sent = jnp.stack(
        [
            jnp.concatenate(
                [w_qkv[:, i * width + e * cols : i * width + (e + 1) * cols] for i in range(3)]
                + [extra],
                axis=1,
            )
            for e in range(zs)
        ]
    )
    at[MINE] = lax.all_to_all(sent, "expert", split_axis=0, concat_axis=0, tiled=True)
    moved = [(b, (b % dps) * zs + b // dps) for b in range(dps * zs)]

    for e in range(local):
        at[W, 0, e] = jnp.concatenate(
            [pick(w_gate_up, own ^ e, 1), pick(w_down, own ^ e, 1)], axis=1
        )
    at[X, 0] = tokens
    at[OUT] = w_out
    at.fence(MINE, (X, 0), OUT, *at.having(W))

    at[ATTN] = lax.all_gather(
        at[MINE].reshape(zs * own_rows, 3 * cols + EXTRA), "dp", axis=0, tiled=True
    )
    if laid_out:
        at[W, 1, 0] = flip(at[W, 0, 1], 1)
        at[W, 1, 2] = flip(at[W, 0, 3], 1)
    at[LENGTHS], at[ORDER], at[ROUTES], at[COT] = lengths, permutation, routes, cotangent
    for i in range(1, zs):
        at[X, i] = hop(at[X, i - 1])
        if i == 1:
            at.fence((X, 1), LENGTHS, ORDER, ROUTES, COT, OUT)
            places_and_tables(at, dp, zs, rows)
        elif i == 2:
            at.fence((X, 2), COS, SIN, SEG, ROUTES, COT)
            at[MASK] = jnp.sum(
                (at[ROUTES][:, :, None] == jnp.arange(experts, dtype=jnp.int32)).astype(BF16),
                axis=1,
            )
            mask_pad = jnp.concatenate(
                [at[MASK], jnp.zeros((rows, EXTRA - experts), BF16)], axis=1
            )
            at[G, 0] = jnp.concatenate([at[COT], mask_pad], axis=1)
            at[OUT] = lax.ppermute(at[OUT], ("dp", "expert"), moved)
        else:
            at.fence((X, i))
    xs = [(X, i) for i in range(zs)]
    at.fence(ATTN, OUT, (G, 0), MASK, *xs, *at.having(W))

    cut = e_rows // 4
    if laid_out:
        at[W, 2, 0] = flip(at[W, 0, 2], 2)
        at[W, 4, 0] = flip(at[W, 0, 0], 4)
    at[G, 1] = hop(at[G, 0])
    out_w = lax.all_gather(at[OUT], "dp", axis=0, tiled=True)
    attn_w = at[ATTN]
    qkv_w = attn_w[:, : 3 * cols]
    router_full = attn_w[:, 3 * cols : 3 * cols + experts]
    gains = attn_w[:, 3 * cols + experts : 3 * cols + experts + 4].astype(F32).T
    router_t = router_full.T
    x_all = by_line([at[key] for key in xs])
    xf = x_all.astype(F32)
    r_attn = inv_rms(xf)
    a_all = (xf * r_attn * gains[0]).astype(BF16)
    at[QKV] = nn(a_all, qkv_w)
    at.fence(QKV, (G, 1))
    qkv = at[QKV]
    q, k = qkv[:, :cols], qkv[:, cols : 2 * cols]
    at[SQUARES] = lax.psum(
        jnp.stack([jnp.sum(q * q, axis=1), jnp.sum(k * k, axis=1)]), "expert"
    )
    at.fence(SQUARES, (G, 1))
    at[G, 2] = hop(at[G, 1])
    by_block = lambda v: v.reshape(2, zs, rows).transpose(1, 0, 2)
    r_qk = by_block(lax.rsqrt(at[SQUARES] / width + EPSILON))
    gain_qk = lax.dynamic_slice_in_dim(gains[1:3], z * cols, cols, axis=1)
    cos, sin, seg = at[COS], at[SIN], at[SEG]
    qr, kr, vb, o = attend(qkv, r_qk, gain_qk, cos, sin, seg)
    at[ADDED] = nn(o, out_w, BF16)
    at.fence(ADDED, (G, 2), *(w for w in at.having(W) if laid_out))
    at[ADDED] = lax.psum_scatter(at[ADDED], "expert", scatter_dimension=0, tiled=True)
    for i in range(3, zs):
        at[G, i] = hop(at[G, i - 1])
    if laid_out:
        at[W, 3, 0] = flip(at[W, 1, 2], 2)
        at[W, 5, 0] = flip(at[W, 1, 0], 4)
        at[WA, 6] = flip(at[W, 2, 0][: 11 * cut // 4], 4)
    first_g = [(G, i) for i in range(mid)]
    last_g = [(G, i) for i in range(mid, zs)]
    at[FAR_GA] = flip(jnp.concatenate([at[key] for key in first_g], axis=0), top)
    weight_keys = at.having(W) + at.having(WA)
    at.fence(ADDED, FAR_GA, (G, zs - 1), *(w for w in weight_keys if laid_out))
    marks = (0, 3 * cut // 4, 9 * cut // 4, e_rows)
    hid = tokens.astype(F32) + at[ADDED].astype(F32)
    r_ffn = inv_rms(hid)
    m = (hid * r_ffn * gains[3]).astype(BF16)

    at[M, 0] = m
    mine_e = (jnp.arange(experts) == expert).astype(F32)

    def chunk_places(kind, parts):
        masks = jnp.concatenate([x[:, width : width + experts] for x in parts], axis=0)
        masks = masks.astype(F32).reshape(-1, rows, experts)
        on = jnp.sum(masks * mine_e, axis=2)
        pos = jnp.where(on > 0, jnp.cumsum(on, axis=1) - 1.0, -1.0).astype(jnp.int32)
        at[kind, 0], at[kind, 1], at[kind, 2] = pos, pos.T, masks.transpose(0, 2, 1)
        out = jax.ShapeDtypeStruct((pos.shape[0] * CAP, width), BF16)
        (at[kind, 3],) = pick_rows(gather_cot_kernel, "gather_cot", parts, [pos], [out], expert_at)

    waiting = [(G, key) for key in last_g] + [(M, (M, i)) for i in range(zs)]
    near_cores = [fan([m], top)[1:]]
    for i in range(1, zs):
        at[M, i] = hop(at[M, i - 1])
        kind, key = waiting.pop(0)
        at[FAR, *key] = flip(at[key], top)
        beside = [(FAR, *key)]
        if laid_out:
            at[WB, i] = flip(at[W, 3, 0][marks[i - 1] : marks[i]], 4)
            beside.append((WB, i))
            if i == 1:
                at[WA, 7] = flip(at[W, 2, 0][11 * cut // 4 :], 4)
                beside.append((WA, 7))
        if i == 1:
            g_near = [jnp.concatenate([at[key] for key in first_g + last_g], axis=0)]
            chunk_places(NEAR, [x for xs in fan(g_near, top) for x in xs])
        if i == 2:
            beside += at.having(NEAR)
        if i == zs - 1:
            g_far = [at[FAR_GA], *[at[FAR, *k] for k in last_g]]
            chunk_places(DISTANT, [x for xs in fan(g_far, top) for x in xs])
            beside += at.having(DISTANT)
        at.fence((M, i), *beside)
        near_cores.append(fan([at[M, i]], top)[1:])
    key = waiting.pop(0)[1]
    at[FAR, *key] = flip(at[key], top)

    def chunk_gather(kind, blocks, cores):
        flat = [*blocks, *(x[0] for d in range(top - 1) for x in (c[d] for c in cores))]
        slots = at[kind, 0].shape[0] * CAP
        outs = [
            jax.ShapeDtypeStruct((slots, width), BF16),
            jax.ShapeDtypeStruct((slots, 1), F32),
        ]
        others = [at[kind, 0], at[kind, 2], router_t]
        picked, gate = pick_rows(gather_kernel, "gather", flat, others, outs, expert_at)
        return picked, at[kind, 3], gate

    def chunk_expert(kind, groups, got):
        heights = [h for group in groups for h in group]
        backs, outs = run_expert(*got, at[kind, 1], weights, expert_at, heights, ff)
        back = []
        for group in groups:
            back.append(backs[: len(group)])
            backs = backs[len(group) :]
        return back, (got[0], got[1], *outs)

    ms = [at[M, i] for i in range(zs)]
    near_rows = chunk_gather(NEAR, ms, near_cores)
    for i, v in enumerate(near_rows):
        at[ROWS, i] = v
    at.fence(*at.having(ROWS), (FAR, *key))
    while waiting:
        key = waiting.pop(0)[1]
        at[FAR, *key] = flip(at[key], top)
    if laid_out:
        keys = [(W, r, 0) for r in range(6)] + [(WA, 6), (WA, 7), (WB, 1), (WB, 2), (WB, 3)]
        weights = [at[key] for key in keys]
    else:
        weights = spread({e: at[W, 0, e] for e in range(local)}, dps)
    own_heights = [rows] * zs
    near_back, near_outs = chunk_expert(
        NEAR, [own_heights] + [[zs * rows]] * (top - 1), [at[ROWS, i] for i in range(3)]
    )
    far_ms = [(FAR, M, i) for i in range(zs)]
    at[NEAR_GACT] = near_outs[4]
    at.fence(NEAR_GACT, *far_ms)
    ms = [at[key] for key in far_ms]
    far_rows = chunk_gather(DISTANT, ms, [fan([v], top)[1:] for v in ms])
    far_back, far_outs = chunk_expert(
        DISTANT, [own_heights] + [[mid * rows, (zs - mid) * rows]] * (top - 1), far_rows
    )
    near_outs = (*near_outs[:4], at[NEAR_GACT])

    quarter = dps // 4
    near_sum = fold(near_back)
    far_sum = fold(far_back)
    chunk_keys = [(C, n) for n in range(10)]
    for key, v in zip(chunk_keys, (*near_outs, *far_outs), strict=True):
        at[key] = v
    for i, v in enumerate(far_sum):
        at[BACKS, i] = v
    at.fence(*at.having(BACKS), *chunk_keys)

    halves_cut = [(0, e_rows // 2, e_rows) if laid_out else (0, e_rows)] * quarter

    def chunk_grads(kind, first, cuts):
        c = [at[key] for key in chunk_keys]
        made = list(grads([c[:5], c[5:]], first, e_rows, cuts))
        for row, cut in enumerate(cuts):
            for start in cut[:-1]:
                at[kind, row, start] = made.pop(0)

    def send_part(key, row, start):
        at[PIECE, key, row, start] = flip(at[key, row, start], far_bit)

    def sum_row(keep, key, row):
        starts = sorted(k[2] for k in at.having(key) if k[1] == row)
        if not laid_out:
            send_part(key, row, 0)
        return add_pieces(at[keep, row, 0], [at[PIECE, key, row, start] for start in starts])

    whole_cut = [(0, e_rows)] * quarter
    last = zs - 1

    at[THERE] = flip(at[BACKS, last], top)
    chunk_grads(SEND_HIGH, 3 * quarter, halves_cut)
    at.fence(THERE, *at.having(SEND_HIGH), *chunk_keys)
    half = e_rows // 2
    early, most = 3 * e_rows // 8, 7 * e_rows // 8
    for i in reversed(range(zs)):
        here = near_sum[i].astype(F32) + at[THERE].astype(F32)
        if i < last:
            here = here + at[ACC].astype(F32)
        at[ACC] = here.astype(BF16)
        if not i:
            break
        at[ACC] = hop(at[ACC], -1)
        at[THERE] = flip(at[BACKS, i - 1], top)
        beside = []
        if i == last:
            if laid_out:
                send_part(SEND_HIGH, 0, 0)
            for n, y in enumerate(result(at[C, 9], at[DISTANT, 1], weights, top, me_at)):
                at[Y_PART, n] = y
            beside = [*at.having(Y_PART), *at.having(PIECE)]
        if i == last - 1:
            for n, y in enumerate(result(at[C, 4], at[NEAR, 1], weights, top, me_at)):
                at[NEAR_PART, n] = y
            if laid_out:
                send_part(SEND_HIGH, 0, half)
            beside = [*at.having(NEAR_PART), *at.having(PIECE)]
        if i == last - 2:
            if laid_out:
                send_part(SEND_HIGH, 1, 0)
            low_cut = halves_cut
            if laid_out:
                low_cut = [halves_cut[0], (0, e_rows - early, e_rows)]
            chunk_grads(SEND_LOW, 2 * quarter, low_cut)
            at[Y_FAR] = fold([[at[key]] for key in at.having(Y_PART)])[0]
            beside = [Y_FAR, *at.having(SEND_LOW), *at.having(PIECE)]
        at.fence(ACC, THERE, *beside, *chunk_keys)
    at.fence(ACC, *at.having(NEAR_PART))
    dm = at[ACC].astype(F32)
    at[Y_FAR] = flip(at[Y_FAR], top)
    if laid_out:
        send_part(SEND_HIGH, 1, half)
        send_part(SEND_LOW, 0, 0)

    own_mask = at[MASK].astype(F32)
    own_logits = jnp.where(own_mask > 0, nn(m, router_full), -1e30)
    own_e = jnp.where(
        own_mask > 0, jnp.exp(own_logits - jnp.max(own_logits, axis=1, keepdims=True)), 0.0
    )
    gate_own = own_e / jnp.sum(own_e, axis=1, keepdims=True)
    dgates = dm[:, width : width + experts] + dm[:, width + experts : width + 2 * experts]
    dz = (
        gate_own * (dgates - jnp.sum(gate_own * dgates, axis=1, keepdims=True))
    ).astype(BF16)
    dmt = nt(dz, router_full) + dm[:, :width]
    grad_out = cotangent.astype(F32)
    dh = grad_out + rms_back(hid, r_ffn, gains[3], dmt)
    at[DHB] = lax.all_gather(dh.astype(BF16), "expert", axis=0, tiled=True)
    router_part = tn(dz, m)
    gain_ffn = jnp.sum(dmt * hid * r_ffn, axis=0)
    at[Y_NEAR] = fold([[at[key]] for key in at.having(NEAR_PART)])[0]
    chunk_grads(KEEP_HIGH, quarter, whole_cut)
    if laid_out:
        for i in range(quarter):
            at[TAIL, quarter + i, 0] = sum_row(KEEP_HIGH, SEND_HIGH, i)
    chunk_grads(KEEP_LOW, 0, whole_cut)
    at[ROUTER], at[GAIN_FFN] = router_part, gain_ffn
    tails = at.having(TAIL)
    keeps = at.having(KEEP_LOW) + at.having(KEEP_HIGH) + at.having(SEND_LOW)
    at.fence(DHB, Y_FAR, Y_NEAR, ROUTER, GAIN_FFN, *keeps, *at.having(PIECE), *tails)
    dhb = at[DHB]
    if laid_out:
        at[TAIL, 0, 2] = flip(at[TAIL, 2, 0], 2)
        send_part(SEND_LOW, 0, half)
        send_part(SEND_LOW, 1, 0)
    if not laid_out:
        for i in range(quarter):
            at[TAIL, quarter + i, 0] = sum_row(KEEP_HIGH, SEND_HIGH, i)
    y_own = add(at[Y_NEAR], at[Y_FAR])
    at[Y] = lax.psum_scatter(
        by_line([y_own[i * rows : (i + 1) * rows] for i in range(zs)]),
        "expert",
        scatter_dimension=0,
        tiled=True,
    )

    dqn, dkn, dv, sums = attend_back(dhb, out_w, qkv, qr, kr, vb, gain_qk, cos, sin, seg)
    means = lax.psum(sums.reshape(-1, rows), "expert").reshape(zs, 2, rows) / width
    out_sum = Halving(at, OUT_GRAD, tn(o, dhb, BF16))
    dqkv, gains_qk = join_back(qkv, dqn, dkn, dv, r_qk, means, gain_qk)
    at[DQKV] = dqkv
    at.fence(DQKV, Y, *at.having(OUT_GRAD), *at.having(PIECE), *at.having(TAIL))
    out_sum.begin(1)

    at[ODD] = attn_grads(a_all, at[DQKV], [], me_at, 1, 2)
    at.fence(ODD, DQKV, *at.having(OUT_GRAD), *at.having(TAIL), *at.having(SEND_LOW))
    out_sum.end()
    out_sum.begin(far_bit)
    at[ODD] = flip(at[ODD], 1)
    if laid_out:
        at[HALF, 0] = flip(at[TAIL, 3, 0][:most], 2)
        send_part(SEND_LOW, 1, e_rows - early)
    at[DA], at[GAIN_ATTN] = first_back(at[DQKV], attn_w, x_all, r_attn, rows)
    even = attn_grads(a_all, at[DQKV], [], me_at, 0, 2)
    at[HELD] = add(even, at[ODD])
    at.fence(HELD, DQKV, DA, GAIN_ATTN, *at.having(OUT_GRAD), *at.having(HALF), *at.having(PIECE))
    at[DA] = lax.psum_scatter(at[DA], "expert", scatter_dimension=0, tiled=True)
    sides = halves(at[HELD], zs * own_rows)
    stage(at, sides, 0)
    out_sum.end()
    out_sum.begin(2)
    at[BESIDE] = extra_columns(
        at[ROUTER], at[GAIN_ATTN], gains_qk, at[GAIN_FFN][None], jnp.reshape(z, (1,))
    )
    for turn_ in range(1, len(bits_of(2, dps))):
        at.fence(*at.having(SIDE), BESIDE, *at.having(OUT_GRAD), *at.having(KEEP_LOW), *at.having(PIECE))
        out_sum.end()
        if laid_out:
            at[OUT_GRAD, 0] = lax.ppermute(
                at[OUT_GRAD, 0], ("dp", "expert"), [(b, a) for a, b in moved]
            )
        if turn_ < len(bits_of(2, dps)) - 1:
            out_sum.begin(2 << turn_)
        if turn_ == 1:
            small_sum = Halving(at, SMALL, at[BESIDE])
            small_sum.begin(1)
            for i in range(quarter):
                at[TAIL, i, 0] = sum_row(KEEP_LOW, SEND_LOW, i)
        sides = unstage(at, sides, turn_ - 1)
        stage(at, sides, turn_)
    at.fence(*at.having(SIDE), *at.having(SMALL), *at.having(TAIL))
    sides = unstage(at, sides, len(bits_of(2, dps)) - 1)
    at[BACK] = jnp.concatenate([sides[0][0][0], sides[1][0][0]], axis=1)
    at.fence(BACK, *at.having(OUT_GRAD), *at.having(SMALL), *at.having(HALF), *at.having(TAIL))
    small_sum.end()
    if not laid_out:
        at[OUT_GRAD, 0] = lax.ppermute(
            at[OUT_GRAD, 0], ("dp", "expert"), [(b, a) for a, b in moved]
        )
    at[BACK] = lax.all_to_all(
        at[BACK].reshape(zs, own_rows, 3 * cols),
        "expert",
        split_axis=0,
        concat_axis=0,
        tiled=True,
    )
    own_at = jnp.reshape(own, (1,))
    bits = bits_of(2, dps)
    small_sum.begin(bits[0])
    if laid_out:
        at[HALF, most] = flip(at[TAIL, 3, 0][most:], 2)
        at[TAIL, 0, 1] = flip(at[TAIL, 1, 0], 1)
        blocks = [(at[TAIL, 0, e], 0) for e in range(local - 1)]
        at[HALF, 0] = flip(at[HALF, 0], 1)
        at[GU], at[DN] = form([*blocks, (at[HALF, 0], 0)], own_at, e_rows, 0, most)
        at.fence(GU, DN, DA, *at.having(SMALL))
        blocks += [(flip(at[HALF, most], 1), most)]
        at[GU], at[DN] = form(blocks, own_at, e_rows, most, e_rows, (at[GU], at[DN]))
    else:
        rest = gather_back({k[1]: at[k] for k in at.having(TAIL)}, local, dps)
        at[GU], at[DN] = form([(rest[e], 0) for e in range(local)], own_at, e_rows, 0, e_rows)
    small_sum.end()
    for bit in bits[1:]:
        small_sum.begin(bit)
        small_sum.end()
    at.fence(BACK, GU, DN, *at.having(OUT_GRAD), *at.having(SMALL))
    grad_w_out = at[OUT_GRAD, 0].astype(F32)
    back = at[BACK].astype(F32)
    grad_w_qkv = jnp.concatenate(
        [back[e, :, i * cols : (i + 1) * cols] for i in range(3) for e in range(zs)], axis=1
    )
    place = place_in_ring(z, zs)
    blocks = at[SMALL, 0].reshape(zs, own_rows, EXTRA)
    extra_sum = pick(blocks, z, 0).astype(F32)
    for i in range(1, zs):
        to = at_place(lax.rem(place + i, zs), zs)
        extra_sum = extra_sum + hop(pick(blocks, to, 0), i).astype(F32)
    grad_router = extra_sum[:, :experts]
    grad_gains = extra_sum[:, experts : experts + 4]
    da = at[DA].astype(F32)

    output = hid + at[Y].astype(F32)
    x_own = tokens.astype(F32)
    grad_tokens = dh + rms_back(x_own, inv_rms(x_own), gains[0], da)
    return (
        output,
        grad_tokens,
        grad_gains,
        grad_w_qkv,
        grad_w_out,
        grad_router,
        at[GU],
        at[DN],
    )


def solution(mesh):
    both = P(("dp", "expert"), None)
    experts = P("dp", "expert", None)
    return jax.shard_map(
        on_device,
        mesh=mesh,
        in_specs=(both, P(), P(), both, both, both, both, both, experts, experts, both),
        out_specs=(both, both, both, both, both, both, experts, experts),
        check_vma=False,
    )
```
